32 devices in a mesh: pipe: 4 (over z), expert: 4 (over y, x), dp: 2 (over core).
Axes of the slice: x: 2, y: 2, z: 4, core: 2. Of those that a mesh axis runs over, the one named last changes fastest.
Arguments:
- section_inputs: bfloat16 [4, 256, 2048], P('pipe', ('expert', 'dp')), may hold values from -6 to 6
- saved_inputs: bfloat16 [4, 256, 2048], P('pipe', ('expert', 'dp')), may hold values from -6 to 6
- output_grads: bfloat16 [4, 256, 2048], P('pipe', ('expert', 'dp')), may hold values from -6 to 6
- forward_routes: int32 [4, 256, 8], P('pipe', ('expert', 'dp')), may hold values from 0 to 63, as said below
- backward_routes: int32 [4, 256, 8], P('pipe', ('expert', 'dp')), may hold values from 0 to 63, as said below
- forward_gates: float32 [4, 256, 8], P('pipe', ('expert', 'dp')), may hold values from 0.1 to 0.9
- backward_gates: float32 [4, 256, 8], P('pipe', ('expert', 'dp')), may hold values from 0.1 to 0.9
- expert_weights: bfloat16 [4, 64, 2048, 768], P('pipe', 'expert'), may hold values from -0.125 to 0.125
Outputs:
- next_inputs: bfloat16 [4, 256, 2048], P('pipe', ('expert', 'dp'))
- prior_grads: bfloat16 [4, 256, 2048], P('pipe', ('expert', 'dp'))
- weight_grads: bfloat16 [4, 64, 2048, 768], P('pipe', 'expert', 'dp')
The draws below stay inside these ranges and needn't reach their ends.
Inputs may be any that keep to these rules, and one draw needn't show every extreme that they name: `forward_routes`: each token names 8 different experts. Among the tokens of one aligned block of 32 (the tokens of one device) no expert is named more than 5 times, and in each section one expert is named exactly 5 times in every block. `backward_routes`: as for forward_routes.
All inputs are finite; a program needn't handle non-finite values.
Results may differ from the reference program's by a relative error of at most 0.012.
Values may be sent and summed in bfloat16 or wider, within the bound.
No kernel may reach another device: no remote copies, remote signals or barrier semaphores. Data moves between devices by JAX's collectives and lax.ppermute only.
A program may use at most 320 MiB of HBM per device.

```python
import jax
import jax.numpy as jnp

D = 2048
HID = 768
EXPERTS = 64
TOP = 8
TOK_DEV = 32
SECTIONS = 4
TOKENS = 256
CAP = 5
N_DP = 2


def block_route(key, hottest):
    order_key, crowd_key, token_key, column_key = jax.random.split(key, 4)
    labels = jnp.arange(EXPERTS, dtype=jnp.int32)
    ranking = jnp.argsort(jax.random.permutation(order_key, EXPERTS)).astype(jnp.int32)
    hot_rank = ranking[hottest]
    ranking = jnp.where(labels == hottest, 0, jnp.where(ranking < hot_rank, ranking + 1, ranking)).astype(jnp.int32)
    crowded = jax.random.randint(crowd_key, (), 1, EXPERTS // 8 + 1, dtype=jnp.int32)
    leftover = TOK_DEV * TOP - crowded * CAP
    spread = EXPERTS - crowded
    base_count = leftover // spread
    extra_count = leftover - base_count * spread
    by_rank = jnp.where(labels < crowded, CAP, jnp.where(labels - crowded < extra_count, base_count + 1, base_count)).astype(jnp.int32)
    counts = by_rank[ranking]
    listed = jnp.repeat(labels, counts, total_repeat_length=TOK_DEV * TOP)
    dealt_ids = listed.reshape(TOP, TOK_DEV).T
    dealt_ids = dealt_ids[jax.random.permutation(token_key, TOK_DEV)]
    column_keys = jax.random.split(column_key, TOK_DEV)
    return jax.vmap(jax.random.permutation)(column_keys, dealt_ids).astype(jnp.int32)


def section_routes(key):
    blocks = TOKENS // TOK_DEV
    hot_key, block_key = jax.random.split(key)
    hottest = jax.random.randint(hot_key, (), 0, EXPERTS, dtype=jnp.int32)
    block_keys = jax.random.split(block_key, blocks)

    def one_block(single_key):
        return block_route(single_key, hottest)
    return jax.vmap(one_block)(block_keys).reshape(TOKENS, TOP)


def route_table(key):
    section_keys = jax.random.split(key, SECTIONS)
    return jax.vmap(section_routes)(section_keys)


def draw_forward_routes(key, part):
    return route_table(jax.random.fold_in(key, 11))


def draw_backward_routes(key, part):
    return route_table(jax.random.fold_in(key, 23))


def shard_levels(own_key, shape, cuts, least, high):
    loudness, own = 1.0, jax.random.fold_in(own_key, 6)
    for dim, blocks in cuts:
        heights = jnp.exp(jax.random.uniform(jax.random.fold_in(own, dim), (blocks,), jnp.float32, least / len(cuts), high / len(cuts)))
        loudness = loudness * jnp.repeat(heights, shape[dim] // blocks).reshape([-1 if axis == dim else 1 for axis in range(len(shape))])
    return loudness


def scatter_about(own_key, extent, width, bound, cuts=(), kind=jnp.bfloat16):
    array = jax.random.normal(own_key, extent, jnp.float32) * width
    if len(cuts) > 0:
        array = shard_levels(own_key, extent, cuts, -0.22, 0.18) * array
    return jnp.clip(array, min=-bound, max=bound).astype(kind)


def setup_inputs(seed: int = 0) -> dict:
    keys = jax.random.split(jax.random.key(seed), 9)
    section_inputs = scatter_about(keys[0], (SECTIONS, TOKENS, D), 1.0, 6.0, ((0, 4), (1, 8)))
    saved_inputs = scatter_about(keys[1], (SECTIONS, TOKENS, D), 1.0, 6.0, ((0, 4), (1, 8)))
    output_grads = scatter_about(keys[2], (SECTIONS, TOKENS, D), 1.0, 6.0, ((0, 4), (1, 8)))
    forward_routes = draw_forward_routes(jax.random.fold_in(keys[8], 71), 0)
    backward_routes = draw_backward_routes(jax.random.fold_in(keys[8], 71), 0)
    forward_gates = jnp.clip(0.1 + 0.79999997 * jax.random.uniform(keys[5], (SECTIONS, TOKENS, TOP), jnp.float32) ** shard_levels(keys[5], (SECTIONS, TOKENS, TOP), ((0, 4), (1, 8)), -0.2, 0.2), 0.1, 0.9)
    backward_gates = jnp.clip(0.1 + 0.79999997 * jax.random.uniform(keys[6], (SECTIONS, TOKENS, TOP), jnp.float32) ** shard_levels(keys[6], (SECTIONS, TOKENS, TOP), ((0, 4), (1, 8)), -0.2, 0.2), 0.1, 0.9)
    expert_weights = scatter_about(keys[7], (SECTIONS, EXPERTS, D, HID), D ** -0.5, 0.125, ((0, 4), (1, 4)))
    return {"section_inputs": section_inputs, "saved_inputs": saved_inputs, "output_grads": output_grads, "forward_routes": forward_routes, "backward_routes": backward_routes, "forward_gates": forward_gates, "backward_gates": backward_gates, "expert_weights": expert_weights}


def slot_index(routing, experts, capacity):
    one_hot = (routing[..., None] == jnp.arange(experts, dtype=jnp.int32)).astype(jnp.int32)
    before = jnp.cumsum(one_hot, axis=-2) - one_hot
    return (routing * capacity + jnp.sum(before * one_hot, axis=-1)).astype(jnp.int32)


def pack_rows(source, slot_ids, slot_total, spread):
    row_count = slot_ids.shape[0]
    owner_row = jnp.zeros((slot_total,), jnp.int32).at[slot_ids].set(jnp.arange(row_count, dtype=jnp.int32) + 1)
    filled = owner_row > 0
    picked = jnp.take(source, (jnp.maximum(owner_row - 1, 0) // spread).astype(jnp.int32), axis=0)
    return jnp.where(filled[:, None], picked, jnp.zeros_like(picked))


def gather_slots(table, slot_ids):
    return jnp.take(table, slot_ids, axis=0)


def silu_slope(hidden):
    sigma = jax.nn.sigmoid(hidden)
    return sigma * (1.0 + hidden * (1.0 - sigma))


def reference(section_inputs, saved_inputs, output_grads, forward_routes, backward_routes, forward_gates, backward_gates, expert_weights):
    blocks = TOKENS // TOK_DEV
    row_total = TOK_DEV * TOP
    slot_total = EXPERTS * CAP
    halves = blocks // N_DP
    packer = jax.vmap(pack_rows, in_axes=(0, 0, None, None))
    picker = jax.vmap(gather_slots)
    layer_list = []
    grad_list = []
    weight_list = []
    for section_id in range(SECTIONS):
        weights = expert_weights[section_id].astype(jnp.float32)
        inputs = section_inputs[section_id].reshape(blocks, TOK_DEV, D)
        forward_slot = slot_index(forward_routes[section_id].reshape(blocks, row_total), EXPERTS, CAP)
        slot_rows = packer(inputs, forward_slot, slot_total, TOP).reshape(blocks, EXPERTS, CAP, D)
        hidden = jnp.einsum('becd,edf->becf', slot_rows.astype(jnp.float32), weights)
        active = jax.nn.silu(hidden).astype(jnp.bfloat16)
        result = jnp.einsum('becf,edf->becd', active.astype(jnp.float32), weights).astype(jnp.bfloat16)
        picked = picker(result.reshape(blocks, slot_total, D), forward_slot).reshape(blocks, TOK_DEV, TOP, D)
        gate_values = forward_gates[section_id].reshape(blocks, TOK_DEV, TOP, 1)
        layer_out = inputs.astype(jnp.float32) + jnp.sum(gate_values * picked.astype(jnp.float32), axis=2)
        layer_list.append(layer_out.astype(jnp.bfloat16).reshape(TOKENS, D))

        saved_block = saved_inputs[section_id].reshape(blocks, TOK_DEV, D)
        grad_block = output_grads[section_id].reshape(blocks, TOK_DEV, D)
        backward_slot = slot_index(backward_routes[section_id].reshape(blocks, row_total), EXPERTS, CAP)
        saved_rows = packer(saved_block, backward_slot, slot_total, TOP).reshape(blocks, EXPERTS, CAP, D)
        scaled = backward_gates[section_id].reshape(blocks, TOK_DEV, TOP, 1) * grad_block.astype(jnp.float32)[:, :, None, :]
        scaled = scaled.astype(jnp.bfloat16).reshape(blocks, row_total, D)
        slot_grads = packer(scaled, backward_slot, slot_total, 1).reshape(blocks, EXPERTS, CAP, D)
        back_hidden = jnp.einsum('becd,edf->becf', saved_rows.astype(jnp.float32), weights)
        back_active = jax.nn.silu(back_hidden).astype(jnp.bfloat16)
        active_grads = jnp.einsum('becd,edf->becf', slot_grads.astype(jnp.float32), weights)
        hidden_grads = (active_grads * silu_slope(back_hidden)).astype(jnp.bfloat16)
        row_grads = jnp.einsum('becf,edf->becd', hidden_grads.astype(jnp.float32), weights).astype(jnp.bfloat16)
        picked_grads = picker(row_grads.reshape(blocks, slot_total, D), backward_slot).reshape(blocks, TOK_DEV, TOP, D)
        input_grads = grad_block.astype(jnp.float32) + jnp.sum(picked_grads.astype(jnp.float32), axis=2)
        grad_list.append(input_grads.astype(jnp.bfloat16).reshape(TOKENS, D))

        saved_split = saved_rows.reshape(halves, N_DP, EXPERTS, CAP, D).astype(jnp.float32)
        hidden_split = hidden_grads.reshape(halves, N_DP, EXPERTS, CAP, HID).astype(jnp.float32)
        slot_split = slot_grads.reshape(halves, N_DP, EXPERTS, CAP, D).astype(jnp.float32)
        active_split = back_active.reshape(halves, N_DP, EXPERTS, CAP, HID).astype(jnp.float32)
        half_grads = jnp.einsum('bgecd,bgecf->gedf', saved_split, hidden_split) + jnp.einsum('bgecd,bgecf->gedf', slot_split, active_split)
        half_grads = half_grads.astype(jnp.bfloat16)
        weight_list.append(jnp.sum(half_grads.astype(jnp.float32), axis=0).astype(jnp.bfloat16))
    next_inputs = jnp.roll(jnp.stack(layer_list), 1, axis=0)
    prior_grads = jnp.roll(jnp.stack(grad_list), -1, axis=0)
    return next_inputs, prior_grads, jnp.stack(weight_list)
```

```python
import functools

import jax
import jax.numpy as jnp
from jax import lax
from jax.experimental import pallas as pl
from jax.experimental.pallas import tpu as pltpu
from jax.sharding import PartitionSpec as P

CAP = 5
LANES = 128
CHUNK = 256
VMEM_LIMIT = 48 * 1024 * 1024


def shifted(value, axis, steps):
    count = lax.axis_size(axis)
    pairs = [(source, (source + steps) % count) for source in range(count)]
    return lax.ppermute(value, axis, pairs)


def slot_index(routing, experts, capacity):
    one_hot = (routing[..., None] == jnp.arange(experts, dtype=jnp.int32)).astype(jnp.int32)
    before = jnp.cumsum(one_hot, axis=-2) - one_hot
    return routing * capacity + jnp.sum(before * one_hot, axis=-1)


def pack_rows(source, slot_ids, slot_total, spread):
    row_count = slot_ids.shape[0]
    owner_row = (
        jnp.zeros((slot_total,), jnp.int32)
        .at[slot_ids]
        .set(jnp.arange(row_count, dtype=jnp.int32) + 1)
    )
    filled = owner_row > 0
    picked = jnp.take(source, jnp.maximum(owner_row - 1, 0) // spread, axis=0)
    return jnp.where(filled[:, None], picked, jnp.zeros_like(picked))


def expert_forward(slot_rows, weights):
    hidden = jnp.einsum("nlcd,ldh->nlch", slot_rows, weights, preferred_element_type=jnp.float32)
    active = jax.nn.silu(hidden).astype(jnp.bfloat16)
    return jnp.einsum("nlch,ldh->nlcd", active, weights, preferred_element_type=jnp.float32).astype(
        jnp.bfloat16
    )


def expert_backward(saved_rows, slot_grads, weights):
    hidden = jnp.einsum("nlcd,ldh->nlch", saved_rows, weights, preferred_element_type=jnp.float32)
    active = jax.nn.silu(hidden).astype(jnp.bfloat16)
    active_grads = jnp.einsum(
        "nlcd,ldh->nlch", slot_grads, weights, preferred_element_type=jnp.float32
    )
    sigma = jax.nn.sigmoid(hidden)
    hidden_grads = (active_grads * sigma * (1.0 + hidden * (1.0 - sigma))).astype(jnp.bfloat16)
    row_grads = jnp.einsum(
        "nlch,ldh->nlcd", hidden_grads, weights, preferred_element_type=jnp.float32
    ).astype(jnp.bfloat16)
    weight_part = jnp.einsum(
        "nlcd,nlch->ldh", saved_rows, hidden_grads, preferred_element_type=jnp.float32
    )
    weight_part = weight_part + jnp.einsum(
        "nlcd,nlch->ldh", slot_grads, active, preferred_element_type=jnp.float32
    )
    return (row_grads, weight_part)


def packed_plan(
    section_inputs,
    saved_inputs,
    output_grads,
    forward_routes,
    backward_routes,
    forward_gates,
    backward_gates,
    expert_weights,
):
    token_count = section_inputs.shape[1]
    route_count = forward_routes.shape[2]
    local_count = expert_weights.shape[1]
    model_width = expert_weights.shape[2]
    groups = lax.axis_size("expert")
    experts = groups * local_count
    slot_total = experts * CAP
    block_shape = (groups, local_count, CAP, model_width)
    weights = expert_weights[0]
    forward_slot = slot_index(forward_routes[0].reshape(-1), experts, CAP)
    backward_slot = slot_index(backward_routes[0].reshape(-1), experts, CAP)
    forward_rows = pack_rows(section_inputs[0], forward_slot, slot_total, route_count).reshape(
        block_shape
    )
    saved_rows = pack_rows(saved_inputs[0], backward_slot, slot_total, route_count).reshape(
        block_shape
    )
    grad_block = output_grads[0]
    scaled = backward_gates[0][:, :, None] * grad_block.astype(jnp.float32)[:, None, :]
    scaled = scaled.astype(jnp.bfloat16).reshape(token_count * route_count, model_width)
    slot_grads = pack_rows(scaled, backward_slot, slot_total, 1).reshape(block_shape)
    forward_back = lax.all_to_all(
        expert_forward(
            lax.all_to_all(forward_rows, "expert", split_axis=0, concat_axis=0, tiled=True), weights
        ),
        "expert",
        split_axis=0,
        concat_axis=0,
        tiled=True,
    )
    saved_recv, grads_recv = (
        lax.all_to_all(saved_rows, "expert", split_axis=0, concat_axis=0, tiled=True),
        lax.all_to_all(slot_grads, "expert", split_axis=0, concat_axis=0, tiled=True),
    )
    row_grads, weight_part = expert_backward(saved_recv, grads_recv, weights)
    grads_back = lax.all_to_all(row_grads, "expert", split_axis=0, concat_axis=0, tiled=True)
    forward_pick = jnp.take(forward_back.reshape(slot_total, model_width), forward_slot, axis=0)
    forward_pick = forward_pick.reshape(token_count, route_count, model_width).astype(jnp.float32)
    layer_out = section_inputs[0].astype(jnp.float32) + jnp.sum(
        forward_gates[0][:, :, None] * forward_pick, axis=1
    )
    layer_out = layer_out.astype(jnp.bfloat16)
    grads_pick = jnp.take(grads_back.reshape(slot_total, model_width), backward_slot, axis=0)
    grads_pick = grads_pick.reshape(token_count, route_count, model_width).astype(jnp.float32)
    input_grads = (grad_block.astype(jnp.float32) + jnp.sum(grads_pick, axis=1)).astype(
        jnp.bfloat16
    )
    next_inputs = shifted(layer_out, "pipe", 1)[None]
    prior_grads = shifted(input_grads, "pipe", -1)[None]
    weight_grads = lax.psum_scatter(
        weight_part.astype(jnp.bfloat16), "dp", scatter_dimension=1, tiled=True
    )[None]
    return (next_inputs, prior_grads, weight_grads)


def fill_picks(notes_ref, first, count, start, top, slots, picks, gates):
    tokens = notes_ref.shape[0]
    turned = notes_ref[...].T
    ids = (first + lax.broadcasted_iota(jnp.int32, (count, tokens), 0)).astype(jnp.float32)
    named = jnp.zeros((count, tokens), jnp.float32)
    gated = jnp.zeros((count, tokens), jnp.float32)
    for column in range(top):
        same = turned[start + column : start + column + 1, :] == ids
        named = named + jnp.where(same, 1.0, 0.0)
        gated = gated + jnp.where(same, turned[start + top + column : start + top + column + 1, :], 0.0)
    row = lax.broadcasted_iota(jnp.int32, (tokens, tokens), 0)
    column = lax.broadcasted_iota(jnp.int32, (tokens, tokens), 1)
    earlier = jnp.where(row < column, 1.0, 0.0).astype(jnp.bfloat16)
    place = jnp.dot(named.astype(jnp.bfloat16), earlier, preferred_element_type=jnp.float32)
    place = jnp.where(named > 0.0, place, -1.0)
    slot = lax.broadcasted_iota(jnp.int32, (slots, tokens), 0).astype(jnp.float32)
    for expert in range(count):
        rows = pl.ds(expert * slots, slots)
        hit = place[expert : expert + 1, :] == slot
        picks[rows, :] = jnp.where(hit, 1.0, 0.0).astype(jnp.bfloat16)
        own = jnp.sum(jnp.where(hit, gated[expert : expert + 1, :], 0.0), axis=1, keepdims=True)
        gates[rows, :] = jnp.broadcast_to(own, (slots, LANES))


def spread_gate(gates, rows, width):
    return jnp.broadcast_to(gates[rows, 0:1], (gates[rows, 0:1].shape[0], width))


def combine(picks, results, out_ref):
    width = out_ref.shape[1]
    for start in range(0, width, CHUNK):
        columns = pl.ds(start, CHUNK)
        out_ref[:, columns] = lax.dot_general(
            picks[...],
            results[:, columns],
            (((0,), (0,)), ((), ())),
            preferred_element_type=jnp.float32,
        ).astype(out_ref.dtype)


def forward_kernel(
    count, top, slots, place_ref, notes_ref, tokens_ref, weights_ref, out_ref, picks, gates, rows, results
):
    step = pl.program_id(0)
    width = tokens_ref.shape[1]

    @pl.when(step == 0)
    def _():
        fill_picks(notes_ref, place_ref[1], count, 2 * top, top, slots, picks, gates)
        for start in range(0, width, CHUNK):
            columns = pl.ds(start, CHUNK)
            rows[:, columns] = jnp.dot(
                picks[...], tokens_ref[:, columns], preferred_element_type=jnp.float32
            ).astype(rows.dtype)

    mine = pl.ds(pl.multiple_of(step * slots, slots), slots)
    hidden = jnp.dot(rows[mine, :], weights_ref[0], preferred_element_type=jnp.float32)
    active = (hidden * jax.nn.sigmoid(hidden)).astype(jnp.bfloat16)
    result = lax.dot_general(
        active, weights_ref[0], (((1,), (1,)), ((), ())), preferred_element_type=jnp.float32
    )
    results[mine, :] = (result * spread_gate(gates, mine, width)).astype(results.dtype)

    @pl.when(step == count - 1)
    def _():
        combine(picks, results, out_ref)


def backward_kernel(
    count,
    top,
    slots,
    place_ref,
    notes_ref,
    saved_ref,
    grads_ref,
    weights_ref,
    out_ref,
    inner_ref,
    picks,
    gates,
    rows,
    results,
):
    step = pl.program_id(0)
    width = saved_ref.shape[1]

    @pl.when(step == 0)
    def _():
        fill_picks(notes_ref, place_ref[1], count, 0, top, slots, picks, gates)
        gate = spread_gate(gates, pl.ds(0, count * slots), CHUNK)
        for start in range(0, width, CHUNK):
            columns = pl.ds(start, CHUNK)
            saved = jnp.dot(
                picks[...], saved_ref[:, columns], preferred_element_type=jnp.float32
            ).astype(rows.dtype)
            grads = jnp.dot(picks[...], grads_ref[:, columns], preferred_element_type=jnp.float32)
            grads = (grads * gate).astype(rows.dtype)
            for expert in range(count):
                part = slice(expert * slots, (expert + 1) * slots)
                rows[pl.ds(expert * 2 * slots, slots), columns] = saved[part]
                rows[pl.ds(expert * 2 * slots + slots, slots), columns] = grads[part]

    mine = pl.ds(pl.multiple_of(step * slots, slots), slots)
    both = pl.ds(pl.multiple_of(step * 2 * slots, 2 * slots), 2 * slots)
    product = jnp.dot(rows[both, :], weights_ref[0], preferred_element_type=jnp.float32)
    hidden, active_grads = product[:slots], product[slots:]
    sigma = jax.nn.sigmoid(hidden)
    hidden_grads = (active_grads * sigma * (1.0 + hidden * (1.0 - sigma))).astype(jnp.bfloat16)
    inner_ref[0, :slots, :] = hidden_grads
    inner_ref[0, slots:, :] = (hidden * sigma).astype(jnp.bfloat16)
    results[mine, :] = lax.dot_general(
        hidden_grads, weights_ref[0], (((1,), (1,)), ((), ())), preferred_element_type=jnp.float32
    ).astype(results.dtype)

    @pl.when(step == count - 1)
    def _():
        combine(picks, results, out_ref)


def weight_kernel(
    count,
    top,
    slots,
    place_ref,
    notes_ref,
    saved_ref,
    grads_ref,
    own_ref,
    other_ref,
    out_ref,
    picks,
    gates,
    rows,
):
    step = pl.program_id(0)
    width = saved_ref.shape[1]

    def gather(first):
        fill_picks(notes_ref, first, count, 0, top, slots, picks, gates)
        gate = spread_gate(gates, pl.ds(0, count * slots), CHUNK)
        for start in range(0, width, CHUNK):
            columns = pl.ds(start, CHUNK)
            saved = jnp.dot(
                picks[...], saved_ref[:, columns], preferred_element_type=jnp.float32
            ).astype(rows.dtype)
            grads = jnp.dot(picks[...], grads_ref[:, columns], preferred_element_type=jnp.float32)
            grads = (grads * gate).astype(rows.dtype)
            for expert in range(count):
                part = slice(expert * slots, (expert + 1) * slots)
                rows[pl.ds(expert * 2 * slots, slots), columns] = saved[part]
                rows[pl.ds(expert * 2 * slots + slots, slots), columns] = grads[part]

    @pl.when(step == 0)
    def _():
        gather(place_ref[1])

    @pl.when(step == count)
    def _():
        gather(place_ref[2])

    def product(inner):
        index = lax.rem(step, count)
        both = pl.ds(pl.multiple_of(index * 2 * slots, 2 * slots), 2 * slots)
        for start in range(0, width, CHUNK):
            columns = pl.ds(start, CHUNK)
            out_ref[0, columns, :] = lax.dot_general(
                rows[both, columns],
                inner,
                (((0,), (0,)), ((), ())),
                preferred_element_type=jnp.float32,
            ).astype(out_ref.dtype)

    @pl.when(step < count)
    def _():
        product(own_ref[0])

    @pl.when(step >= count)
    def _():
        product(other_ref[0])


def gathered_plan(
    section_inputs,
    saved_inputs,
    output_grads,
    forward_routes,
    backward_routes,
    forward_gates,
    backward_gates,
    expert_weights,
):
    token_count = section_inputs.shape[1]
    top = forward_routes.shape[2]
    _, local_count, width, inner_width = expert_weights.shape
    groups, pair = lax.axis_size("expert"), lax.axis_size("dp")
    count = local_count // pair
    total = groups * pair * token_count
    slots = -(-groups * pair * CAP // 16) * 16
    half = width // pair
    weights = expert_weights[0]

    notes = jnp.concatenate(
        [
            backward_routes[0].astype(jnp.float32),
            backward_gates[0],
            forward_routes[0].astype(jnp.float32),
            forward_gates[0],
            jnp.zeros((token_count, LANES - 4 * top), jnp.float32),
        ],
        axis=1,
    )
    everyone = functools.partial(lax.all_gather, axis_name=("expert", "dp"), axis=0, tiled=True)
    notes_all = everyone(notes)
    inputs_all = everyone(section_inputs[0])
    saved_all = everyone(saved_inputs[0])
    grads_all = everyone(output_grads[0])

    side = lax.axis_index("dp")
    base = lax.axis_index("expert") * local_count
    place = jnp.stack([side, base + side * count, base + (1 - side) * count]).astype(jnp.int32)

    def whole(array):
        return pl.BlockSpec(array.shape, lambda step, place: (0,) * array.ndim)

    weight_spec = pl.BlockSpec(
        (1, width, inner_width), lambda step, place: (place[0] * count + step, 0, 0)
    )
    sums = jax.ShapeDtypeStruct((total, width), jnp.bfloat16)
    params = pltpu.CompilerParams(vmem_limit_bytes=VMEM_LIMIT, dimension_semantics=("arbitrary",))
    pass_flops = 2 * 2 * count * CHUNK * width * inner_width
    weight_bytes = count * width * inner_width * 2

    layer_part = pl.pallas_call(
        functools.partial(forward_kernel, count, top, slots),
        grid_spec=pltpu.PrefetchScalarGridSpec(
            num_scalar_prefetch=1,
            grid=(count,),
            in_specs=[whole(notes_all), whole(inputs_all), weight_spec],
            out_specs=whole(sums),
            scratch_shapes=[
                pltpu.VMEM((count * slots, total), jnp.bfloat16),
                pltpu.VMEM((count * slots, LANES), jnp.float32),
                pltpu.VMEM((count * slots, width), jnp.bfloat16),
                pltpu.VMEM((count * slots, width), jnp.bfloat16),
            ],
        ),
        out_shape=sums,
        compiler_params=params,
        cost_estimate=pl.CostEstimate(
            flops=pass_flops, bytes_accessed=weight_bytes, transcendentals=0
        ),
        name="expert_forward",
    )(place, notes_all, inputs_all, weights)

    inner = jax.ShapeDtypeStruct((count, 2 * slots, inner_width), jnp.bfloat16)
    grad_part, inner_own = pl.pallas_call(
        functools.partial(backward_kernel, count, top, slots),
        grid_spec=pltpu.PrefetchScalarGridSpec(
            num_scalar_prefetch=1,
            grid=(count,),
            in_specs=[whole(notes_all), whole(saved_all), whole(grads_all), weight_spec],
            out_specs=[
                whole(sums),
                pl.BlockSpec((1, 2 * slots, inner_width), lambda step, place: (step, 0, 0)),
            ],
            scratch_shapes=[
                pltpu.VMEM((count * slots, total), jnp.bfloat16),
                pltpu.VMEM((count * slots, LANES), jnp.float32),
                pltpu.VMEM((count * 2 * slots, width), jnp.bfloat16),
                pltpu.VMEM((count * slots, width), jnp.bfloat16),
            ],
        ),
        out_shape=[sums, inner],
        compiler_params=params,
        cost_estimate=pl.CostEstimate(
            flops=pass_flops, bytes_accessed=weight_bytes, transcendentals=0
        ),
        name="expert_backward",
    )(place, notes_all, saved_all, grads_all, weights)
    inner_other = shifted(inner_own, "dp", 1)

    def own_block(step, place):
        return (jnp.minimum(step, count - 1), 0, 0)

    def other_block(step, place):
        return (jnp.maximum(step - count, 0), 0, 0)

    def out_block(step, place):
        side = jnp.where(step < count, place[0], 1 - place[0])
        return (side * count + lax.rem(step, count), 0, 0)

    half_spec = pl.BlockSpec((total, half), lambda step, place: (0, place[0]))
    weight_grads = pl.pallas_call(
        functools.partial(weight_kernel, count, top, slots),
        grid_spec=pltpu.PrefetchScalarGridSpec(
            num_scalar_prefetch=1,
            grid=(2 * count,),
            in_specs=[
                whole(notes_all),
                half_spec,
                half_spec,
                pl.BlockSpec((1, 2 * slots, inner_width), own_block),
                pl.BlockSpec((1, 2 * slots, inner_width), other_block),
            ],
            out_specs=pl.BlockSpec((1, half, inner_width), out_block),
            scratch_shapes=[
                pltpu.VMEM((count * slots, total), jnp.bfloat16),
                pltpu.VMEM((count * slots, LANES), jnp.float32),
                pltpu.VMEM((count * 2 * slots, half), jnp.bfloat16),
            ],
        ),
        out_shape=jax.ShapeDtypeStruct((local_count, half, inner_width), jnp.bfloat16),
        compiler_params=params,
        cost_estimate=pl.CostEstimate(
            flops=pass_flops // 2, bytes_accessed=weight_bytes, transcendentals=0
        ),
        name="weight_gradient",
    )(place, notes_all, saved_all, grads_all, inner_own, inner_other)

    def home(part, own):
        mine = lax.psum_scatter(part, ("expert", "dp"), scatter_dimension=0, tiled=True)
        return (own.astype(jnp.float32) + mine.astype(jnp.float32)).astype(jnp.bfloat16)

    next_inputs = shifted(home(layer_part, section_inputs[0]), "pipe", 1)[None]
    prior_grads = shifted(home(grad_part, output_grads[0]), "pipe", -1)[None]
    return (next_inputs, prior_grads, weight_grads[None])


def on_device(*arrays):
    token_count = arrays[0].shape[1]
    local_count = arrays[-1].shape[1]
    groups, pair = lax.axis_size("expert"), lax.axis_size("dp")
    gathered = groups * token_count
    packed = groups * local_count * CAP
    if gathered <= packed and pair == 2 and local_count % pair == 0:
        return gathered_plan(*arrays)
    return packed_plan(*arrays)


def solution(mesh):
    placed = (
        P("pipe", ("expert", "dp"), None),
        P("pipe", ("expert", "dp"), None),
        P("pipe", ("expert", "dp"), None),
        P("pipe", ("expert", "dp"), None),
        P("pipe", ("expert", "dp"), None),
        P("pipe", ("expert", "dp"), None),
        P("pipe", ("expert", "dp"), None),
        P("pipe", "expert", None, None),
    )
    return jax.shard_map(
        on_device,
        mesh=mesh,
        in_specs=placed,
        out_specs=(
            P("pipe", ("expert", "dp"), None),
            P("pipe", ("expert", "dp"), None),
            P("pipe", "expert", "dp", None),
        ),
        check_vma=False,
    )
```

```python
import functools

import jax
import jax.numpy as jnp
from jax import lax
from jax.experimental import pallas as pl
from jax.experimental.pallas import tpu as pltpu
from jax.sharding import PartitionSpec as P

CAP = 5
LANES = 128
CHUNK = 256
VMEM_LIMIT = 48 * 1024 * 1024


def shifted(value, axis, steps):
    count = lax.axis_size(axis)
    pairs = [(source, (source + steps) % count) for source in range(count)]
    return lax.ppermute(value, axis, pairs)


def slot_index(routing, experts, capacity):
    one_hot = (routing[..., None] == jnp.arange(experts, dtype=jnp.int32)).astype(jnp.int32)
    before = jnp.cumsum(one_hot, axis=-2) - one_hot
    return routing * capacity + jnp.sum(before * one_hot, axis=-1)


def pack_rows(source, slot_ids, slot_total, spread):
    row_count = slot_ids.shape[0]
    owner_row = (
        jnp.zeros((slot_total,), jnp.int32)
        .at[slot_ids]
        .set(jnp.arange(row_count, dtype=jnp.int32) + 1)
    )
    filled = owner_row > 0
    picked = jnp.take(source, jnp.maximum(owner_row - 1, 0) // spread, axis=0)
    return jnp.where(filled[:, None], picked, jnp.zeros_like(picked))


def expert_forward(slot_rows, weights):
    hidden = jnp.einsum("nlcd,ldh->nlch", slot_rows, weights, preferred_element_type=jnp.float32)
    active = jax.nn.silu(hidden).astype(jnp.bfloat16)
    return jnp.einsum("nlch,ldh->nlcd", active, weights, preferred_element_type=jnp.float32).astype(
        jnp.bfloat16
    )


def expert_backward(saved_rows, slot_grads, weights):
    hidden = jnp.einsum("nlcd,ldh->nlch", saved_rows, weights, preferred_element_type=jnp.float32)
    active = jax.nn.silu(hidden).astype(jnp.bfloat16)
    active_grads = jnp.einsum(
        "nlcd,ldh->nlch", slot_grads, weights, preferred_element_type=jnp.float32
    )
    sigma = jax.nn.sigmoid(hidden)
    hidden_grads = (active_grads * sigma * (1.0 + hidden * (1.0 - sigma))).astype(jnp.bfloat16)
    row_grads = jnp.einsum(
        "nlch,ldh->nlcd", hidden_grads, weights, preferred_element_type=jnp.float32
    ).astype(jnp.bfloat16)
    weight_part = jnp.einsum(
        "nlcd,nlch->ldh", saved_rows, hidden_grads, preferred_element_type=jnp.float32
    )
    weight_part = weight_part + jnp.einsum(
        "nlcd,nlch->ldh", slot_grads, active, preferred_element_type=jnp.float32
    )
    return (row_grads, weight_part)


def packed_plan(
    section_inputs,
    saved_inputs,
    output_grads,
    forward_routes,
    backward_routes,
    forward_gates,
    backward_gates,
    expert_weights,
):
    token_count = section_inputs.shape[1]
    route_count = forward_routes.shape[2]
    local_count = expert_weights.shape[1]
    model_width = expert_weights.shape[2]
    groups = lax.axis_size("expert")
    experts = groups * local_count
    slot_total = experts * CAP
    block_shape = (groups, local_count, CAP, model_width)
    weights = expert_weights[0]
    forward_slot = slot_index(forward_routes[0].reshape(-1), experts, CAP)
    backward_slot = slot_index(backward_routes[0].reshape(-1), experts, CAP)
    forward_rows = pack_rows(section_inputs[0], forward_slot, slot_total, route_count).reshape(
        block_shape
    )
    saved_rows = pack_rows(saved_inputs[0], backward_slot, slot_total, route_count).reshape(
        block_shape
    )
    grad_block = output_grads[0]
    scaled = backward_gates[0][:, :, None] * grad_block.astype(jnp.float32)[:, None, :]
    scaled = scaled.astype(jnp.bfloat16).reshape(token_count * route_count, model_width)
    slot_grads = pack_rows(scaled, backward_slot, slot_total, 1).reshape(block_shape)
    forward_back = lax.all_to_all(
        expert_forward(
            lax.all_to_all(forward_rows, "expert", split_axis=0, concat_axis=0, tiled=True), weights
        ),
        "expert",
        split_axis=0,
        concat_axis=0,
        tiled=True,
    )
    saved_recv, grads_recv = (
        lax.all_to_all(saved_rows, "expert", split_axis=0, concat_axis=0, tiled=True),
        lax.all_to_all(slot_grads, "expert", split_axis=0, concat_axis=0, tiled=True),
    )
    row_grads, weight_part = expert_backward(saved_recv, grads_recv, weights)
    grads_back = lax.all_to_all(row_grads, "expert", split_axis=0, concat_axis=0, tiled=True)
    forward_pick = jnp.take(forward_back.reshape(slot_total, model_width), forward_slot, axis=0)
    forward_pick = forward_pick.reshape(token_count, route_count, model_width).astype(jnp.float32)
    layer_out = section_inputs[0].astype(jnp.float32) + jnp.sum(
        forward_gates[0][:, :, None] * forward_pick, axis=1
    )
    layer_out = layer_out.astype(jnp.bfloat16)
    grads_pick = jnp.take(grads_back.reshape(slot_total, model_width), backward_slot, axis=0)
    grads_pick = grads_pick.reshape(token_count, route_count, model_width).astype(jnp.float32)
    input_grads = (grad_block.astype(jnp.float32) + jnp.sum(grads_pick, axis=1)).astype(
        jnp.bfloat16
    )
    next_inputs = shifted(layer_out, "pipe", 1)[None]
    prior_grads = shifted(input_grads, "pipe", -1)[None]
    weight_grads = lax.psum_scatter(
        weight_part.astype(jnp.bfloat16), "dp", scatter_dimension=1, tiled=True
    )[None]
    return (next_inputs, prior_grads, weight_grads)


def swapped(value, code):
    axes = ("expert", "dp")
    count = lax.axis_size(axes[0]) * lax.axis_size(axes[1])
    return lax.ppermute(value, axes, [(source, source ^ code) for source in range(count)])


def notes_kernel(place_ref, back_routes, back_gates, fore_routes, fore_gates, out_ref, spare):
    top, size = back_routes.shape
    spare[...] = jnp.zeros_like(spare)
    for place, ref in enumerate((back_routes, back_gates, fore_routes, fore_gates)):
        spare[pl.ds(place * top, top), 0:size] = ref[...].astype(jnp.float32)
    out_ref[...] = pltpu.roll(spare[...], place_ref[3], axis=1)


def picks_kernel(count, top, slots, place_ref, near_ref, far_ref, *refs):
    outs, turned = refs[:-1], refs[-1]
    tokens = turned.shape[1]
    turned[...] = near_ref[...] + far_ref[...]
    row = lax.broadcasted_iota(jnp.int32, (tokens, tokens), 0)
    column = lax.broadcasted_iota(jnp.int32, (tokens, tokens), 1)
    earlier = jnp.where(row < column, 1.0, 0.0).astype(jnp.bfloat16)
    slot = lax.broadcasted_iota(jnp.int32, (slots, tokens), 0).astype(jnp.float32)

    def fill(first, start, picks, gates, flipped):
        ids = (first + lax.broadcasted_iota(jnp.int32, (count, tokens), 0)).astype(jnp.float32)
        named = jnp.zeros((count, tokens), jnp.float32)
        gated = jnp.zeros((count, tokens), jnp.float32)
        for column in range(start, start + top):
            same = turned[column : column + 1, :] == ids
            named = named + jnp.where(same, 1.0, 0.0)
            gated = gated + jnp.where(same, turned[column + top : column + top + 1, :], 0.0)
        place = jnp.dot(named.astype(jnp.bfloat16), earlier, preferred_element_type=jnp.float32)
        place = jnp.where(named > 0.0, place, -1.0)
        for expert in range(count):
            rows = pl.ds(expert * slots, slots)
            hit = place[expert : expert + 1, :] == slot
            picks[rows, :] = jnp.where(hit, 1.0, 0.0).astype(jnp.bfloat16)
            own = jnp.sum(jnp.where(hit, gated[expert : expert + 1, :], 0.0), axis=1, keepdims=True)
            gates[rows, :] = jnp.broadcast_to(own, (slots, LANES))
        if flipped is not None:
            flipped[...] = picks[...].T

    fill(place_ref[1], 2 * top, outs[0], outs[1], outs[2])
    fill(place_ref[1], 0, outs[3], outs[4], outs[5])
    fill(place_ref[2], 0, outs[6], outs[7], None)


def spread_gate(gates, rows, width):
    gate = gates[rows, 0:1]
    return jnp.broadcast_to(gate, (gate.shape[0], width))


def assemble(place_ref, blocks, tokens, lead):
    for code, block in enumerate(blocks):
        size = block.shape[-2]
        rows = pl.ds(pl.multiple_of(place_ref[3 + code], size), size)
        if lead is None:
            tokens[rows, :] = block[...]
        else:
            tokens[rows, :] = block[lead]


def combine(place_ref, flipped, results, sums, outs):
    width = sums.shape[1]
    for start in range(0, width, CHUNK):
        columns = pl.ds(start, CHUNK)
        sums[:, columns] = jnp.dot(
            flipped[...], results[:, columns], preferred_element_type=jnp.float32
        ).astype(sums.dtype)
    for out, codes in outs:
        size = out.shape[1]
        for lead, code in enumerate(codes):
            rows = pl.ds(pl.multiple_of(place_ref[3 + code], size), size)
            out[lead] = sums[rows, :]


def gather_pairs(count, slots, picks, gates, saved_ref, grads_ref, rows):
    width = saved_ref.shape[1]
    gate = spread_gate(gates, pl.ds(0, count * slots), CHUNK)
    for start in range(0, width, CHUNK):
        columns = pl.ds(start, CHUNK)
        saved = jnp.dot(
            picks[...], saved_ref[:, columns], preferred_element_type=jnp.float32
        ).astype(rows.dtype)
        grads = jnp.dot(picks[...], grads_ref[:, columns], preferred_element_type=jnp.float32)
        grads = (grads * gate).astype(rows.dtype)
        for expert in range(count):
            part = slice(expert * slots, (expert + 1) * slots)
            rows[pl.ds(expert * 2 * slots, slots), columns] = saved[part]
            rows[pl.ds(expert * 2 * slots + slots, slots), columns] = grads[part]


def forward_kernel(count, slots, devices, out_codes, place_ref, *refs):
    picks, gates, flipped, weights_ref = refs[:4]
    blocks = refs[4 : 4 + devices]
    outs = list(zip(refs[4 + devices :], out_codes))
    tokens, rows, results = refs[-3:]
    step = pl.program_id(0)
    width = tokens.shape[1]

    @pl.when(step == 0)
    def _():
        assemble(place_ref, blocks, tokens, None)
        for start in range(0, width, CHUNK):
            columns = pl.ds(start, CHUNK)
            rows[:, columns] = jnp.dot(
                picks[...], tokens[:, columns], preferred_element_type=jnp.float32
            ).astype(rows.dtype)

    mine = pl.ds(pl.multiple_of(step * slots, slots), slots)
    hidden = jnp.dot(rows[mine, :], weights_ref[0], preferred_element_type=jnp.float32)
    active = (hidden * jax.nn.sigmoid(hidden)).astype(jnp.bfloat16)
    result = lax.dot_general(
        active, weights_ref[0], (((1,), (1,)), ((), ())), preferred_element_type=jnp.float32
    )
    results[mine, :] = (result * spread_gate(gates, mine, width)).astype(results.dtype)

    @pl.when(step == count - 1)
    def _():
        combine(place_ref, flipped, results, tokens, outs)


def backward_kernel(count, slots, devices, out_codes, place_ref, *refs):
    picks, gates, flipped, weights_ref = refs[:4]
    blocks = refs[4 : 4 + devices]
    outs = list(zip(refs[4 + devices :], out_codes))
    inner_ref, saved_ref, grads_ref, rows, results = refs[-5:]
    step = pl.program_id(0)

    @pl.when(step == 0)
    def _():
        assemble(place_ref, blocks, saved_ref, 0)
        assemble(place_ref, blocks, grads_ref, 1)
        gather_pairs(count, slots, picks, gates, saved_ref, grads_ref, rows)

    mine = pl.ds(pl.multiple_of(step * slots, slots), slots)
    both = pl.ds(pl.multiple_of(step * 2 * slots, 2 * slots), 2 * slots)
    product = jnp.dot(rows[both, :], weights_ref[0], preferred_element_type=jnp.float32)
    hidden, active_grads = product[:slots], product[slots:]
    sigma = jax.nn.sigmoid(hidden)
    hidden_grads = (active_grads * sigma * (1.0 + hidden * (1.0 - sigma))).astype(jnp.bfloat16)
    inner_ref[0, :slots, :] = hidden_grads
    inner_ref[0, slots:, :] = (hidden * sigma).astype(jnp.bfloat16)
    results[mine, :] = lax.dot_general(
        hidden_grads, weights_ref[0], (((1,), (1,)), ((), ())), preferred_element_type=jnp.float32
    ).astype(results.dtype)

    @pl.when(step == count - 1)
    def _():
        combine(place_ref, flipped, results, saved_ref, outs)


def weight_kernel(count, slots, devices, place_ref, *refs):
    picks, gates, inner_ref = refs[:3]
    blocks = refs[3 : 3 + devices]
    out_ref, saved_ref, grads_ref, rows = refs[-4:]
    step = pl.program_id(0)

    @pl.when(step == 0)
    def _():
        assemble(place_ref, blocks, saved_ref, 0)
        assemble(place_ref, blocks, grads_ref, 1)
        gather_pairs(count, slots, picks, gates, saved_ref, grads_ref, rows)

    both = pl.ds(pl.multiple_of(step * 2 * slots, 2 * slots), 2 * slots)
    flat = rows[both, :].T
    for start in range(0, inner_ref.shape[-1], CHUNK):
        columns = pl.ds(start, CHUNK)
        out_ref[0, :, columns] = jnp.dot(
            flat, inner_ref[0, :, columns], preferred_element_type=jnp.float32
        ).astype(out_ref.dtype)


def gathered_plan(
    section_inputs,
    saved_inputs,
    output_grads,
    forward_routes,
    backward_routes,
    forward_gates,
    backward_gates,
    expert_weights,
):
    token_count = section_inputs.shape[1]
    top = forward_routes.shape[2]
    _, local_count, width, inner_width = expert_weights.shape
    groups, pair = lax.axis_size("expert"), lax.axis_size("dp")
    devices = groups * pair
    count = local_count // pair
    total = devices * token_count
    slots = -(-devices * CAP // 16) * 16
    rows = count * slots
    half = width // pair
    weights = expert_weights[0]

    side, group = lax.axis_index("dp"), lax.axis_index("expert")
    index = group * pair + side
    base = group * local_count
    place = jnp.stack(
        [side, base + side * count, base + (1 - side) * count]
        + [(index ^ code) * token_count for code in range(devices)]
    ).astype(jnp.int32)
    params = pltpu.CompilerParams(vmem_limit_bytes=VMEM_LIMIT, dimension_semantics=("arbitrary",))

    def whole(shape):
        return pl.BlockSpec(shape, lambda *_: (0,) * len(shape))

    def call(kernel, name, steps, in_specs, out_specs, out_shape, scratch, flops=0, aliases=()):
        return pl.pallas_call(
            kernel,
            grid_spec=pltpu.PrefetchScalarGridSpec(
                num_scalar_prefetch=1,
                grid=(steps,),
                in_specs=in_specs,
                out_specs=out_specs,
                scratch_shapes=scratch,
            ),
            out_shape=out_shape,
            compiler_params=params,
            cost_estimate=pl.CostEstimate(
                flops=flops, bytes_accessed=flops // 512 + 1024, transcendentals=0
            ),
            input_output_aliases=dict(aliases),
            name=name,
        )

    def onward(block):
        return swapped(block, 1)

    def across(block):
        return [swapped(block, code) for code in range(pair, devices, pair)]

    def after(first, then):
        then, _ = lax.optimization_barrier((then, first))
        return then

    forward_near = [section_inputs[0]] + across(section_inputs[0])
    forward_far = [onward(block) for block in forward_near]
    inputs_all = [block for both in zip(forward_near, forward_far) for block in both]

    table = jax.ShapeDtypeStruct((4 * top, total), jnp.float32)
    small = whole((top, token_count))
    notes = call(
        notes_kernel,
        "notes",
        1,
        [small] * 4,
        whole(table.shape),
        table,
        [pltpu.VMEM(table.shape, jnp.float32)],
    )(place, backward_routes[0].T, backward_gates[0].T, forward_routes[0].T, forward_gates[0].T)
    code = pair
    while code < devices:
        notes = notes + swapped(notes, code)
        code *= 2
    notes_far = onward(notes)

    pick = jax.ShapeDtypeStruct((rows, total), jnp.bfloat16)
    flip = jax.ShapeDtypeStruct((total, rows), jnp.bfloat16)
    gate = jax.ShapeDtypeStruct((rows, LANES), jnp.float32)
    pick_outs = [pick, gate, flip, pick, gate, flip, pick, gate]
    picks = call(
        functools.partial(picks_kernel, count, top, slots),
        "slot_picks",
        1,
        [whole(table.shape)] * 2,
        [whole(out.shape) for out in pick_outs],
        pick_outs,
        [pltpu.VMEM(table.shape, jnp.float32)],
    )(place, notes, notes_far)
    forward_picks, own_picks, other_picks = picks[:3], picks[3:6], picks[6:]

    backward_own = after(forward_near, jnp.stack([saved_inputs[0], output_grads[0]]))
    backward_near = across(backward_own)

    pick_specs = [whole(pick.shape), whole(gate.shape), whole(flip.shape)]
    weight_spec = pl.BlockSpec(
        (1, width, inner_width), lambda step, place: (place[0] * count + step, 0, 0)
    )
    pass_flops = 2 * 2 * count * CHUNK * width * inner_width
    codes = range(devices)
    tokens = pltpu.VMEM((total, width), jnp.bfloat16)
    slot_rows = pltpu.VMEM((rows, width), jnp.bfloat16)

    chip_block = jax.ShapeDtypeStruct((pair, token_count, width), jnp.bfloat16)
    forward_codes = [codes[first : first + pair] for first in range(0, devices, pair)]
    layer_parts = call(
        functools.partial(forward_kernel, count, slots, devices, forward_codes),
        "expert_forward",
        count,
        pick_specs + [weight_spec] + [whole((token_count, width))] * devices,
        [whole(chip_block.shape)] * groups,
        [chip_block] * groups,
        [tokens, slot_rows, slot_rows],
        pass_flops,
    )(place, *forward_picks, weights, *inputs_all)
    layer_near = [
        swapped(part, code) for part, code in zip(layer_parts[1:], range(pair, devices, pair))
    ]

    backward_near = [backward_own] + after(layer_parts, backward_near)
    backward_far = [onward(block) for block in backward_near]
    backward_all = [block for both in zip(backward_near, backward_far) for block in both]

    inner = jax.ShapeDtypeStruct((count, 2 * slots, inner_width), jnp.bfloat16)
    own_block = jax.ShapeDtypeStruct((1, token_count, width), jnp.bfloat16)
    far_block = jax.ShapeDtypeStruct((groups, token_count, width), jnp.bfloat16)
    backward_codes = [codes[first : first + 1] for first in range(0, devices, pair)]
    backward_codes.append(codes[1::pair])
    *grad_parts, grad_far, inner_own = call(
        functools.partial(backward_kernel, count, slots, devices, backward_codes),
        "expert_backward",
        count,
        pick_specs + [weight_spec] + [whole(backward_own.shape)] * devices,
        [whole(own_block.shape)] * groups
        + [whole(far_block.shape)]
        + [pl.BlockSpec((1, 2 * slots, inner_width), lambda step, place: (step, 0, 0))],
        [own_block] * groups + [far_block, inner],
        [tokens, tokens, pltpu.VMEM((2 * rows, width), jnp.bfloat16), slot_rows],
        pass_flops,
    )(place, *own_picks, weights, *backward_all)
    inner_other = onward(inner_own)
    grad_far = onward(grad_far)

    def summed(*blocks):
        return functools.reduce(jnp.add, [block.astype(jnp.float32) for block in blocks])

    layer_near = after(grad_parts, layer_near)
    layer_mine = summed(layer_parts[0][0], *[block[0] for block in layer_near])
    layer_other = summed(layer_parts[0][1], *[block[1] for block in layer_near])
    layer_other = onward(layer_other.astype(jnp.bfloat16))

    def gradient(whose, inner_rows, picked, earlier):
        out = jax.ShapeDtypeStruct((local_count, half, inner_width), jnp.bfloat16)
        earlier = [] if earlier is None else [earlier]

        def out_block(step, place):
            owner = place[0] if whose == 0 else 1 - place[0]
            return (owner * count + step, 0, 0)

        specs = [
            pick_specs[0],
            pick_specs[1],
            pl.BlockSpec((1, 2 * slots, inner_width), lambda step, place: (step, 0, 0)),
        ]
        specs += [
            pl.BlockSpec((2, token_count, half), lambda step, place: (0, 0, place[0]))
        ] * devices
        specs += [pl.BlockSpec(memory_space=pl.ANY)] * len(earlier)
        half_tokens = pltpu.VMEM((total, half), jnp.bfloat16)
        return call(
            functools.partial(weight_kernel, count, slots, devices),
            "weight_gradient_" + ("own", "other")[whose],
            count,
            specs,
            pl.BlockSpec((1, half, inner_width), out_block),
            out,
            [half_tokens, half_tokens, pltpu.VMEM((2 * rows, half), jnp.bfloat16)],
            pass_flops // 2,
            [(len(specs), 0)] if earlier else [],
        )(place, *picked[:2], inner_rows, *backward_all, *earlier)

    own_done = gradient(0, inner_own, own_picks, None)

    layer_other, grad_far = after(own_done, (layer_other, grad_far))
    layer_out = (summed(section_inputs[0], layer_other) + layer_mine).astype(jnp.bfloat16)
    next_inputs = shifted(layer_out, "pipe", 1)[None]
    grad_sums = [
        summed(part[0], grad_far[place_]).astype(jnp.bfloat16)
        for place_, part in enumerate(grad_parts)
    ]
    grad_near = [
        swapped(part, code) for part, code in zip(grad_sums[1:], range(pair, devices, pair))
    ]
    weight_grads = gradient(1, inner_other, other_picks, own_done)

    grad_near = after(weight_grads, grad_near)
    input_grads = summed(output_grads[0], grad_sums[0], *grad_near).astype(jnp.bfloat16)
    prior_grads = shifted(input_grads, "pipe", -1)[None]
    return (next_inputs, prior_grads, weight_grads[None])


def on_device(*arrays):
    token_count = arrays[0].shape[1]
    local_count = arrays[-1].shape[1]
    groups, pair = lax.axis_size("expert"), lax.axis_size("dp")
    gathered = groups * token_count
    packed = groups * local_count * CAP
    paired = pair == 2 and local_count % pair == 0 and groups & (groups - 1) == 0
    if gathered <= packed and paired and gathered * pair % LANES == 0:
        return gathered_plan(*arrays)
    return packed_plan(*arrays)


def solution(mesh):
    placed = (
        P("pipe", ("expert", "dp"), None),
        P("pipe", ("expert", "dp"), None),
        P("pipe", ("expert", "dp"), None),
        P("pipe", ("expert", "dp"), None),
        P("pipe", ("expert", "dp"), None),
        P("pipe", ("expert", "dp"), None),
        P("pipe", ("expert", "dp"), None),
        P("pipe", "expert", None, None),
    )
    return jax.shard_map(
        on_device,
        mesh=mesh,
        in_specs=placed,
        out_specs=(
            P("pipe", ("expert", "dp"), None),
            P("pipe", ("expert", "dp"), None),
            P("pipe", "expert", "dp", None),
        ),
        check_vma=False,
    )
```

```python
import functools

import jax
import jax.numpy as jnp
from jax import lax
from jax.experimental import pallas as pl
from jax.experimental.pallas import tpu as pltpu
from jax.sharding import PartitionSpec as P

CAP = 5
LANES = 128
CHUNK = 256
VMEM_LIMIT = 48 * 1024 * 1024


def shifted(value, axis, steps):
    count = lax.axis_size(axis)
    pairs = [(source, (source + steps) % count) for source in range(count)]
    return lax.ppermute(value, axis, pairs)


def slot_index(routing, experts, capacity):
    one_hot = (routing[..., None] == jnp.arange(experts, dtype=jnp.int32)).astype(jnp.int32)
    before = jnp.cumsum(one_hot, axis=-2) - one_hot
    return routing * capacity + jnp.sum(before * one_hot, axis=-1)


def pack_rows(source, slot_ids, slot_total, spread):
    row_count = slot_ids.shape[0]
    owner_row = (
        jnp.zeros((slot_total,), jnp.int32)
        .at[slot_ids]
        .set(jnp.arange(row_count, dtype=jnp.int32) + 1)
    )
    filled = owner_row > 0
    picked = jnp.take(source, jnp.maximum(owner_row - 1, 0) // spread, axis=0)
    return jnp.where(filled[:, None], picked, jnp.zeros_like(picked))


def expert_forward(slot_rows, weights):
    hidden = jnp.einsum("nlcd,ldh->nlch", slot_rows, weights, preferred_element_type=jnp.float32)
    active = jax.nn.silu(hidden).astype(jnp.bfloat16)
    return jnp.einsum("nlch,ldh->nlcd", active, weights, preferred_element_type=jnp.float32).astype(
        jnp.bfloat16
    )


def expert_backward(saved_rows, slot_grads, weights):
    hidden = jnp.einsum("nlcd,ldh->nlch", saved_rows, weights, preferred_element_type=jnp.float32)
    active = jax.nn.silu(hidden).astype(jnp.bfloat16)
    active_grads = jnp.einsum(
        "nlcd,ldh->nlch", slot_grads, weights, preferred_element_type=jnp.float32
    )
    sigma = jax.nn.sigmoid(hidden)
    hidden_grads = (active_grads * sigma * (1.0 + hidden * (1.0 - sigma))).astype(jnp.bfloat16)
    row_grads = jnp.einsum(
        "nlch,ldh->nlcd", hidden_grads, weights, preferred_element_type=jnp.float32
    ).astype(jnp.bfloat16)
    weight_part = jnp.einsum(
        "nlcd,nlch->ldh", saved_rows, hidden_grads, preferred_element_type=jnp.float32
    )
    weight_part = weight_part + jnp.einsum(
        "nlcd,nlch->ldh", slot_grads, active, preferred_element_type=jnp.float32
    )
    return (row_grads, weight_part)


def packed_plan(
    section_inputs,
    saved_inputs,
    output_grads,
    forward_routes,
    backward_routes,
    forward_gates,
    backward_gates,
    expert_weights,
):
    token_count = section_inputs.shape[1]
    route_count = forward_routes.shape[2]
    local_count = expert_weights.shape[1]
    model_width = expert_weights.shape[2]
    groups = lax.axis_size("expert")
    experts = groups * local_count
    slot_total = experts * CAP
    block_shape = (groups, local_count, CAP, model_width)
    weights = expert_weights[0]
    forward_slot = slot_index(forward_routes[0].reshape(-1), experts, CAP)
    backward_slot = slot_index(backward_routes[0].reshape(-1), experts, CAP)
    forward_rows = pack_rows(section_inputs[0], forward_slot, slot_total, route_count).reshape(
        block_shape
    )
    saved_rows = pack_rows(saved_inputs[0], backward_slot, slot_total, route_count).reshape(
        block_shape
    )
    grad_block = output_grads[0]
    scaled = backward_gates[0][:, :, None] * grad_block.astype(jnp.float32)[:, None, :]
    scaled = scaled.astype(jnp.bfloat16).reshape(token_count * route_count, model_width)
    slot_grads = pack_rows(scaled, backward_slot, slot_total, 1).reshape(block_shape)
    forward_back = lax.all_to_all(
        expert_forward(
            lax.all_to_all(forward_rows, "expert", split_axis=0, concat_axis=0, tiled=True), weights
        ),
        "expert",
        split_axis=0,
        concat_axis=0,
        tiled=True,
    )
    saved_recv, grads_recv = (
        lax.all_to_all(saved_rows, "expert", split_axis=0, concat_axis=0, tiled=True),
        lax.all_to_all(slot_grads, "expert", split_axis=0, concat_axis=0, tiled=True),
    )
    row_grads, weight_part = expert_backward(saved_recv, grads_recv, weights)
    grads_back = lax.all_to_all(row_grads, "expert", split_axis=0, concat_axis=0, tiled=True)
    forward_pick = jnp.take(forward_back.reshape(slot_total, model_width), forward_slot, axis=0)
    forward_pick = forward_pick.reshape(token_count, route_count, model_width).astype(jnp.float32)
    layer_out = section_inputs[0].astype(jnp.float32) + jnp.sum(
        forward_gates[0][:, :, None] * forward_pick, axis=1
    )
    layer_out = layer_out.astype(jnp.bfloat16)
    grads_pick = jnp.take(grads_back.reshape(slot_total, model_width), backward_slot, axis=0)
    grads_pick = grads_pick.reshape(token_count, route_count, model_width).astype(jnp.float32)
    input_grads = (grad_block.astype(jnp.float32) + jnp.sum(grads_pick, axis=1)).astype(
        jnp.bfloat16
    )
    next_inputs = shifted(layer_out, "pipe", 1)[None]
    prior_grads = shifted(input_grads, "pipe", -1)[None]
    weight_grads = lax.psum_scatter(
        weight_part.astype(jnp.bfloat16), "dp", scatter_dimension=1, tiled=True
    )[None]
    return (next_inputs, prior_grads, weight_grads)


def swapped(value, code):
    axes = ("expert", "dp")
    count = lax.axis_size(axes[0]) * lax.axis_size(axes[1])
    return lax.ppermute(value, axes, [(source, source ^ code) for source in range(count)])


def pack_kernel(fore_tokens, saved, grads, back_routes, back_gates, fore_routes, fore_gates, out_ref, notes):
    size, width = fore_tokens.shape
    top = back_routes.shape[0]
    for place, ref in enumerate((fore_tokens, saved, grads)):
        out_ref[:, pl.ds(place * width, width)] = ref[...]
    notes[...] = jnp.zeros_like(notes)
    for place, (routes, gates) in enumerate(((back_routes, back_gates), (fore_routes, fore_gates))):
        first = place * 4 * top
        notes[pl.ds(first, top), 0:size] = routes[...].astype(jnp.float32)
        rest = gates[...]
        for term in range(1, 4):
            part = rest.astype(jnp.bfloat16).astype(jnp.float32)
            notes[pl.ds(first + term * top, top), 0:size] = part
            rest = rest - part
    out_ref[:, pl.ds(3 * width, LANES)] = notes[...].T[:size, :].astype(jnp.bfloat16)


def picks_kernel(count, top, slots, devices, place_ref, *refs):
    blocks, outs, (notes, turned) = refs[:devices], refs[devices:-2], refs[-2:]
    tokens = notes.shape[0]
    for code, block in enumerate(blocks):
        size = block.shape[0]
        rows = pl.ds(pl.multiple_of(place_ref[3 + code], size), size)
        notes[rows, :] = block[...].astype(jnp.float32)
    turned[...] = notes[...].T
    row = lax.broadcasted_iota(jnp.int32, (tokens, tokens), 0)
    column = lax.broadcasted_iota(jnp.int32, (tokens, tokens), 1)
    earlier = jnp.where(row < column, 1.0, 0.0).astype(jnp.bfloat16)
    slot = lax.broadcasted_iota(jnp.int32, (slots, tokens), 0).astype(jnp.float32)

    def fill(first, start, picks, gates, flipped):
        ids = (first + lax.broadcasted_iota(jnp.int32, (count, tokens), 0)).astype(jnp.float32)
        named = jnp.zeros((count, tokens), jnp.float32)
        gated = jnp.zeros((count, tokens), jnp.float32)
        for column in range(start, start + top):
            same = turned[column : column + 1, :] == ids
            terms = [turned[column + term * top : column + term * top + 1, :] for term in (1, 2, 3)]
            named = named + jnp.where(same, 1.0, 0.0)
            gated = gated + jnp.where(same, terms[0] + terms[1] + terms[2], 0.0)
        place = jnp.dot(named.astype(jnp.bfloat16), earlier, preferred_element_type=jnp.float32)
        place = jnp.where(named > 0.0, place, -1.0)
        for expert in range(count):
            rows = pl.ds(expert * slots, slots)
            hit = place[expert : expert + 1, :] == slot
            picks[rows, :] = jnp.where(hit, 1.0, 0.0).astype(jnp.bfloat16)
            own = jnp.sum(jnp.where(hit, gated[expert : expert + 1, :], 0.0), axis=1, keepdims=True)
            gates[rows, :] = jnp.broadcast_to(own, (slots, LANES))
        if flipped is not None:
            flipped[...] = picks[...].T

    fill(place_ref[1], 4 * top, outs[0], outs[1], outs[2])
    fill(place_ref[1], 0, outs[3], outs[4], outs[5])
    fill(place_ref[2], 0, outs[6], outs[7], None)


def spread_gate(gates, rows, width):
    gate = gates[rows, 0:1]
    return jnp.broadcast_to(gate, (gate.shape[0], width))


def assemble(place_ref, blocks, columns, tokens):
    for code, block in enumerate(blocks):
        size = block.shape[0]
        rows = pl.ds(pl.multiple_of(place_ref[3 + code], size), size)
        tokens[rows, :] = block[:, columns]


def combine(place_ref, flipped, results, sums, outs):
    width = sums.shape[1]
    for start in range(0, width, CHUNK):
        columns = pl.ds(start, CHUNK)
        sums[:, columns] = jnp.dot(
            flipped[...], results[:, columns], preferred_element_type=jnp.float32
        ).astype(sums.dtype)
    for out, lead, code in outs:
        size = out.shape[-2]
        rows = pl.ds(pl.multiple_of(place_ref[3 + code], size), size)
        out[lead] = sums[rows, :]


def gather(count, slots, picks, gates, tokens_ref, rows, first, stride):
    width = tokens_ref.shape[1]
    for start in range(0, width, CHUNK):
        columns = pl.ds(start, CHUNK)
        taken = jnp.dot(picks[...], tokens_ref[:, columns], preferred_element_type=jnp.float32)
        if gates is not None:
            taken = taken * spread_gate(gates, pl.ds(0, count * slots), CHUNK)
        taken = taken.astype(rows.dtype)
        for expert in range(count):
            part = slice(expert * slots, (expert + 1) * slots)
            rows[pl.ds(first + expert * stride, slots), columns] = taken[part]


def expert_kernel(count, slots, devices, pair, place_ref, *refs):
    fore_picks, fore_gates, fore_flip, back_picks, back_gates, back_flip, weights_ref = refs[:7]
    blocks = refs[7 : 7 + devices]
    near_outs = refs[7 + devices : 7 + devices + devices // pair]
    far_out, inner_ref, tokens, rows, fore_results, back_results, second = refs[-7:]
    step = pl.program_id(0)
    width = tokens.shape[1]

    @pl.when(step == 0)
    def _():
        taken = ((fore_picks, None), (back_picks, None), (back_picks, back_gates))
        for place, (picks, gates) in enumerate(taken):
            assemble(place_ref, blocks, pl.ds(place * width, width), tokens)
            gather(count, slots, picks, gates, tokens, rows, place * slots, 3 * slots)

    mine = pl.ds(pl.multiple_of(step * slots, slots), slots)
    three = pl.ds(pl.multiple_of(step * 3 * slots, 3 * slots), 3 * slots)
    product = jnp.dot(rows[three, :], weights_ref[0], preferred_element_type=jnp.float32)
    ahead, hidden, active_grads = product[:slots], product[slots : 2 * slots], product[2 * slots :]
    sigma = jax.nn.sigmoid(hidden)
    hidden_grads = (active_grads * sigma * (1.0 + hidden * (1.0 - sigma))).astype(jnp.bfloat16)
    inner_ref[0, :slots, :] = hidden_grads
    inner_ref[0, slots:, :] = (hidden * sigma).astype(jnp.bfloat16)
    second[:slots, :] = (ahead * jax.nn.sigmoid(ahead)).astype(jnp.bfloat16)
    second[slots:, :] = hidden_grads
    result = lax.dot_general(
        second[...], weights_ref[0], (((1,), (1,)), ((), ())), preferred_element_type=jnp.float32
    )
    fore_results[mine, :] = (result[:slots] * spread_gate(fore_gates, mine, width)).astype(
        fore_results.dtype
    )
    back_results[mine, :] = result[slots:].astype(back_results.dtype)

    @pl.when(step == count - 1)
    def _():
        for lead, (flipped, results) in enumerate(((fore_flip, fore_results), (back_flip, back_results))):
            outs = [(out, lead, pair * group) for group, out in enumerate(near_outs)]
            outs += [(far_out, (group, lead), pair * group + 1) for group in range(len(near_outs))]
            combine(place_ref, flipped, results, tokens, outs)


def weight_kernel(count, slots, devices, place_ref, *refs):
    picks, gates, inner_ref = refs[:3]
    saved, grads = refs[3 : 3 + devices], refs[3 + devices : 3 + 2 * devices]
    out_ref, tokens, rows = refs[-3:]
    step = pl.program_id(0)
    half = tokens.shape[1]

    @pl.when(step == 0)
    def _():
        for place, (blocks, scale) in enumerate(((saved, None), (grads, gates))):
            assemble(place_ref, blocks, pl.ds(0, half), tokens)
            gather(count, slots, picks, scale, tokens, rows, place * slots, 2 * slots)

    both = pl.ds(pl.multiple_of(step * 2 * slots, 2 * slots), 2 * slots)
    flat = rows[both, :].T
    for start in range(0, inner_ref.shape[-1], CHUNK):
        columns = pl.ds(start, CHUNK)
        out_ref[0, :, columns] = jnp.dot(
            flat, inner_ref[0, :, columns], preferred_element_type=jnp.float32
        ).astype(out_ref.dtype)


def gathered_plan(
    section_inputs,
    saved_inputs,
    output_grads,
    forward_routes,
    backward_routes,
    forward_gates,
    backward_gates,
    expert_weights,
):
    token_count = section_inputs.shape[1]
    top = forward_routes.shape[2]
    _, local_count, width, inner_width = expert_weights.shape
    groups, pair = lax.axis_size("expert"), lax.axis_size("dp")
    devices = groups * pair
    count = local_count // pair
    total = devices * token_count
    slots = -(-devices * CAP // 16) * 16
    rows = count * slots
    half = width // pair
    weights = expert_weights[0]

    side, group = lax.axis_index("dp"), lax.axis_index("expert")
    index = group * pair + side
    base = group * local_count
    place = jnp.stack(
        [side, base + side * count, base + (1 - side) * count]
        + [(index ^ code) * token_count for code in range(devices)]
    ).astype(jnp.int32)
    params = pltpu.CompilerParams(vmem_limit_bytes=VMEM_LIMIT, dimension_semantics=("arbitrary",))

    def whole(shape):
        return pl.BlockSpec(shape, lambda *_: (0,) * len(shape))

    def call(kernel, name, steps, in_specs, out_specs, out_shape, scratch, flops=0, aliases=()):
        return pl.pallas_call(
            kernel,
            grid_spec=pltpu.PrefetchScalarGridSpec(
                num_scalar_prefetch=1,
                grid=(steps,),
                in_specs=in_specs,
                out_specs=out_specs,
                scratch_shapes=scratch,
            ),
            out_shape=out_shape,
            compiler_params=params,
            cost_estimate=pl.CostEstimate(
                flops=flops, bytes_accessed=flops // 512 + 1024, transcendentals=0
            ),
            input_output_aliases=dict(aliases),
            name=name,
        )

    def onward(block):
        return swapped(block, 1)

    def across(parts):
        return [swapped(part, code) for part, code in zip(parts, range(pair, devices, pair))]

    def after(first, then):
        then, _ = lax.optimization_barrier((then, first))
        return then

    def summed(*blocks):
        return functools.reduce(jnp.add, [block.astype(jnp.float32) for block in blocks])

    packed = jax.ShapeDtypeStruct((token_count, 3 * width + LANES), jnp.bfloat16)
    own = pl.pallas_call(
        pack_kernel,
        in_specs=[pl.BlockSpec(memory_space=pltpu.VMEM)] * 7,
        out_specs=pl.BlockSpec(memory_space=pltpu.VMEM),
        out_shape=packed,
        scratch_shapes=[pltpu.VMEM((LANES, LANES), jnp.float32)],
        compiler_params=pltpu.CompilerParams(vmem_limit_bytes=VMEM_LIMIT),
        name="pack",
    )(
        section_inputs[0],
        saved_inputs[0],
        output_grads[0],
        backward_routes[0].T,
        backward_gates[0].T,
        forward_routes[0].T,
        forward_gates[0].T,
    )
    near = [own] + across([own] * (groups - 1))
    blocks = [block for one in near for block in (one, onward(one))]

    pick = jax.ShapeDtypeStruct((rows, total), jnp.bfloat16)
    flip = jax.ShapeDtypeStruct((total, rows), jnp.bfloat16)
    gate = jax.ShapeDtypeStruct((rows, LANES), jnp.float32)
    pick_outs = [pick, gate, flip, pick, gate, flip, pick, gate]
    picks = call(
        functools.partial(picks_kernel, count, top, slots, devices),
        "slot_picks",
        1,
        [pl.BlockSpec((token_count, LANES), lambda *_: (0, 3 * width // LANES))] * devices,
        [whole(out.shape) for out in pick_outs],
        pick_outs,
        [pltpu.VMEM((total, LANES), jnp.float32), pltpu.VMEM((LANES, total), jnp.float32)],
    )(place, *blocks)

    pass_flops = 2 * 2 * count * CHUNK * width * inner_width
    near_part = jax.ShapeDtypeStruct((2, token_count, width), jnp.bfloat16)
    far_part = jax.ShapeDtypeStruct((groups, 2, token_count, width), jnp.bfloat16)
    inner = jax.ShapeDtypeStruct((count, 2 * slots, inner_width), jnp.bfloat16)
    inner_spec = pl.BlockSpec((1, 2 * slots, inner_width), lambda step, place: (step, 0, 0))
    *near_parts, far_sums, inner_own = call(
        functools.partial(expert_kernel, count, slots, devices, pair),
        "experts",
        count,
        [whole(array.shape) for array in picks[:6]]
        + [pl.BlockSpec((1, width, inner_width), lambda step, place: (place[0] * count + step, 0, 0))]
        + [whole(packed.shape)] * devices,
        [whole(near_part.shape)] * groups + [whole(far_part.shape), inner_spec],
        [near_part] * groups + [far_part, inner],
        [
            pltpu.VMEM((total, width), jnp.bfloat16),
            pltpu.VMEM((3 * rows, width), jnp.bfloat16),
            pltpu.VMEM((rows, width), jnp.bfloat16),
            pltpu.VMEM((rows, width), jnp.bfloat16),
            pltpu.VMEM((2 * slots, inner_width), jnp.bfloat16),
        ],
        pass_flops,
    )(place, *picks[:6], weights, *blocks)
    far_sums = onward(far_sums)
    inner_other = onward(inner_own)

    def gradient(whose, inner_rows, picked, earlier):
        earlier = [] if earlier is None else [earlier]

        def out_block(step, place):
            owner = place[0] if whose == 0 else 1 - place[0]
            return (owner * count + step, 0, 0)

        specs = [whole(pick.shape), whole(gate.shape), inner_spec]
        for first in (pair, 2 * pair):
            specs += [
                pl.BlockSpec((token_count, half), lambda step, place, first=first: (0, first + place[0]))
            ] * devices
        specs += [pl.BlockSpec(memory_space=pl.ANY)] * len(earlier)
        return call(
            functools.partial(weight_kernel, count, slots, devices),
            "weight_gradient_" + ("own", "other")[whose],
            count,
            specs,
            pl.BlockSpec((1, half, inner_width), out_block),
            jax.ShapeDtypeStruct((local_count, half, inner_width), jnp.bfloat16),
            [pltpu.VMEM((total, half), jnp.bfloat16), pltpu.VMEM((2 * rows, half), jnp.bfloat16)],
            pass_flops // 2,
            [(len(specs), 0)] if earlier else [],
        )(place, *picked, inner_rows, *blocks, *blocks, *earlier)

    own_done = gradient(0, inner_own, picks[3:5], None)
    far_sums = after(own_done, far_sums)
    sums = [
        summed(part, far_sums[group]).astype(jnp.bfloat16) for group, part in enumerate(near_parts)
    ]
    near_sums = across(sums[1:])
    weight_grads = gradient(1, inner_other, picks[6:8], own_done)
    near_sums = after(weight_grads, near_sums)
    moved = summed(sums[0], *near_sums)
    layer_out = (section_inputs[0].astype(jnp.float32) + moved[0]).astype(jnp.bfloat16)
    input_grads = (output_grads[0].astype(jnp.float32) + moved[1]).astype(jnp.bfloat16)
    next_inputs = shifted(layer_out, "pipe", 1)[None]
    prior_grads = shifted(input_grads, "pipe", -1)[None]
    return (next_inputs, prior_grads, weight_grads[None])


def on_device(*arrays):
    token_count = arrays[0].shape[1]
    local_count = arrays[-1].shape[1]
    groups, pair = lax.axis_size("expert"), lax.axis_size("dp")
    gathered = groups * token_count
    packed = groups * local_count * CAP
    paired = pair == 2 and local_count % pair == 0 and groups & (groups - 1) == 0
    if gathered <= packed and paired and gathered * pair % LANES == 0:
        return gathered_plan(*arrays)
    return packed_plan(*arrays)


def solution(mesh):
    placed = (
        P("pipe", ("expert", "dp"), None),
        P("pipe", ("expert", "dp"), None),
        P("pipe", ("expert", "dp"), None),
        P("pipe", ("expert", "dp"), None),
        P("pipe", ("expert", "dp"), None),
        P("pipe", ("expert", "dp"), None),
        P("pipe", ("expert", "dp"), None),
        P("pipe", "expert", None, None),
    )
    return jax.shard_map(
        on_device,
        mesh=mesh,
        in_specs=placed,
        out_specs=(
            P("pipe", ("expert", "dp"), None),
            P("pipe", ("expert", "dp"), None),
            P("pipe", "expert", "dp", None),
        ),
        check_vma=False,
    )
```

```python
import functools

import jax
import jax.numpy as jnp
from jax import lax
from jax.experimental import pallas as pl
from jax.experimental.pallas import tpu as pltpu
from jax.sharding import PartitionSpec as P

CAP = 5
LANES = 128
CHUNK = 256
VMEM_LIMIT = 24 * 1024 * 1024
EXPERTS_LIMIT = 44 * 1024 * 1024
WIDE_LIMIT = 60 * 1024 * 1024
WEIGHT_CUTS = 4


def shifted(value, axis, steps):
    count = lax.axis_size(axis)
    pairs = [(source, (source + steps) % count) for source in range(count)]
    return lax.ppermute(value, axis, pairs)


def slot_index(routing, experts, capacity):
    one_hot = (routing[..., None] == jnp.arange(experts, dtype=jnp.int32)).astype(jnp.int32)
    before = jnp.cumsum(one_hot, axis=-2) - one_hot
    return routing * capacity + jnp.sum(before * one_hot, axis=-1)


def pack_rows(source, slot_ids, slot_total, spread):
    row_count = slot_ids.shape[0]
    owner_row = (
        jnp.zeros((slot_total,), jnp.int32)
        .at[slot_ids]
        .set(jnp.arange(row_count, dtype=jnp.int32) + 1)
    )
    filled = owner_row > 0
    picked = jnp.take(source, jnp.maximum(owner_row - 1, 0) // spread, axis=0)
    return jnp.where(filled[:, None], picked, jnp.zeros_like(picked))


def expert_forward(slot_rows, weights):
    hidden = jnp.einsum("nlcd,ldh->nlch", slot_rows, weights, preferred_element_type=jnp.float32)
    active = jax.nn.silu(hidden).astype(jnp.bfloat16)
    return jnp.einsum("nlch,ldh->nlcd", active, weights, preferred_element_type=jnp.float32).astype(
        jnp.bfloat16
    )


def expert_backward(saved_rows, slot_grads, weights):
    hidden = jnp.einsum("nlcd,ldh->nlch", saved_rows, weights, preferred_element_type=jnp.float32)
    active = jax.nn.silu(hidden).astype(jnp.bfloat16)
    active_grads = jnp.einsum(
        "nlcd,ldh->nlch", slot_grads, weights, preferred_element_type=jnp.float32
    )
    sigma = jax.nn.sigmoid(hidden)
    hidden_grads = (active_grads * sigma * (1.0 + hidden * (1.0 - sigma))).astype(jnp.bfloat16)
    row_grads = jnp.einsum(
        "nlch,ldh->nlcd", hidden_grads, weights, preferred_element_type=jnp.float32
    ).astype(jnp.bfloat16)
    weight_part = jnp.einsum(
        "nlcd,nlch->ldh", saved_rows, hidden_grads, preferred_element_type=jnp.float32
    )
    weight_part = weight_part + jnp.einsum(
        "nlcd,nlch->ldh", slot_grads, active, preferred_element_type=jnp.float32
    )
    return (row_grads, weight_part)


def packed_plan(
    section_inputs,
    saved_inputs,
    output_grads,
    forward_routes,
    backward_routes,
    forward_gates,
    backward_gates,
    expert_weights,
):
    token_count = section_inputs.shape[1]
    route_count = forward_routes.shape[2]
    local_count = expert_weights.shape[1]
    model_width = expert_weights.shape[2]
    groups = lax.axis_size("expert")
    experts = groups * local_count
    slot_total = experts * CAP
    block_shape = (groups, local_count, CAP, model_width)
    weights = expert_weights[0]
    forward_slot = slot_index(forward_routes[0].reshape(-1), experts, CAP)
    backward_slot = slot_index(backward_routes[0].reshape(-1), experts, CAP)
    forward_rows = pack_rows(section_inputs[0], forward_slot, slot_total, route_count).reshape(
        block_shape
    )
    saved_rows = pack_rows(saved_inputs[0], backward_slot, slot_total, route_count).reshape(
        block_shape
    )
    grad_block = output_grads[0]
    scaled = backward_gates[0][:, :, None] * grad_block.astype(jnp.float32)[:, None, :]
    scaled = scaled.astype(jnp.bfloat16).reshape(token_count * route_count, model_width)
    slot_grads = pack_rows(scaled, backward_slot, slot_total, 1).reshape(block_shape)
    forward_back = lax.all_to_all(
        expert_forward(
            lax.all_to_all(forward_rows, "expert", split_axis=0, concat_axis=0, tiled=True), weights
        ),
        "expert",
        split_axis=0,
        concat_axis=0,
        tiled=True,
    )
    saved_recv, grads_recv = (
        lax.all_to_all(saved_rows, "expert", split_axis=0, concat_axis=0, tiled=True),
        lax.all_to_all(slot_grads, "expert", split_axis=0, concat_axis=0, tiled=True),
    )
    row_grads, weight_part = expert_backward(saved_recv, grads_recv, weights)
    grads_back = lax.all_to_all(row_grads, "expert", split_axis=0, concat_axis=0, tiled=True)
    forward_pick = jnp.take(forward_back.reshape(slot_total, model_width), forward_slot, axis=0)
    forward_pick = forward_pick.reshape(token_count, route_count, model_width).astype(jnp.float32)
    layer_out = section_inputs[0].astype(jnp.float32) + jnp.sum(
        forward_gates[0][:, :, None] * forward_pick, axis=1
    )
    layer_out = layer_out.astype(jnp.bfloat16)
    grads_pick = jnp.take(grads_back.reshape(slot_total, model_width), backward_slot, axis=0)
    grads_pick = grads_pick.reshape(token_count, route_count, model_width).astype(jnp.float32)
    input_grads = (grad_block.astype(jnp.float32) + jnp.sum(grads_pick, axis=1)).astype(
        jnp.bfloat16
    )
    next_inputs = shifted(layer_out, "pipe", 1)[None]
    prior_grads = shifted(input_grads, "pipe", -1)[None]
    weight_grads = lax.psum_scatter(
        weight_part.astype(jnp.bfloat16), "dp", scatter_dimension=1, tiled=True
    )[None]
    return (next_inputs, prior_grads, weight_grads)


def swapped(value, code):
    axes = ("expert", "dp")
    count = lax.axis_size(axes[0]) * lax.axis_size(axes[1])
    return lax.ppermute(value, axes, [(source, source ^ code) for source in range(count)])


def pack_kernel(*refs):
    sources, out_ref, (*held, notes, done) = refs[:7], refs[7], refs[8:]
    size, width = sources[0].shape
    top = sources[3].shape[0]
    targets = [out_ref.at[:, pl.ds(place * width, width)] for place in range(3)] + held
    copies = [
        pltpu.make_async_copy(source, target, done.at[place])
        for place, (source, target) in enumerate(zip(sources, targets))
    ]
    for copy in copies:
        copy.start()
    for copy in copies:
        copy.wait()
    back_routes, back_gates, fore_routes, fore_gates = held
    notes[...] = jnp.zeros_like(notes)
    for place, (routes, gates) in enumerate(((back_routes, back_gates), (fore_routes, fore_gates))):
        first = place * 4 * top
        notes[pl.ds(first, top), 0:size] = routes[...].astype(jnp.float32)
        rest = gates[...]
        for term in range(1, 4):
            part = rest.astype(jnp.bfloat16).astype(jnp.float32)
            notes[pl.ds(first + term * top, top), 0:size] = part
            rest = rest - part
    out_ref[:, pl.ds(3 * width, LANES)] = notes[...].T[:size, :].astype(jnp.bfloat16)


def picks_kernel(count, top, slots, devices, place_ref, *refs):
    blocks, outs, (notes, turned) = refs[:devices], refs[devices:-2], refs[-2:]
    tokens = notes.shape[0]
    for code, block in enumerate(blocks):
        size = block.shape[0]
        rows = pl.ds(pl.multiple_of(place_ref[3 + code], size), size)
        notes[rows, :] = block[...].astype(jnp.float32)
    turned[...] = notes[...].T
    row = lax.broadcasted_iota(jnp.int32, (tokens, tokens), 0)
    column = lax.broadcasted_iota(jnp.int32, (tokens, tokens), 1)
    earlier = jnp.where(row < column, 1.0, 0.0).astype(jnp.bfloat16)
    slot = lax.broadcasted_iota(jnp.int32, (slots, tokens), 0).astype(jnp.float32)

    def fill(first, start, picks, gates, flipped):
        ids = (first + lax.broadcasted_iota(jnp.int32, (count, tokens), 0)).astype(jnp.float32)
        named = jnp.zeros((count, tokens), jnp.float32)
        gated = jnp.zeros((count, tokens), jnp.float32)
        for column in range(start, start + top):
            same = turned[column : column + 1, :] == ids
            terms = [turned[column + term * top : column + term * top + 1, :] for term in (1, 2, 3)]
            named = named + jnp.where(same, 1.0, 0.0)
            gated = gated + jnp.where(same, terms[0] + terms[1] + terms[2], 0.0)
        place = jnp.dot(named.astype(jnp.bfloat16), earlier, preferred_element_type=jnp.float32)
        place = jnp.where(named > 0.0, place, -1.0)
        for expert in range(count):
            rows = pl.ds(expert * slots, slots)
            hit = place[expert : expert + 1, :] == slot
            picks[rows, :] = jnp.where(hit, 1.0, 0.0).astype(jnp.bfloat16)
            own = jnp.sum(jnp.where(hit, gated[expert : expert + 1, :], 0.0), axis=1, keepdims=True)
            gates[rows, :] = jnp.broadcast_to(own, (slots, LANES))
        if flipped is not None:
            flipped[...] = picks[...].T

    fill(place_ref[1], 4 * top, outs[0], outs[1], outs[2])
    fill(place_ref[1], 0, outs[3], outs[4], outs[5])
    fill(place_ref[2], 0, outs[6], outs[7], None)


def spread_gate(gates, rows, width):
    gate = gates[rows, 0:1]
    return jnp.broadcast_to(gate, (gate.shape[0], width))


def assemble(place_ref, blocks, columns, tokens):
    for code, block in enumerate(blocks):
        size = block.shape[0]
        rows = pl.ds(pl.multiple_of(place_ref[3 + code], size), size)
        tokens[rows, :] = block[:, columns]


def combine(flipped, results, sums):
    width = sums.shape[1]
    for start in range(0, width, CHUNK):
        columns = pl.ds(start, CHUNK)
        sums[:, columns] = jnp.dot(
            flipped[...], results[:, columns], preferred_element_type=jnp.float32
        ).astype(sums.dtype)


def gather(count, slots, picks, gates, tokens_ref, rows, first, stride):
    width = tokens_ref.shape[1]
    for start in range(0, width, CHUNK):
        columns = pl.ds(start, CHUNK)
        taken = jnp.dot(picks[...], tokens_ref[:, columns], preferred_element_type=jnp.float32)
        if gates is not None:
            taken = taken * spread_gate(gates, pl.ds(0, count * slots), CHUNK)
        taken = taken.astype(rows.dtype)
        for expert in range(count):
            part = slice(expert * slots, (expert + 1) * slots)
            rows[pl.ds(first + expert * stride, slots), columns] = taken[part]


def expert_kernel(count, slots, devices, pair, place_ref, *refs):
    picks_in, weights_in, blocks = refs[:6], refs[6], refs[7 : 7 + devices]
    groups = devices // pair
    near_outs, far_out, inner_out = refs[7 + devices : 7 + devices + groups], *refs[7 + devices + groups :][:2]
    scratch = refs[9 + devices + groups :]
    held, tokens = scratch[:6], scratch[6:9]
    rows, fore_results, back_results, second, inner, weights_ref = scratch[9:15]
    weights_done, in_done, out_done, inner_done = scratch[15:]
    fore_picks, fore_gates, fore_flip, back_picks, back_gates, back_flip = held
    size, width = blocks[0].shape[0], tokens[0].shape[1]

    def home(code):
        return pl.ds(pl.multiple_of(place_ref[3 + code], size), size)

    arriving = [
        pltpu.make_async_copy(source, target, in_done.at[3 * devices + place])
        for place, (source, target) in enumerate(zip(picks_in, held))
    ]
    coming = [
        [
            pltpu.make_async_copy(
                block.at[:, pl.ds(place * width, width)],
                tokens[place].at[home(code), :],
                in_done.at[place * devices + code],
            )
            for code, block in enumerate(blocks)
        ]
        for place in range(3)
    ]
    for copy in arriving + coming[0] + coming[1] + coming[2]:
        copy.start()

    def weight_copies(step):
        cut = width // WEIGHT_CUTS
        return [
            pltpu.make_async_copy(
                weights_in.at[place_ref[0] * count + step, pl.ds(place * cut, cut), :],
                weights_ref.at[step, pl.ds(place * cut, cut), :],
                weights_done.at[step, place],
            )
            for place in range(WEIGHT_CUTS)
        ]

    for step in range(count):
        for copy in weight_copies(step):
            copy.start()
    for copy in arriving:
        copy.wait()
    taken = ((fore_picks, None), (back_picks, None), (back_picks, back_gates))
    for place, (picks, gates) in enumerate(taken):
        for copy in coming[place]:
            copy.wait()
        gather(count, slots, picks, gates, tokens[place], rows, place * slots, 3 * slots)

    def inner_copy(step):
        return pltpu.make_async_copy(inner.at[step], inner_out.at[step], inner_done.at[step])

    @pl.loop(0, count)
    def _(step):
        mine = pl.ds(pl.multiple_of(step * slots, slots), slots)
        three = pl.ds(pl.multiple_of(step * 3 * slots, 3 * slots), 3 * slots)
        for copy in weight_copies(step):
            copy.wait()
        product = jnp.dot(rows[three, :], weights_ref[step], preferred_element_type=jnp.float32)
        ahead, hidden, active_grads = (
            product[:slots],
            product[slots : 2 * slots],
            product[2 * slots :],
        )
        sigma = jax.nn.sigmoid(hidden)
        hidden_grads = (active_grads * sigma * (1.0 + hidden * (1.0 - sigma))).astype(jnp.bfloat16)
        inner[step, :slots, :] = hidden_grads
        inner[step, slots:, :] = (hidden * sigma).astype(jnp.bfloat16)
        inner_copy(step).start()
        second[:slots, :] = (ahead * jax.nn.sigmoid(ahead)).astype(jnp.bfloat16)
        second[slots:, :] = hidden_grads
        result = lax.dot_general(
            second[...],
            weights_ref[step],
            (((1,), (1,)), ((), ())),
            preferred_element_type=jnp.float32,
        )
        fore_results[mine, :] = (result[:slots] * spread_gate(fore_gates, mine, width)).astype(
            fore_results.dtype
        )
        back_results[mine, :] = result[slots:].astype(back_results.dtype)

    leaving = []
    for lead, (flipped, results) in enumerate(((fore_flip, fore_results), (back_flip, back_results))):
        sums = tokens[lead]
        combine(flipped, results, sums)
        targets = [(out.at[lead], pair * group) for group, out in enumerate(near_outs)]
        targets += [(far_out.at[group, lead], pair * group + 1) for group in range(groups)]
        for target, code in targets:
            done = out_done.at[lead * devices + code]
            leaving.append(pltpu.make_async_copy(sums.at[home(code), :], target, done))
            leaving[-1].start()
    for copy in leaving:
        copy.wait()
    for step in range(count):
        inner_copy(step).wait()


def weight_kernel(count, slots, devices, place_ref, *refs):
    picks, gates, inner_ref = refs[:3]
    saved, grads = refs[3 : 3 + devices], refs[3 + devices : 3 + 2 * devices]
    out_ref, tokens, rows = refs[-3:]
    step = pl.program_id(0)
    half = tokens.shape[1]

    @pl.when(step == 0)
    def _():
        for place, (blocks, scale) in enumerate(((saved, None), (grads, gates))):
            assemble(place_ref, blocks, pl.ds(0, half), tokens)
            gather(count, slots, picks, scale, tokens, rows, place * slots, 2 * slots)

    both = pl.ds(pl.multiple_of(step * 2 * slots, 2 * slots), 2 * slots)
    flat = rows[both, :].T
    for start in range(0, inner_ref.shape[-1], CHUNK):
        columns = pl.ds(start, CHUNK)
        out_ref[0, :, columns] = jnp.dot(
            flat, inner_ref[0, :, columns], preferred_element_type=jnp.float32
        ).astype(out_ref.dtype)


def gathered_plan(
    section_inputs,
    saved_inputs,
    output_grads,
    forward_routes,
    backward_routes,
    forward_gates,
    backward_gates,
    expert_weights,
):
    token_count = section_inputs.shape[1]
    top = forward_routes.shape[2]
    _, local_count, width, inner_width = expert_weights.shape
    groups, pair = lax.axis_size("expert"), lax.axis_size("dp")
    devices = groups * pair
    count = local_count // pair
    total = devices * token_count
    slots = -(-devices * CAP // 16) * 16
    rows = count * slots
    half = width // pair
    weights = expert_weights[0]

    side, group = lax.axis_index("dp"), lax.axis_index("expert")
    index = group * pair + side
    base = group * local_count
    place = jnp.stack(
        [side, base + side * count, base + (1 - side) * count]
        + [(index ^ code) * token_count for code in range(devices)]
    ).astype(jnp.int32)
    params = pltpu.CompilerParams(vmem_limit_bytes=VMEM_LIMIT, dimension_semantics=("arbitrary",))

    def whole(shape):
        return pl.BlockSpec(shape, lambda *_: (0,) * len(shape))

    def call(kernel, name, steps, in_specs, out_specs, out_shape, scratch, flops=0, aliases=()):
        return pl.pallas_call(
            kernel,
            grid_spec=pltpu.PrefetchScalarGridSpec(
                num_scalar_prefetch=1,
                grid=(steps,),
                in_specs=in_specs,
                out_specs=out_specs,
                scratch_shapes=scratch,
            ),
            out_shape=out_shape,
            compiler_params=params,
            cost_estimate=pl.CostEstimate(
                flops=flops, bytes_accessed=flops // 512 + 1024, transcendentals=0
            ),
            input_output_aliases=dict(aliases),
            name=name,
        )

    def onward(block):
        return swapped(block, 1)

    def across(parts):
        return [swapped(part, code) for part, code in zip(parts, range(pair, devices, pair))]

    def after(first, then):
        then, _ = lax.optimization_barrier((then, first))
        return then

    def summed(*blocks):
        return functools.reduce(jnp.add, [block.astype(jnp.float32) for block in blocks])

    packed = jax.ShapeDtypeStruct((token_count, 3 * width + LANES), jnp.bfloat16)
    own = pl.pallas_call(
        pack_kernel,
        in_specs=[pl.BlockSpec(memory_space=pl.ANY)] * 7,
        out_specs=pl.BlockSpec(memory_space=pltpu.VMEM),
        out_shape=packed,
        scratch_shapes=[
            pltpu.VMEM((top, token_count), jnp.int32),
            pltpu.VMEM((top, token_count), jnp.float32),
            pltpu.VMEM((top, token_count), jnp.int32),
            pltpu.VMEM((top, token_count), jnp.float32),
            pltpu.VMEM((LANES, LANES), jnp.float32),
            pltpu.SemaphoreType.DMA((7,)),
        ],
        compiler_params=pltpu.CompilerParams(vmem_limit_bytes=WIDE_LIMIT),
        name="pack",
    )(
        section_inputs[0],
        saved_inputs[0],
        output_grads[0],
        backward_routes[0].T,
        backward_gates[0].T,
        forward_routes[0].T,
        forward_gates[0].T,
    )
    near = [own] + across([own] * (groups - 1))
    blocks = [block for one in near for block in (one, onward(one))]

    pick = jax.ShapeDtypeStruct((rows, total), jnp.bfloat16)
    flip = jax.ShapeDtypeStruct((total, rows), jnp.bfloat16)
    gate = jax.ShapeDtypeStruct((rows, LANES), jnp.float32)
    pick_outs = [pick, gate, flip, pick, gate, flip, pick, gate]
    picks = call(
        functools.partial(picks_kernel, count, top, slots, devices),
        "slot_picks",
        1,
        [pl.BlockSpec((token_count, LANES), lambda *_: (0, 3 * width // LANES))] * devices,
        [whole(out.shape) for out in pick_outs],
        pick_outs,
        [pltpu.VMEM((total, LANES), jnp.float32), pltpu.VMEM((LANES, total), jnp.float32)],
    )(place, *blocks)

    pass_flops = 2 * 2 * count * CHUNK * width * inner_width
    near_part = jax.ShapeDtypeStruct((2, token_count, width), jnp.bfloat16)
    far_part = jax.ShapeDtypeStruct((groups, 2, token_count, width), jnp.bfloat16)
    inner = jax.ShapeDtypeStruct((count, 2 * slots, inner_width), jnp.bfloat16)
    inner_spec = pl.BlockSpec((1, 2 * slots, inner_width), lambda step, place: (step, 0, 0))
    in_smem, anywhere = (pl.BlockSpec(memory_space=space) for space in (pltpu.SMEM, pl.ANY))
    tokens = pltpu.VMEM((total, width), jnp.bfloat16)
    *near_parts, far_sums, inner_own = pl.pallas_call(
        functools.partial(expert_kernel, count, slots, devices, pair),
        in_specs=[in_smem] + [anywhere] * (7 + devices),
        out_specs=[anywhere] * (groups + 2),
        out_shape=[near_part] * groups + [far_part, inner],
        scratch_shapes=[pltpu.VMEM(array.shape, array.dtype) for array in pick_outs[:6]]
        + [tokens] * 3
        + [
            pltpu.VMEM((3 * rows, width), jnp.bfloat16),
            pltpu.VMEM((rows, width), jnp.bfloat16),
            pltpu.VMEM((rows, width), jnp.bfloat16),
            pltpu.VMEM((2 * slots, inner_width), jnp.bfloat16),
            pltpu.VMEM(inner.shape, inner.dtype),
            pltpu.VMEM((count, width, inner_width), jnp.bfloat16),
            pltpu.SemaphoreType.DMA((count, WEIGHT_CUTS)),
            pltpu.SemaphoreType.DMA((3 * devices + 6,)),
            pltpu.SemaphoreType.DMA((2 * devices,)),
            pltpu.SemaphoreType.DMA((count,)),
        ],
        compiler_params=pltpu.CompilerParams(vmem_limit_bytes=EXPERTS_LIMIT),
        cost_estimate=pl.CostEstimate(
            flops=pass_flops, bytes_accessed=pass_flops // 512, transcendentals=0
        ),
        name="experts",
    )(
        place,
        *picks[:6],
        weights,
        *blocks,
    )
    far_sums = onward(far_sums)
    inner_other = onward(inner_own)

    def gradient(whose, inner_rows, picked, earlier):
        earlier = [] if earlier is None else [earlier]

        def out_block(step, place):
            owner = place[0] if whose == 0 else 1 - place[0]
            return (owner * count + step, 0, 0)

        specs = [whole(pick.shape), whole(gate.shape), inner_spec]
        for first in (pair, 2 * pair):
            specs += [
                pl.BlockSpec((token_count, half), lambda step, place, first=first: (0, first + place[0]))
            ] * devices
        specs += [pl.BlockSpec(memory_space=pl.ANY)] * len(earlier)
        return call(
            functools.partial(weight_kernel, count, slots, devices),
            "weight_gradient_" + ("own", "other")[whose],
            count,
            specs,
            pl.BlockSpec((1, half, inner_width), out_block),
            jax.ShapeDtypeStruct((local_count, half, inner_width), jnp.bfloat16),
            [pltpu.VMEM((total, half), jnp.bfloat16), pltpu.VMEM((2 * rows, half), jnp.bfloat16)],
            pass_flops // 2,
            [(len(specs), 0)] if earlier else [],
        )(place, *picked, inner_rows, *blocks, *blocks, *earlier)

    own_done = gradient(0, inner_own, picks[3:5], None)
    far_sums = after(own_done, far_sums)
    sums = [
        summed(part, far_sums[group]).astype(jnp.bfloat16) for group, part in enumerate(near_parts)
    ]
    near_sums = across(sums[1:])
    weight_grads = gradient(1, inner_other, picks[6:8], own_done)
    near_sums = after(weight_grads, near_sums)
    moved = summed(sums[0], *near_sums)
    layer_out = (section_inputs[0].astype(jnp.float32) + moved[0]).astype(jnp.bfloat16)
    input_grads = (output_grads[0].astype(jnp.float32) + moved[1]).astype(jnp.bfloat16)
    next_inputs = shifted(layer_out, "pipe", 1)[None]
    prior_grads = shifted(input_grads, "pipe", -1)[None]
    return (next_inputs, prior_grads, weight_grads[None])


def on_device(*arrays):
    token_count = arrays[0].shape[1]
    local_count = arrays[-1].shape[1]
    groups, pair = lax.axis_size("expert"), lax.axis_size("dp")
    gathered = groups * token_count
    packed = groups * local_count * CAP
    paired = pair == 2 and local_count % pair == 0 and groups & (groups - 1) == 0
    if gathered <= packed and paired and gathered * pair % LANES == 0:
        return gathered_plan(*arrays)
    return packed_plan(*arrays)


def solution(mesh):
    placed = (
        P("pipe", ("expert", "dp"), None),
        P("pipe", ("expert", "dp"), None),
        P("pipe", ("expert", "dp"), None),
        P("pipe", ("expert", "dp"), None),
        P("pipe", ("expert", "dp"), None),
        P("pipe", ("expert", "dp"), None),
        P("pipe", ("expert", "dp"), None),
        P("pipe", "expert", None, None),
    )
    return jax.shard_map(
        on_device,
        mesh=mesh,
        in_specs=placed,
        out_specs=(
            P("pipe", ("expert", "dp"), None),
            P("pipe", ("expert", "dp"), None),
            P("pipe", "expert", "dp", None),
        ),
        check_vma=False,
    )
```

```python
import functools

import jax
import jax.numpy as jnp
from jax import lax
from jax.experimental import pallas as pl
from jax.experimental.pallas import tpu as pltpu
from jax.sharding import PartitionSpec as P

CAP = 5
LANES = 128
CHUNK = 256
VMEM_LIMIT = 24 * 1024 * 1024
EXPERTS_LIMIT = 36 * 1024 * 1024
WEIGHT_CUTS = 4
WEIGHT_SLOTS = 3


def shifted(value, axis, steps):
    count = lax.axis_size(axis)
    pairs = [(source, (source + steps) % count) for source in range(count)]
    return lax.ppermute(value, axis, pairs)


def slot_index(routing, experts, capacity):
    one_hot = (routing[..., None] == jnp.arange(experts, dtype=jnp.int32)).astype(jnp.int32)
    before = jnp.cumsum(one_hot, axis=-2) - one_hot
    return routing * capacity + jnp.sum(before * one_hot, axis=-1)


def pack_rows(source, slot_ids, slot_total, spread):
    row_count = slot_ids.shape[0]
    owner_row = (
        jnp.zeros((slot_total,), jnp.int32)
        .at[slot_ids]
        .set(jnp.arange(row_count, dtype=jnp.int32) + 1)
    )
    filled = owner_row > 0
    picked = jnp.take(source, jnp.maximum(owner_row - 1, 0) // spread, axis=0)
    return jnp.where(filled[:, None], picked, jnp.zeros_like(picked))


def expert_forward(slot_rows, weights):
    hidden = jnp.einsum("nlcd,ldh->nlch", slot_rows, weights, preferred_element_type=jnp.float32)
    active = jax.nn.silu(hidden).astype(jnp.bfloat16)
    return jnp.einsum("nlch,ldh->nlcd", active, weights, preferred_element_type=jnp.float32).astype(
        jnp.bfloat16
    )


def expert_backward(saved_rows, slot_grads, weights):
    hidden = jnp.einsum("nlcd,ldh->nlch", saved_rows, weights, preferred_element_type=jnp.float32)
    active = jax.nn.silu(hidden).astype(jnp.bfloat16)
    active_grads = jnp.einsum(
        "nlcd,ldh->nlch", slot_grads, weights, preferred_element_type=jnp.float32
    )
    sigma = jax.nn.sigmoid(hidden)
    hidden_grads = (active_grads * sigma * (1.0 + hidden * (1.0 - sigma))).astype(jnp.bfloat16)
    row_grads = jnp.einsum(
        "nlch,ldh->nlcd", hidden_grads, weights, preferred_element_type=jnp.float32
    ).astype(jnp.bfloat16)
    weight_part = jnp.einsum(
        "nlcd,nlch->ldh", saved_rows, hidden_grads, preferred_element_type=jnp.float32
    )
    weight_part = weight_part + jnp.einsum(
        "nlcd,nlch->ldh", slot_grads, active, preferred_element_type=jnp.float32
    )
    return (row_grads, weight_part)


def packed_plan(
    section_inputs,
    saved_inputs,
    output_grads,
    forward_routes,
    backward_routes,
    forward_gates,
    backward_gates,
    expert_weights,
):
    token_count = section_inputs.shape[1]
    route_count = forward_routes.shape[2]
    local_count = expert_weights.shape[1]
    model_width = expert_weights.shape[2]
    groups = lax.axis_size("expert")
    experts = groups * local_count
    slot_total = experts * CAP
    block_shape = (groups, local_count, CAP, model_width)
    weights = expert_weights[0]
    forward_slot = slot_index(forward_routes[0].reshape(-1), experts, CAP)
    backward_slot = slot_index(backward_routes[0].reshape(-1), experts, CAP)
    forward_rows = pack_rows(section_inputs[0], forward_slot, slot_total, route_count).reshape(
        block_shape
    )
    saved_rows = pack_rows(saved_inputs[0], backward_slot, slot_total, route_count).reshape(
        block_shape
    )
    grad_block = output_grads[0]
    scaled = backward_gates[0][:, :, None] * grad_block.astype(jnp.float32)[:, None, :]
    scaled = scaled.astype(jnp.bfloat16).reshape(token_count * route_count, model_width)
    slot_grads = pack_rows(scaled, backward_slot, slot_total, 1).reshape(block_shape)
    forward_back = lax.all_to_all(
        expert_forward(
            lax.all_to_all(forward_rows, "expert", split_axis=0, concat_axis=0, tiled=True), weights
        ),
        "expert",
        split_axis=0,
        concat_axis=0,
        tiled=True,
    )
    saved_recv, grads_recv = (
        lax.all_to_all(saved_rows, "expert", split_axis=0, concat_axis=0, tiled=True),
        lax.all_to_all(slot_grads, "expert", split_axis=0, concat_axis=0, tiled=True),
    )
    row_grads, weight_part = expert_backward(saved_recv, grads_recv, weights)
    grads_back = lax.all_to_all(row_grads, "expert", split_axis=0, concat_axis=0, tiled=True)
    forward_pick = jnp.take(forward_back.reshape(slot_total, model_width), forward_slot, axis=0)
    forward_pick = forward_pick.reshape(token_count, route_count, model_width).astype(jnp.float32)
    layer_out = section_inputs[0].astype(jnp.float32) + jnp.sum(
        forward_gates[0][:, :, None] * forward_pick, axis=1
    )
    layer_out = layer_out.astype(jnp.bfloat16)
    grads_pick = jnp.take(grads_back.reshape(slot_total, model_width), backward_slot, axis=0)
    grads_pick = grads_pick.reshape(token_count, route_count, model_width).astype(jnp.float32)
    input_grads = (grad_block.astype(jnp.float32) + jnp.sum(grads_pick, axis=1)).astype(
        jnp.bfloat16
    )
    next_inputs = shifted(layer_out, "pipe", 1)[None]
    prior_grads = shifted(input_grads, "pipe", -1)[None]
    weight_grads = lax.psum_scatter(
        weight_part.astype(jnp.bfloat16), "dp", scatter_dimension=1, tiled=True
    )[None]
    return (next_inputs, prior_grads, weight_grads)


def swapped(value, code):
    axes = ("expert", "dp")
    count = lax.axis_size(axes[0]) * lax.axis_size(axes[1])
    return lax.ppermute(value, axes, [(source, source ^ code) for source in range(count)])


def pack_kernel(*refs):
    sources, out_ref, (*held, notes, done) = refs[:7], refs[7], refs[8:]
    size, width = sources[0].shape
    top = sources[3].shape[0]
    targets = [out_ref.at[:, pl.ds(place * width, width)] for place in range(3)] + held
    copies = [
        pltpu.make_async_copy(source, target, done.at[place])
        for place, (source, target) in enumerate(zip(sources, targets))
    ]
    for copy in copies:
        copy.start()
    for copy in copies:
        copy.wait()
    back_routes, back_gates, fore_routes, fore_gates = held
    notes[...] = jnp.zeros_like(notes)
    for place, (routes, gates) in enumerate(((back_routes, back_gates), (fore_routes, fore_gates))):
        first = place * 4 * top
        notes[pl.ds(first, top), 0:size] = routes[...].astype(jnp.float32)
        rest = gates[...]
        for term in range(1, 4):
            part = rest.astype(jnp.bfloat16).astype(jnp.float32)
            notes[pl.ds(first + term * top, top), 0:size] = part
            rest = rest - part
    out_ref[:, pl.ds(3 * width, LANES)] = notes[...].T[:size, :].astype(jnp.bfloat16)


def picks_kernel(count, top, slots, devices, place_ref, *refs):
    blocks, outs, (notes, turned) = refs[:devices], refs[devices:-2], refs[-2:]
    tokens = notes.shape[0]
    for code, block in enumerate(blocks):
        size = block.shape[0]
        rows = pl.ds(pl.multiple_of(place_ref[3 + code], size), size)
        notes[rows, :] = block[...].astype(jnp.float32)
    turned[...] = notes[...].T
    row = lax.broadcasted_iota(jnp.int32, (tokens, tokens), 0)
    column = lax.broadcasted_iota(jnp.int32, (tokens, tokens), 1)
    earlier = jnp.where(row < column, 1.0, 0.0).astype(jnp.bfloat16)
    slot = lax.broadcasted_iota(jnp.int32, (slots, tokens), 0).astype(jnp.float32)

    def fill(first, start, picks, gates, flipped):
        ids = (first + lax.broadcasted_iota(jnp.int32, (count, tokens), 0)).astype(jnp.float32)
        named = jnp.zeros((count, tokens), jnp.float32)
        gated = jnp.zeros((count, tokens), jnp.float32)
        for column in range(start, start + top):
            same = turned[column : column + 1, :] == ids
            terms = [turned[column + term * top : column + term * top + 1, :] for term in (1, 2, 3)]
            named = named + jnp.where(same, 1.0, 0.0)
            gated = gated + jnp.where(same, terms[0] + terms[1] + terms[2], 0.0)
        place = jnp.dot(named.astype(jnp.bfloat16), earlier, preferred_element_type=jnp.float32)
        place = jnp.where(named > 0.0, place, -1.0)
        for expert in range(count):
            rows = pl.ds(expert * slots, slots)
            hit = place[expert : expert + 1, :] == slot
            picks[rows, :] = jnp.where(hit, 1.0, 0.0).astype(jnp.bfloat16)
            own = jnp.sum(jnp.where(hit, gated[expert : expert + 1, :], 0.0), axis=1, keepdims=True)
            gates[rows, :] = jnp.broadcast_to(own, (slots, LANES))
        if flipped is not None:
            flipped[...] = picks[...].T

    fill(place_ref[1], 4 * top, outs[0], outs[1], outs[2])
    fill(place_ref[1], 0, outs[3], outs[4], outs[5])
    fill(place_ref[2], 0, outs[6], outs[7], None)


def spread_gate(gates, rows, width):
    gate = gates[rows, 0:1]
    return jnp.broadcast_to(gate, (gate.shape[0], width))


def assemble(place_ref, blocks, columns, tokens):
    for code, block in enumerate(blocks):
        size = block.shape[0]
        rows = pl.ds(pl.multiple_of(place_ref[3 + code], size), size)
        tokens[rows, :] = block[:, columns]


def combine(flipped, results, sums):
    width = sums.shape[1]
    for start in range(0, width, CHUNK):
        columns = pl.ds(start, CHUNK)
        sums[:, columns] = jnp.dot(
            flipped[...], results[:, columns], preferred_element_type=jnp.float32
        ).astype(sums.dtype)


def gather(count, slots, picks, gates, tokens_ref, rows, first, stride):
    width = tokens_ref.shape[1]
    for start in range(0, width, CHUNK):
        columns = pl.ds(start, CHUNK)
        taken = jnp.dot(picks[...], tokens_ref[:, columns], preferred_element_type=jnp.float32)
        if gates is not None:
            taken = taken * spread_gate(gates, pl.ds(0, count * slots), CHUNK)
        taken = taken.astype(rows.dtype)
        for expert in range(count):
            part = slice(expert * slots, (expert + 1) * slots)
            rows[pl.ds(first + expert * stride, slots), columns] = taken[part]


def expert_kernel(count, slots, devices, pair, place_ref, *refs):
    picks_in, weights_in, blocks = refs[:6], refs[6], refs[7 : 7 + devices]
    groups = devices // pair
    outs, inner_out = refs[7 + devices : 9 + devices + 2 * groups], refs[9 + devices + 2 * groups]
    scratch = refs[10 + devices + 2 * groups :]
    held, tokens = scratch[:6], scratch[6:9]
    rows, fore_results, back_results, second, inner, weights_ref = scratch[9:15]
    weights_done, in_done, out_done, inner_done = scratch[15:]
    fore_picks, fore_gates, fore_flip, back_picks, back_gates, back_flip = held
    size, width = blocks[0].shape[0], tokens[0].shape[1]

    def home(code):
        return pl.ds(pl.multiple_of(place_ref[3 + code], size), size)

    arriving = [
        pltpu.make_async_copy(source, target, in_done.at[3 * devices + place])
        for place, (source, target) in enumerate(zip(picks_in, held))
    ]
    coming = [
        [
            pltpu.make_async_copy(
                block.at[:, pl.ds(place * width, width)],
                tokens[place].at[home(code), :],
                in_done.at[place * devices + code],
            )
            for code, block in enumerate(blocks)
        ]
        for place in range(3)
    ]
    for copy in arriving + coming[0] + coming[1] + coming[2]:
        copy.start()

    def weight_copies(step):
        cut = width // WEIGHT_CUTS
        return [
            pltpu.make_async_copy(
                weights_in.at[place_ref[0] * count + step, pl.ds(place * cut, cut), :],
                weights_ref.at[lax.rem(step, WEIGHT_SLOTS), pl.ds(place * cut, cut), :],
                weights_done.at[lax.rem(step, WEIGHT_SLOTS), place],
            )
            for place in range(WEIGHT_CUTS)
        ]

    for step in range(min(count, WEIGHT_SLOTS - 1)):
        for copy in weight_copies(step):
            copy.start()
    for copy in arriving:
        copy.wait()
    taken = ((fore_picks, None), (back_picks, None), (back_picks, back_gates))
    for place, (picks, gates) in enumerate(taken):
        for copy in coming[place]:
            copy.wait()
        gather(count, slots, picks, gates, tokens[place], rows, place * slots, 3 * slots)

    def inner_copy(step):
        return pltpu.make_async_copy(inner.at[step], inner_out.at[step], inner_done.at[step])

    @pl.loop(0, count)
    def _(step):
        mine = pl.ds(pl.multiple_of(step * slots, slots), slots)
        three = pl.ds(pl.multiple_of(step * 3 * slots, 3 * slots), 3 * slots)
        slot = lax.rem(step, WEIGHT_SLOTS)

        @pl.when(step + WEIGHT_SLOTS - 1 < count)
        def _():
            for copy in weight_copies(step + WEIGHT_SLOTS - 1):
                copy.start()

        for copy in weight_copies(step):
            copy.wait()
        product = jnp.dot(rows[three, :], weights_ref[slot], preferred_element_type=jnp.float32)
        ahead, hidden, active_grads = (
            product[:slots],
            product[slots : 2 * slots],
            product[2 * slots :],
        )
        sigma = jax.nn.sigmoid(hidden)
        hidden_grads = (active_grads * sigma * (1.0 + hidden * (1.0 - sigma))).astype(jnp.bfloat16)
        inner[step, :slots, :] = hidden_grads
        inner[step, slots:, :] = (hidden * sigma).astype(jnp.bfloat16)
        inner_copy(step).start()
        second[:slots, :] = (ahead * jax.nn.sigmoid(ahead)).astype(jnp.bfloat16)
        second[slots:, :] = hidden_grads
        result = lax.dot_general(
            second[...],
            weights_ref[slot],
            (((1,), (1,)), ((), ())),
            preferred_element_type=jnp.float32,
        )
        fore_results[mine, :] = (result[:slots] * spread_gate(fore_gates, mine, width)).astype(
            fore_results.dtype
        )
        back_results[mine, :] = result[slots:].astype(back_results.dtype)

    leaving = []
    for lead, (flipped, results) in enumerate(((fore_flip, fore_results), (back_flip, back_results))):
        sums = tokens[lead]
        combine(flipped, results, sums)
        *near_outs, far_out = outs[lead * (groups + 1) : (lead + 1) * (groups + 1)]
        targets = [(far_out.at[group], pair * group + 1) for group in range(groups)]
        targets += [(out, pair * group) for group, out in enumerate(near_outs)]
        for target, code in targets:
            done = out_done.at[lead * devices + code]
            leaving.append(pltpu.make_async_copy(sums.at[home(code), :], target, done))
            leaving[-1].start()
    for copy in leaving:
        copy.wait()
    for step in range(count):
        inner_copy(step).wait()


def weight_kernel(whose, first, number, count, slots, devices, place_ref, *refs):
    held_in, blocks = refs[:3], refs[3 : 3 + devices]
    out_ref, picks, gates, inner, saved, grads, rows, staged, in_done, out_done = refs[-10:]
    size, half = blocks[0].shape[0], saved.shape[1]
    side = place_ref[0]
    owner = side if whose == 0 else 1 - side
    part = pl.ds(first * slots, number * slots)

    arriving = [
        pltpu.make_async_copy(source, target, in_done.at[2 * devices + place])
        for place, (source, target) in enumerate(
            (
                (held_in[0].at[part, :], picks),
                (held_in[1].at[part, :], gates),
                (held_in[2].at[pl.ds(first, number)], inner),
            )
        )
    ]
    coming = [
        [
            pltpu.make_async_copy(
                block.at[:, pl.ds(pl.multiple_of((2 * place + 2 + side) * half, half), half)],
                target.at[pl.ds(pl.multiple_of(place_ref[3 + code], size), size), :],
                in_done.at[place * devices + code],
            )
            for code, block in enumerate(blocks)
        ]
        for place, target in enumerate((saved, grads))
    ]
    for copy in arriving + coming[0] + coming[1]:
        copy.start()
    for copy in arriving:
        copy.wait()
    for place, (tokens, scale) in enumerate(((saved, None), (grads, gates))):
        for copy in coming[place]:
            copy.wait()
        gather(number, slots, picks, scale, tokens, rows, place * slots, 2 * slots)

    leaving = []
    for step in range(number):
        flat = rows[pl.ds(step * 2 * slots, 2 * slots), :].T
        for start in range(0, half, CHUNK):
            chunk = pl.ds(start, CHUNK)
            staged[step, chunk, :] = jnp.dot(
                flat[start : start + CHUNK], inner[step], preferred_element_type=jnp.float32
            ).astype(staged.dtype)
            leaving.append(
                pltpu.make_async_copy(
                    staged.at[step, chunk, :],
                    out_ref.at[owner * count + first + step, chunk, :],
                    out_done.at[step, start // CHUNK],
                )
            )
            leaving[-1].start()
    for copy in leaving:
        copy.wait()


def gathered_plan(
    section_inputs,
    saved_inputs,
    output_grads,
    forward_routes,
    backward_routes,
    forward_gates,
    backward_gates,
    expert_weights,
):
    token_count = section_inputs.shape[1]
    top = forward_routes.shape[2]
    _, local_count, width, inner_width = expert_weights.shape
    groups, pair = lax.axis_size("expert"), lax.axis_size("dp")
    devices = groups * pair
    count = local_count // pair
    total = devices * token_count
    slots = -(-devices * CAP // 16) * 16
    rows = count * slots
    half = width // pair
    weights = expert_weights[0]

    side, group = lax.axis_index("dp"), lax.axis_index("expert")
    index = group * pair + side
    base = group * local_count
    place = jnp.stack(
        [side, base + side * count, base + (1 - side) * count]
        + [(index ^ code) * token_count for code in range(devices)]
    ).astype(jnp.int32)
    params = pltpu.CompilerParams(vmem_limit_bytes=VMEM_LIMIT, dimension_semantics=("arbitrary",))

    def whole(shape):
        return pl.BlockSpec(shape, lambda *_: (0,) * len(shape))

    def call(kernel, name, steps, in_specs, out_specs, out_shape, scratch, flops=0, aliases=()):
        return pl.pallas_call(
            kernel,
            grid_spec=pltpu.PrefetchScalarGridSpec(
                num_scalar_prefetch=1,
                grid=(steps,),
                in_specs=in_specs,
                out_specs=out_specs,
                scratch_shapes=scratch,
            ),
            out_shape=out_shape,
            compiler_params=params,
            cost_estimate=pl.CostEstimate(
                flops=flops, bytes_accessed=flops // 512 + 1024, transcendentals=0
            ),
            input_output_aliases=dict(aliases),
            name=name,
        )

    def onward(block):
        return swapped(block, 1)

    def across(parts):
        return [swapped(part, code) for part, code in zip(parts, range(pair, devices, pair))]

    def after(first, then):
        then, _ = lax.optimization_barrier((then, first))
        return then

    def summed(*blocks):
        return functools.reduce(jnp.add, [block.astype(jnp.float32) for block in blocks])

    packed = jax.ShapeDtypeStruct((token_count, 3 * width + LANES), jnp.bfloat16)
    own = pl.pallas_call(
        pack_kernel,
        in_specs=[pl.BlockSpec(memory_space=pl.ANY)] * 7,
        out_specs=pl.BlockSpec(memory_space=pltpu.VMEM),
        out_shape=packed,
        scratch_shapes=[
            pltpu.VMEM((top, token_count), jnp.int32),
            pltpu.VMEM((top, token_count), jnp.float32),
            pltpu.VMEM((top, token_count), jnp.int32),
            pltpu.VMEM((top, token_count), jnp.float32),
            pltpu.VMEM((LANES, LANES), jnp.float32),
            pltpu.SemaphoreType.DMA((7,)),
        ],
        compiler_params=pltpu.CompilerParams(vmem_limit_bytes=VMEM_LIMIT),
        name="pack",
    )(
        *[
            pltpu.with_memory_space_constraint(array, pltpu.HBM)
            for array in (
                section_inputs[0],
                saved_inputs[0],
                output_grads[0],
                backward_routes[0].T,
                backward_gates[0].T,
                forward_routes[0].T,
                forward_gates[0].T,
            )
        ]
    )
    near = [own] + across([own] * (groups - 1))
    blocks = [block for one in near for block in (one, onward(one))]

    pick = jax.ShapeDtypeStruct((rows, total), jnp.bfloat16)
    flip = jax.ShapeDtypeStruct((total, rows), jnp.bfloat16)
    gate = jax.ShapeDtypeStruct((rows, LANES), jnp.float32)
    pick_outs = [pick, gate, flip, pick, gate, flip, pick, gate]
    picks = call(
        functools.partial(picks_kernel, count, top, slots, devices),
        "slot_picks",
        1,
        [pl.BlockSpec((token_count, LANES), lambda *_: (0, 3 * width // LANES))] * devices,
        [whole(out.shape) for out in pick_outs],
        pick_outs,
        [pltpu.VMEM((total, LANES), jnp.float32), pltpu.VMEM((LANES, total), jnp.float32)],
    )(place, *blocks)

    pass_flops = 2 * 2 * count * CHUNK * width * inner_width
    near_part = jax.ShapeDtypeStruct((token_count, width), jnp.bfloat16)
    far_part = jax.ShapeDtypeStruct((groups, token_count, width), jnp.bfloat16)
    inner = jax.ShapeDtypeStruct((count, 2 * slots, inner_width), jnp.bfloat16)
    in_smem, anywhere = (pl.BlockSpec(memory_space=space) for space in (pltpu.SMEM, pl.ANY))
    tokens = pltpu.VMEM((total, width), jnp.bfloat16)
    *parts, inner_own = pl.pallas_call(
        functools.partial(expert_kernel, count, slots, devices, pair),
        in_specs=[in_smem] + [anywhere] * (7 + devices),
        out_specs=[anywhere] * (2 * groups + 3),
        out_shape=([near_part] * groups + [far_part]) * 2 + [inner],
        scratch_shapes=[pltpu.VMEM(array.shape, array.dtype) for array in pick_outs[:6]]
        + [tokens] * 3
        + [
            pltpu.VMEM((3 * rows, width), jnp.bfloat16),
            pltpu.VMEM((rows, width), jnp.bfloat16),
            pltpu.VMEM((rows, width), jnp.bfloat16),
            pltpu.VMEM((2 * slots, inner_width), jnp.bfloat16),
            pltpu.VMEM(inner.shape, inner.dtype),
            pltpu.VMEM((WEIGHT_SLOTS, width, inner_width), jnp.bfloat16),
            pltpu.SemaphoreType.DMA((WEIGHT_SLOTS, WEIGHT_CUTS)),
            pltpu.SemaphoreType.DMA((3 * devices + 6,)),
            pltpu.SemaphoreType.DMA((2 * devices,)),
            pltpu.SemaphoreType.DMA((count,)),
        ],
        compiler_params=pltpu.CompilerParams(vmem_limit_bytes=EXPERTS_LIMIT),
        cost_estimate=pl.CostEstimate(
            flops=pass_flops, bytes_accessed=pass_flops // 512, transcendentals=0
        ),
        name="experts",
    )(
        place,
        *picks[:6],
        weights,
        *blocks,
    )
    *layer_parts, layer_far = parts[: groups + 1]
    *grad_parts, grad_far = parts[groups + 1 :]
    layer_far, grad_far, inner_other = onward(layer_far), onward(grad_far), onward(inner_own)

    def gradient(whose, first, number, inner_rows, earlier):
        earlier = [] if earlier is None else [earlier]
        held = list(picks[3:5] if whose == 0 else picks[6:8]) + [inner_rows]
        operands = held + blocks + earlier
        half_tokens = pltpu.VMEM((total, half), jnp.bfloat16)
        return pl.pallas_call(
            functools.partial(weight_kernel, whose, first, number, count, slots, devices),
            in_specs=[in_smem] + [anywhere] * len(operands),
            out_specs=anywhere,
            out_shape=jax.ShapeDtypeStruct((local_count, half, inner_width), jnp.bfloat16),
            scratch_shapes=[
                pltpu.VMEM((number * slots, total), jnp.bfloat16),
                pltpu.VMEM((number * slots, LANES), jnp.float32),
                pltpu.VMEM((number, 2 * slots, inner_width), jnp.bfloat16),
                half_tokens,
                half_tokens,
                pltpu.VMEM((number * 2 * slots, half), jnp.bfloat16),
                pltpu.VMEM((number, half, inner_width), jnp.bfloat16),
                pltpu.SemaphoreType.DMA((2 * devices + 3,)),
                pltpu.SemaphoreType.DMA((number, half // CHUNK)),
            ],
            compiler_params=pltpu.CompilerParams(vmem_limit_bytes=VMEM_LIMIT),
            cost_estimate=pl.CostEstimate(
                flops=number * pass_flops // count // 2,
                bytes_accessed=number * half * inner_width * 4,
                transcendentals=0,
            ),
            input_output_aliases={len(operands): 0} if earlier else {},
            name=f"weight_gradient_{whose}_{first}",
        )(place, *operands)

    def pair_sums(near_parts, far):
        return [summed(part, far[group]).astype(jnp.bfloat16) for group, part in enumerate(near_parts)]

    piece = -(-count // 2)
    done = gradient(0, 0, piece, inner_own, None)
    layer_sums = pair_sums(layer_parts, after(done, layer_far))
    layer_near = across(layer_sums[1:])
    grad_sums = pair_sums(grad_parts, after((layer_sums, inner_other), grad_far))
    grad_near = across(grad_sums[1:])
    done = after(grad_sums, done)
    if piece < count:
        done = gradient(0, piece, count - piece, inner_own, done)
    done = gradient(1, 0, piece, inner_other, after(layer_near[0], done))
    layer_near = after(done, layer_near)
    layer_out = summed(section_inputs[0], layer_sums[0], *layer_near).astype(jnp.bfloat16)
    next_inputs = shifted(layer_out, "pipe", 1)[None]
    done = after(layer_out, done)
    if piece < count:
        done = gradient(1, piece, count - piece, inner_other, done)
    grad_near = after((done, next_inputs), grad_near)
    input_grads = summed(output_grads[0], grad_sums[0], *grad_near).astype(jnp.bfloat16)
    prior_grads = shifted(input_grads, "pipe", -1)[None]
    return (next_inputs, prior_grads, done[None])


def on_device(*arrays):
    token_count = arrays[0].shape[1]
    local_count = arrays[-1].shape[1]
    groups, pair = lax.axis_size("expert"), lax.axis_size("dp")
    gathered = groups * token_count
    packed = groups * local_count * CAP
    paired = pair == 2 and local_count % pair == 0 and groups & (groups - 1) == 0
    if gathered <= packed and paired and gathered * pair % LANES == 0:
        return gathered_plan(*arrays)
    return packed_plan(*arrays)


def solution(mesh):
    placed = (
        P("pipe", ("expert", "dp"), None),
        P("pipe", ("expert", "dp"), None),
        P("pipe", ("expert", "dp"), None),
        P("pipe", ("expert", "dp"), None),
        P("pipe", ("expert", "dp"), None),
        P("pipe", ("expert", "dp"), None),
        P("pipe", ("expert", "dp"), None),
        P("pipe", "expert", None, None),
    )
    return jax.shard_map(
        on_device,
        mesh=mesh,
        in_specs=placed,
        out_specs=(
            P("pipe", ("expert", "dp"), None),
            P("pipe", ("expert", "dp"), None),
            P("pipe", "expert", "dp", None),
        ),
        check_vma=False,
    )
```

```python
import functools

import jax
import jax.numpy as jnp
from jax import lax
from jax.experimental import pallas as pl
from jax.experimental.pallas import tpu as pltpu
from jax.sharding import PartitionSpec as P

CAP = 5
LANES = 128
CHUNK = 256
VMEM_LIMIT = 24 * 1024 * 1024
EXPERTS_LIMIT = 40 * 1024 * 1024
WEIGHT_CUTS = 4


def shifted(value, axis, steps):
    count = lax.axis_size(axis)
    pairs = [(source, (source + steps) % count) for source in range(count)]
    return lax.ppermute(value, axis, pairs)


def slot_index(routing, experts, capacity):
    one_hot = (routing[..., None] == jnp.arange(experts, dtype=jnp.int32)).astype(jnp.int32)
    before = jnp.cumsum(one_hot, axis=-2) - one_hot
    return routing * capacity + jnp.sum(before * one_hot, axis=-1)


def pack_rows(source, slot_ids, slot_total, spread):
    row_count = slot_ids.shape[0]
    owner_row = (
        jnp.zeros((slot_total,), jnp.int32)
        .at[slot_ids]
        .set(jnp.arange(row_count, dtype=jnp.int32) + 1)
    )
    filled = owner_row > 0
    picked = jnp.take(source, jnp.maximum(owner_row - 1, 0) // spread, axis=0)
    return jnp.where(filled[:, None], picked, jnp.zeros_like(picked))


def expert_forward(slot_rows, weights):
    hidden = jnp.einsum("nlcd,ldh->nlch", slot_rows, weights, preferred_element_type=jnp.float32)
    active = jax.nn.silu(hidden).astype(jnp.bfloat16)
    return jnp.einsum("nlch,ldh->nlcd", active, weights, preferred_element_type=jnp.float32).astype(
        jnp.bfloat16
    )


def expert_backward(saved_rows, slot_grads, weights):
    hidden = jnp.einsum("nlcd,ldh->nlch", saved_rows, weights, preferred_element_type=jnp.float32)
    active = jax.nn.silu(hidden).astype(jnp.bfloat16)
    active_grads = jnp.einsum(
        "nlcd,ldh->nlch", slot_grads, weights, preferred_element_type=jnp.float32
    )
    sigma = jax.nn.sigmoid(hidden)
    hidden_grads = (active_grads * sigma * (1.0 + hidden * (1.0 - sigma))).astype(jnp.bfloat16)
    row_grads = jnp.einsum(
        "nlch,ldh->nlcd", hidden_grads, weights, preferred_element_type=jnp.float32
    ).astype(jnp.bfloat16)
    weight_part = jnp.einsum(
        "nlcd,nlch->ldh", saved_rows, hidden_grads, preferred_element_type=jnp.float32
    )
    weight_part = weight_part + jnp.einsum(
        "nlcd,nlch->ldh", slot_grads, active, preferred_element_type=jnp.float32
    )
    return (row_grads, weight_part)


def packed_plan(
    section_inputs,
    saved_inputs,
    output_grads,
    forward_routes,
    backward_routes,
    forward_gates,
    backward_gates,
    expert_weights,
):
    token_count = section_inputs.shape[1]
    route_count = forward_routes.shape[2]
    local_count = expert_weights.shape[1]
    model_width = expert_weights.shape[2]
    groups = lax.axis_size("expert")
    experts = groups * local_count
    slot_total = experts * CAP
    block_shape = (groups, local_count, CAP, model_width)
    weights = expert_weights[0]
    forward_slot = slot_index(forward_routes[0].reshape(-1), experts, CAP)
    backward_slot = slot_index(backward_routes[0].reshape(-1), experts, CAP)
    forward_rows = pack_rows(section_inputs[0], forward_slot, slot_total, route_count).reshape(
        block_shape
    )
    saved_rows = pack_rows(saved_inputs[0], backward_slot, slot_total, route_count).reshape(
        block_shape
    )
    grad_block = output_grads[0]
    scaled = backward_gates[0][:, :, None] * grad_block.astype(jnp.float32)[:, None, :]
    scaled = scaled.astype(jnp.bfloat16).reshape(token_count * route_count, model_width)
    slot_grads = pack_rows(scaled, backward_slot, slot_total, 1).reshape(block_shape)
    forward_back = lax.all_to_all(
        expert_forward(
            lax.all_to_all(forward_rows, "expert", split_axis=0, concat_axis=0, tiled=True), weights
        ),
        "expert",
        split_axis=0,
        concat_axis=0,
        tiled=True,
    )
    saved_recv, grads_recv = (
        lax.all_to_all(saved_rows, "expert", split_axis=0, concat_axis=0, tiled=True),
        lax.all_to_all(slot_grads, "expert", split_axis=0, concat_axis=0, tiled=True),
    )
    row_grads, weight_part = expert_backward(saved_recv, grads_recv, weights)
    grads_back = lax.all_to_all(row_grads, "expert", split_axis=0, concat_axis=0, tiled=True)
    forward_pick = jnp.take(forward_back.reshape(slot_total, model_width), forward_slot, axis=0)
    forward_pick = forward_pick.reshape(token_count, route_count, model_width).astype(jnp.float32)
    layer_out = section_inputs[0].astype(jnp.float32) + jnp.sum(
        forward_gates[0][:, :, None] * forward_pick, axis=1
    )
    layer_out = layer_out.astype(jnp.bfloat16)
    grads_pick = jnp.take(grads_back.reshape(slot_total, model_width), backward_slot, axis=0)
    grads_pick = grads_pick.reshape(token_count, route_count, model_width).astype(jnp.float32)
    input_grads = (grad_block.astype(jnp.float32) + jnp.sum(grads_pick, axis=1)).astype(
        jnp.bfloat16
    )
    next_inputs = shifted(layer_out, "pipe", 1)[None]
    prior_grads = shifted(input_grads, "pipe", -1)[None]
    weight_grads = lax.psum_scatter(
        weight_part.astype(jnp.bfloat16), "dp", scatter_dimension=1, tiled=True
    )[None]
    return (next_inputs, prior_grads, weight_grads)


def swapped(value, code):
    axes = ("expert", "dp")
    count = lax.axis_size(axes[0]) * lax.axis_size(axes[1])
    return lax.ppermute(value, axes, [(source, source ^ code) for source in range(count)])


def pack_kernel(*refs):
    sources, out_ref, (*held, notes, done) = refs[:7], refs[7], refs[8:]
    size, width = sources[0].shape
    top = sources[3].shape[0]
    targets = [out_ref.at[:, pl.ds(place * width, width)] for place in range(3)] + held
    copies = [
        pltpu.make_async_copy(source, target, done.at[place])
        for place, (source, target) in enumerate(zip(sources, targets))
    ]
    for copy in copies:
        copy.start()
    for copy in copies:
        copy.wait()
    back_routes, back_gates, fore_routes, fore_gates = held
    notes[...] = jnp.zeros_like(notes)
    for place, (routes, gates) in enumerate(((back_routes, back_gates), (fore_routes, fore_gates))):
        first = place * 4 * top
        notes[pl.ds(first, top), 0:size] = routes[...].astype(jnp.float32)
        rest = gates[...]
        for term in range(1, 4):
            part = rest.astype(jnp.bfloat16).astype(jnp.float32)
            notes[pl.ds(first + term * top, top), 0:size] = part
            rest = rest - part
    out_ref[:, pl.ds(3 * width, LANES)] = notes[...].T[:size, :].astype(jnp.bfloat16)


def picks_kernel(count, top, slots, devices, place_ref, *refs):
    blocks, outs, (notes, turned) = refs[:devices], refs[devices:-2], refs[-2:]
    tokens = notes.shape[0]
    for code, block in enumerate(blocks):
        size = block.shape[0]
        rows = pl.ds(pl.multiple_of(place_ref[3 + code], size), size)
        notes[rows, :] = block[...].astype(jnp.float32)
    turned[...] = notes[...].T
    row = lax.broadcasted_iota(jnp.int32, (tokens, tokens), 0)
    column = lax.broadcasted_iota(jnp.int32, (tokens, tokens), 1)
    earlier = jnp.where(row < column, 1.0, 0.0).astype(jnp.bfloat16)
    slot = lax.broadcasted_iota(jnp.int32, (slots, tokens), 0).astype(jnp.float32)

    def find(first, start):
        ids = (first + lax.broadcasted_iota(jnp.int32, (count, tokens), 0)).astype(jnp.float32)
        named = jnp.zeros((count, tokens), jnp.float32)
        gated = jnp.zeros((count, tokens), jnp.float32)
        for column in range(start, start + top):
            same = turned[column : column + 1, :] == ids
            terms = [turned[column + term * top : column + term * top + 1, :] for term in (1, 2, 3)]
            named = named + jnp.where(same, 1.0, 0.0)
            gated = gated + jnp.where(same, terms[0] + terms[1] + terms[2], 0.0)
        place = jnp.dot(named.astype(jnp.bfloat16), earlier, preferred_element_type=jnp.float32)
        return jnp.where(named > 0.0, place, -1.0), gated

    def fill(place, gated, picks, gates, flipped):
        for expert in range(count):
            rows = pl.ds(expert * slots, slots)
            hit = place[expert : expert + 1, :] == slot
            picks[rows, :] = jnp.where(hit, 1.0, 0.0).astype(jnp.bfloat16)
            own = jnp.sum(jnp.where(hit, gated[expert : expert + 1, :], 0.0), axis=1, keepdims=True)
            gates[rows, :] = jnp.broadcast_to(own, (slots, LANES))
        flipped[...] = picks[...].T

    places, gated = find(place_ref[1], 4 * top)
    fill(places, gated, outs[0], outs[1], outs[2])
    places, gated = find(place_ref[1], 0)
    fill(places, gated, outs[3], outs[4], outs[5])
    other_places, other_gated = find(place_ref[2], 0)
    turned[...] = jnp.zeros_like(turned)
    for row, value in enumerate((places, other_places, gated, other_gated)):
        turned[pl.ds(row * count, count), :] = value
    outs[6][...] = turned[...].T


def spread_gate(gates, rows, width):
    gate = gates[rows, 0:1]
    return jnp.broadcast_to(gate, (gate.shape[0], width))


def assemble(place_ref, blocks, columns, tokens):
    for code, block in enumerate(blocks):
        size = block.shape[0]
        rows = pl.ds(pl.multiple_of(place_ref[3 + code], size), size)
        tokens[rows, :] = block[:, columns]


def combine(flipped, results, sums):
    width = sums.shape[1]
    for start in range(0, width, CHUNK):
        columns = pl.ds(start, CHUNK)
        sums[:, columns] = jnp.dot(
            flipped[...], results[:, columns], preferred_element_type=jnp.float32
        ).astype(sums.dtype)


def gather(count, slots, picks, gates, tokens_ref, rows, first, stride):
    width = tokens_ref.shape[1]
    for start in range(0, width, CHUNK):
        columns = pl.ds(start, CHUNK)
        taken = jnp.dot(picks[...], tokens_ref[:, columns], preferred_element_type=jnp.float32)
        if gates is not None:
            taken = taken * spread_gate(gates, pl.ds(0, count * slots), CHUNK)
        taken = taken.astype(rows.dtype)
        for expert in range(count):
            part = slice(expert * slots, (expert + 1) * slots)
            rows[pl.ds(first + expert * stride, slots), columns] = taken[part]


def expert_kernel(count, slots, devices, pair, place_ref, *refs):
    picks_in, weights, blocks = refs[:6], refs[6 : 6 + WEIGHT_CUTS], refs[6 + WEIGHT_CUTS :][:devices]
    groups = devices // pair
    outs = refs[6 + WEIGHT_CUTS + devices :][: 2 * groups + 2]
    inner, turned, *scratch = refs[8 + WEIGHT_CUTS + devices + 2 * groups :]
    held, tokens = scratch[:6], scratch[6:9]
    rows, fore_results, back_results, second, in_done, out_done = scratch[9:]
    fore_picks, fore_gates, fore_flip, back_picks, back_gates, back_flip = held
    size, (total, width) = blocks[0].shape[0], tokens[0].shape
    step = pl.program_id(0)

    def home(code):
        return pl.ds(pl.multiple_of(place_ref[3 + code], size), size)

    @pl.when(step == 0)
    def _():
        arriving = [
            pltpu.make_async_copy(source, target, in_done.at[3 * devices + place])
            for place, (source, target) in enumerate(zip(picks_in, held))
        ]
        coming = [
            [
                pltpu.make_async_copy(
                    block.at[:, pl.ds(place * width, width)],
                    tokens[place].at[home(code), :],
                    in_done.at[place * devices + code],
                )
                for code, block in enumerate(blocks)
            ]
            for place in range(3)
        ]
        for copy in arriving + coming[0] + coming[1] + coming[2]:
            copy.start()
        for copy in arriving:
            copy.wait()
        taken = ((fore_picks, None), (back_picks, None), (back_picks, back_gates))
        for place, (picks, gates) in enumerate(taken):
            for copy in coming[place]:
                copy.wait()
            gather(count, slots, picks, gates, tokens[place], rows, place * slots, 3 * slots)

    mine = pl.ds(pl.multiple_of(step * slots, slots), slots)
    three = pl.ds(pl.multiple_of(step * 3 * slots, 3 * slots), 3 * slots)
    cut = width // WEIGHT_CUTS
    product = functools.reduce(
        jnp.add,
        [
            jnp.dot(
                rows[three, pl.ds(place * cut, cut)],
                weight[0],
                preferred_element_type=jnp.float32,
            )
            for place, weight in enumerate(weights)
        ],
    )
    ahead, hidden, active_grads = product[:slots], product[slots : 2 * slots], product[2 * slots :]
    sigma = jax.nn.sigmoid(hidden)
    hidden_grads = (active_grads * sigma * (1.0 + hidden * (1.0 - sigma))).astype(jnp.bfloat16)
    inner[0, :slots, :] = hidden_grads
    inner[0, slots:, :] = (hidden * sigma).astype(jnp.bfloat16)
    second[:slots, :] = (ahead * jax.nn.sigmoid(ahead)).astype(jnp.bfloat16)
    second[slots:, :] = hidden_grads
    for place, weight in enumerate(weights):
        columns = pl.ds(place * cut, cut)
        result = lax.dot_general(
            second[...], weight[0], (((1,), (1,)), ((), ())), preferred_element_type=jnp.float32
        )
        fore_results[mine, columns] = (result[:slots] * spread_gate(fore_gates, mine, cut)).astype(
            fore_results.dtype
        )
        back_results[mine, columns] = result[slots:].astype(back_results.dtype)

    span = turned.shape[0]
    first = place_ref[0] * (width // pair) + step * span
    for place in range(2):
        some = tokens[1 + place][:, pl.ds(pl.multiple_of(first, LANES), span)]
        turned[:, pl.ds(place * total, total)] = some.T

    @pl.when(step == count - 1)
    def _():
        leaving = []
        for lead, (flipped, results) in enumerate(
            ((fore_flip, fore_results), (back_flip, back_results))
        ):
            sums = tokens[lead]
            combine(flipped, results, sums)
            *near_outs, far_out = outs[lead * (groups + 1) : (lead + 1) * (groups + 1)]
            targets = [(far_out.at[group], pair * group + 1) for group in range(groups)]
            targets += [(out, pair * group) for group, out in enumerate(near_outs)]
            for target, code in targets:
                done = out_done.at[lead * devices + code]
                leaving.append(pltpu.make_async_copy(sums.at[home(code), :], target, done))
                leaving[-1].start()
        for copy in leaving:
            copy.wait()


def weight_kernel(whose, first, number, count, slots, place_ref, *refs):
    columns_in, inner_in, turned_in = refs[:3]
    out_ref, columns, inner, turned, picks, rows, staged, in_done, out_done = refs[-9:]
    total, half = columns.shape[0], turned.shape[0]
    side = place_ref[0]
    owner = side if whose == 0 else 1 - side
    arriving = [
        pltpu.make_async_copy(columns_in, columns, in_done.at[0]),
        pltpu.make_async_copy(
            inner_in.at[pl.ds(first, number)], inner.at[:, pl.ds(0, 2 * slots), :], in_done.at[1]
        ),
        pltpu.make_async_copy(turned_in, turned, in_done.at[2]),
    ]
    for copy in arriving:
        copy.start()
    inner[:, pl.ds(2 * slots, LANES - 2 * slots), :] = jnp.zeros(
        (number, LANES - 2 * slots, inner.shape[2]), inner.dtype
    )
    arriving[0].wait()
    lane = lax.broadcasted_iota(jnp.int32, (total, LANES), 1).astype(jnp.float32)
    is_saved = lax.broadcasted_iota(jnp.int32, (1, LANES), 1) < slots
    scales = []
    for step in range(number):
        column = whose * count + first + step
        slot = jnp.broadcast_to(columns[:, column : column + 1], (total, LANES))
        column += 2 * count
        gate = jnp.broadcast_to(columns[:, column : column + 1], (total, LANES))
        saved, grads = slot == lane, slot == lane - slots
        lanes = pl.ds(step * LANES, LANES)
        picks[pl.ds(0, total), lanes] = jnp.where(saved, 1.0, 0.0).astype(picks.dtype)
        picks[pl.ds(total, total), lanes] = jnp.where(
            jnp.logical_and(grads, lane >= slots), 1.0, 0.0
        ).astype(picks.dtype)
        scale = jnp.sum(jnp.where(grads, gate, 0.0), axis=0, keepdims=True)
        scales.append(jnp.where(is_saved, 1.0, scale))
    for copy in arriving[1:]:
        copy.wait()
    for step in range(0, number, 2):
        lanes = pl.ds(step * LANES, 2 * LANES)
        scale = jnp.concatenate(scales[step : step + 2], axis=1)
        rows[:, lanes] = (
            jnp.dot(turned[...], picks[:, lanes], preferred_element_type=jnp.float32) * scale
        ).astype(rows.dtype)

    leaving = []
    for step in range(number):
        for start in range(0, half, CHUNK):
            chunk = pl.ds(start, CHUNK)
            staged[step, chunk, :] = jnp.dot(
                rows[chunk, pl.ds(step * LANES, LANES)],
                inner[step],
                preferred_element_type=jnp.float32,
            ).astype(staged.dtype)
            leaving.append(
                pltpu.make_async_copy(
                    staged.at[step, chunk, :],
                    out_ref.at[owner * count + first + step, chunk, :],
                    out_done.at[step, start // CHUNK],
                )
            )
            leaving[-1].start()
    for copy in leaving:
        copy.wait()


def gathered_plan(
    section_inputs,
    saved_inputs,
    output_grads,
    forward_routes,
    backward_routes,
    forward_gates,
    backward_gates,
    expert_weights,
):
    token_count = section_inputs.shape[1]
    top = forward_routes.shape[2]
    _, local_count, width, inner_width = expert_weights.shape
    groups, pair = lax.axis_size("expert"), lax.axis_size("dp")
    devices = groups * pair
    count = local_count // pair
    total = devices * token_count
    slots = -(-devices * CAP // 16) * 16
    rows = count * slots
    half = width // pair
    weights = expert_weights[0]

    side, group = lax.axis_index("dp"), lax.axis_index("expert")
    index = group * pair + side
    base = group * local_count
    place = jnp.stack(
        [side, base + side * count, base + (1 - side) * count]
        + [(index ^ code) * token_count for code in range(devices)]
    ).astype(jnp.int32)
    params = pltpu.CompilerParams(vmem_limit_bytes=VMEM_LIMIT, dimension_semantics=("arbitrary",))

    def whole(shape):
        return pl.BlockSpec(shape, lambda *_: (0,) * len(shape))

    def call(kernel, name, steps, in_specs, out_specs, out_shape, scratch, flops=0, aliases=()):
        return pl.pallas_call(
            kernel,
            grid_spec=pltpu.PrefetchScalarGridSpec(
                num_scalar_prefetch=1,
                grid=(steps,),
                in_specs=in_specs,
                out_specs=out_specs,
                scratch_shapes=scratch,
            ),
            out_shape=out_shape,
            compiler_params=params,
            cost_estimate=pl.CostEstimate(
                flops=flops, bytes_accessed=flops // 512 + 1024, transcendentals=0
            ),
            input_output_aliases=dict(aliases),
            name=name,
        )

    def onward(block):
        return swapped(block, 1)

    def across(parts):
        return [swapped(part, code) for part, code in zip(parts, range(pair, devices, pair))]

    def after(first, then):
        then, _ = lax.optimization_barrier((then, first))
        return then

    def summed(*blocks):
        return functools.reduce(jnp.add, [block.astype(jnp.float32) for block in blocks])

    packed = jax.ShapeDtypeStruct((token_count, 3 * width + LANES), jnp.bfloat16)
    own = pl.pallas_call(
        pack_kernel,
        in_specs=[pl.BlockSpec(memory_space=pl.ANY)] * 7,
        out_specs=pl.BlockSpec(memory_space=pltpu.VMEM),
        out_shape=packed,
        scratch_shapes=[
            pltpu.VMEM((top, token_count), jnp.int32),
            pltpu.VMEM((top, token_count), jnp.float32),
            pltpu.VMEM((top, token_count), jnp.int32),
            pltpu.VMEM((top, token_count), jnp.float32),
            pltpu.VMEM((LANES, LANES), jnp.float32),
            pltpu.SemaphoreType.DMA((7,)),
        ],
        compiler_params=pltpu.CompilerParams(vmem_limit_bytes=VMEM_LIMIT),
        name="pack",
    )(
        *[
            pltpu.with_memory_space_constraint(array, pltpu.HBM)
            for array in (
                section_inputs[0],
                saved_inputs[0],
                output_grads[0],
                backward_routes[0].T,
                backward_gates[0].T,
                forward_routes[0].T,
                forward_gates[0].T,
            )
        ]
    )
    near = [own] + across([own] * (groups - 1))
    blocks = [block for one in near for block in (one, onward(one))]

    pick = jax.ShapeDtypeStruct((rows, total), jnp.bfloat16)
    flip = jax.ShapeDtypeStruct((total, rows), jnp.bfloat16)
    gate = jax.ShapeDtypeStruct((rows, LANES), jnp.float32)
    columns = jax.ShapeDtypeStruct((total, LANES), jnp.float32)
    pick_outs = [pick, gate, flip, pick, gate, flip, columns]
    picks = call(
        functools.partial(picks_kernel, count, top, slots, devices),
        "slot_picks",
        1,
        [pl.BlockSpec((token_count, LANES), lambda *_: (0, 3 * width // LANES))] * devices,
        [whole(out.shape) for out in pick_outs],
        pick_outs,
        [pltpu.VMEM((total, LANES), jnp.float32), pltpu.VMEM((LANES, total), jnp.float32)],
    )(place, *blocks)

    pass_flops = 2 * 2 * count * CHUNK * width * inner_width
    near_part = jax.ShapeDtypeStruct((token_count, width), jnp.bfloat16)
    far_part = jax.ShapeDtypeStruct((groups, token_count, width), jnp.bfloat16)
    inner = jax.ShapeDtypeStruct((count, 2 * slots, inner_width), jnp.bfloat16)
    turned = jax.ShapeDtypeStruct((half, 2 * total), jnp.bfloat16)
    in_smem, anywhere = (pl.BlockSpec(memory_space=space) for space in (pltpu.SMEM, pl.ANY))
    tokens = pltpu.VMEM((total, width), jnp.bfloat16)
    cut = width // WEIGHT_CUTS
    *parts, inner_own, tokens_turned = pl.pallas_call(
        functools.partial(expert_kernel, count, slots, devices, pair),
        grid_spec=pltpu.PrefetchScalarGridSpec(
            num_scalar_prefetch=1,
            grid=(count,),
            in_specs=[anywhere] * 6
            + [
                pl.BlockSpec(
                    (1, cut, inner_width),
                    lambda step, place, part=part: (place[0] * count + step, part, 0),
                )
                for part in range(WEIGHT_CUTS)
            ]
            + [anywhere] * devices,
            out_specs=[anywhere] * (2 * groups + 2)
            + [
                pl.BlockSpec((1, 2 * slots, inner_width), lambda step, place: (step, 0, 0)),
                pl.BlockSpec((half // count, 2 * total), lambda step, place: (step, 0)),
            ],
            scratch_shapes=[pltpu.VMEM(array.shape, array.dtype) for array in pick_outs[:6]]
            + [tokens] * 3
            + [
                pltpu.VMEM((3 * rows, width), jnp.bfloat16),
                pltpu.VMEM((rows, width), jnp.bfloat16),
                pltpu.VMEM((rows, width), jnp.bfloat16),
                pltpu.VMEM((2 * slots, inner_width), jnp.bfloat16),
                pltpu.SemaphoreType.DMA((3 * devices + 6,)),
                pltpu.SemaphoreType.DMA((2 * devices,)),
            ],
        ),
        out_shape=([near_part] * groups + [far_part]) * 2 + [inner, turned],
        compiler_params=pltpu.CompilerParams(
            vmem_limit_bytes=EXPERTS_LIMIT, dimension_semantics=("arbitrary",)
        ),
        cost_estimate=pl.CostEstimate(
            flops=pass_flops, bytes_accessed=pass_flops // 512, transcendentals=0
        ),
        name="experts",
    )(place, *picks[:6], *[weights] * WEIGHT_CUTS, *blocks)
    *layer_parts, layer_far = parts[: groups + 1]
    *grad_parts, grad_far = parts[groups + 1 :]
    layer_far, grad_far, inner_other = onward(layer_far), onward(grad_far), onward(inner_own)

    def gradient(whose, first, number, inner_rows, earlier):
        earlier = [] if earlier is None else [earlier]
        operands = [picks[6], inner_rows, tokens_turned] + earlier
        return pl.pallas_call(
            functools.partial(weight_kernel, whose, first, number, count, slots),
            in_specs=[in_smem] + [anywhere] * len(operands),
            out_specs=anywhere,
            out_shape=jax.ShapeDtypeStruct((local_count, half, inner_width), jnp.bfloat16),
            scratch_shapes=[
                pltpu.VMEM(columns.shape, columns.dtype),
                pltpu.VMEM((number, LANES, inner_width), jnp.bfloat16),
                pltpu.VMEM(turned.shape, turned.dtype),
                pltpu.VMEM((2 * total, number * LANES), jnp.bfloat16),
                pltpu.VMEM((half, number * LANES), jnp.bfloat16),
                pltpu.VMEM((number, half, inner_width), jnp.bfloat16),
                pltpu.SemaphoreType.DMA((3,)),
                pltpu.SemaphoreType.DMA((number, half // CHUNK)),
            ],
            compiler_params=pltpu.CompilerParams(vmem_limit_bytes=VMEM_LIMIT),
            cost_estimate=pl.CostEstimate(
                flops=number * pass_flops // count // 2,
                bytes_accessed=number * half * inner_width * 4,
                transcendentals=0,
            ),
            input_output_aliases={len(operands): 0} if earlier else {},
            name=f"weight_gradient_{whose}_{first}",
        )(place, *operands)

    def pair_sums(near_parts, far):
        return [summed(part, far[group]).astype(jnp.bfloat16) for group, part in enumerate(near_parts)]

    piece = -(-count // 2)
    done = gradient(0, 0, piece, inner_own, None)
    layer_sums = pair_sums(layer_parts, after(done, layer_far))
    layer_near = across(layer_sums[1:])
    grad_sums = pair_sums(grad_parts, after((layer_sums, inner_other), grad_far))
    grad_near = across(grad_sums[1:])
    done = after(grad_sums, done)
    if piece < count:
        done = gradient(0, piece, count - piece, inner_own, done)
    done = gradient(1, 0, piece, inner_other, after(layer_near[0], done))
    layer_near = after(done, layer_near)
    layer_out = summed(section_inputs[0], layer_sums[0], *layer_near).astype(jnp.bfloat16)
    next_inputs = shifted(layer_out, "pipe", 1)[None]
    done = after(layer_out, done)
    if piece < count:
        done = gradient(1, piece, count - piece, inner_other, done)
    grad_near = after((done, next_inputs), grad_near)
    input_grads = summed(output_grads[0], grad_sums[0], *grad_near).astype(jnp.bfloat16)
    prior_grads = shifted(input_grads, "pipe", -1)[None]
    return (next_inputs, prior_grads, done[None])


def on_device(*arrays):
    token_count = arrays[0].shape[1]
    local_count = arrays[-1].shape[1]
    groups, pair = lax.axis_size("expert"), lax.axis_size("dp")
    gathered = groups * token_count
    packed = groups * local_count * CAP
    paired = pair == 2 and local_count % 8 == 0 and groups & (groups - 1) == 0
    if gathered <= packed and paired and gathered * pair % LANES == 0:
        return gathered_plan(*arrays)
    return packed_plan(*arrays)


def solution(mesh):
    placed = (
        P("pipe", ("expert", "dp"), None),
        P("pipe", ("expert", "dp"), None),
        P("pipe", ("expert", "dp"), None),
        P("pipe", ("expert", "dp"), None),
        P("pipe", ("expert", "dp"), None),
        P("pipe", ("expert", "dp"), None),
        P("pipe", ("expert", "dp"), None),
        P("pipe", "expert", None, None),
    )
    return jax.shard_map(
        on_device,
        mesh=mesh,
        in_specs=placed,
        out_specs=(
            P("pipe", ("expert", "dp"), None),
            P("pipe", ("expert", "dp"), None),
            P("pipe", "expert", "dp", None),
        ),
        check_vma=False,
    )
```

```python
import functools

import jax
import jax.numpy as jnp
from jax import lax
from jax.experimental import pallas as pl
from jax.experimental.pallas import tpu as pltpu
from jax.sharding import PartitionSpec as P

CAP = 5
LANES = 128
CHUNK = 256
VMEM_LIMIT = 24 * 1024 * 1024
EXPERTS_LIMIT = 40 * 1024 * 1024
WEIGHT_CUTS = 4


def shifted(value, axis, steps):
    count = lax.axis_size(axis)
    pairs = [(source, (source + steps) % count) for source in range(count)]
    return lax.ppermute(value, axis, pairs)


def slot_index(routing, experts, capacity):
    one_hot = (routing[..., None] == jnp.arange(experts, dtype=jnp.int32)).astype(jnp.int32)
    before = jnp.cumsum(one_hot, axis=-2) - one_hot
    return routing * capacity + jnp.sum(before * one_hot, axis=-1)


def pack_rows(source, slot_ids, slot_total, spread):
    row_count = slot_ids.shape[0]
    owner_row = (
        jnp.zeros((slot_total,), jnp.int32)
        .at[slot_ids]
        .set(jnp.arange(row_count, dtype=jnp.int32) + 1)
    )
    filled = owner_row > 0
    picked = jnp.take(source, jnp.maximum(owner_row - 1, 0) // spread, axis=0)
    return jnp.where(filled[:, None], picked, jnp.zeros_like(picked))


def expert_forward(slot_rows, weights):
    hidden = jnp.einsum("nlcd,ldh->nlch", slot_rows, weights, preferred_element_type=jnp.float32)
    active = jax.nn.silu(hidden).astype(jnp.bfloat16)
    return jnp.einsum("nlch,ldh->nlcd", active, weights, preferred_element_type=jnp.float32).astype(
        jnp.bfloat16
    )


def expert_backward(saved_rows, slot_grads, weights):
    hidden = jnp.einsum("nlcd,ldh->nlch", saved_rows, weights, preferred_element_type=jnp.float32)
    active = jax.nn.silu(hidden).astype(jnp.bfloat16)
    active_grads = jnp.einsum(
        "nlcd,ldh->nlch", slot_grads, weights, preferred_element_type=jnp.float32
    )
    sigma = jax.nn.sigmoid(hidden)
    hidden_grads = (active_grads * sigma * (1.0 + hidden * (1.0 - sigma))).astype(jnp.bfloat16)
    row_grads = jnp.einsum(
        "nlch,ldh->nlcd", hidden_grads, weights, preferred_element_type=jnp.float32
    ).astype(jnp.bfloat16)
    weight_part = jnp.einsum(
        "nlcd,nlch->ldh", saved_rows, hidden_grads, preferred_element_type=jnp.float32
    )
    weight_part = weight_part + jnp.einsum(
        "nlcd,nlch->ldh", slot_grads, active, preferred_element_type=jnp.float32
    )
    return (row_grads, weight_part)


def packed_plan(
    section_inputs,
    saved_inputs,
    output_grads,
    forward_routes,
    backward_routes,
    forward_gates,
    backward_gates,
    expert_weights,
):
    token_count = section_inputs.shape[1]
    route_count = forward_routes.shape[2]
    local_count = expert_weights.shape[1]
    model_width = expert_weights.shape[2]
    groups = lax.axis_size("expert")
    experts = groups * local_count
    slot_total = experts * CAP
    block_shape = (groups, local_count, CAP, model_width)
    weights = expert_weights[0]
    forward_slot = slot_index(forward_routes[0].reshape(-1), experts, CAP)
    backward_slot = slot_index(backward_routes[0].reshape(-1), experts, CAP)
    forward_rows = pack_rows(section_inputs[0], forward_slot, slot_total, route_count).reshape(
        block_shape
    )
    saved_rows = pack_rows(saved_inputs[0], backward_slot, slot_total, route_count).reshape(
        block_shape
    )
    grad_block = output_grads[0]
    scaled = backward_gates[0][:, :, None] * grad_block.astype(jnp.float32)[:, None, :]
    scaled = scaled.astype(jnp.bfloat16).reshape(token_count * route_count, model_width)
    slot_grads = pack_rows(scaled, backward_slot, slot_total, 1).reshape(block_shape)
    forward_back = lax.all_to_all(
        expert_forward(
            lax.all_to_all(forward_rows, "expert", split_axis=0, concat_axis=0, tiled=True), weights
        ),
        "expert",
        split_axis=0,
        concat_axis=0,
        tiled=True,
    )
    saved_recv, grads_recv = (
        lax.all_to_all(saved_rows, "expert", split_axis=0, concat_axis=0, tiled=True),
        lax.all_to_all(slot_grads, "expert", split_axis=0, concat_axis=0, tiled=True),
    )
    row_grads, weight_part = expert_backward(saved_recv, grads_recv, weights)
    grads_back = lax.all_to_all(row_grads, "expert", split_axis=0, concat_axis=0, tiled=True)
    forward_pick = jnp.take(forward_back.reshape(slot_total, model_width), forward_slot, axis=0)
    forward_pick = forward_pick.reshape(token_count, route_count, model_width).astype(jnp.float32)
    layer_out = section_inputs[0].astype(jnp.float32) + jnp.sum(
        forward_gates[0][:, :, None] * forward_pick, axis=1
    )
    layer_out = layer_out.astype(jnp.bfloat16)
    grads_pick = jnp.take(grads_back.reshape(slot_total, model_width), backward_slot, axis=0)
    grads_pick = grads_pick.reshape(token_count, route_count, model_width).astype(jnp.float32)
    input_grads = (grad_block.astype(jnp.float32) + jnp.sum(grads_pick, axis=1)).astype(
        jnp.bfloat16
    )
    next_inputs = shifted(layer_out, "pipe", 1)[None]
    prior_grads = shifted(input_grads, "pipe", -1)[None]
    weight_grads = lax.psum_scatter(
        weight_part.astype(jnp.bfloat16), "dp", scatter_dimension=1, tiled=True
    )[None]
    return (next_inputs, prior_grads, weight_grads)


def swapped(value, code):
    axes = ("expert", "dp")
    count = lax.axis_size(axes[0]) * lax.axis_size(axes[1])
    return lax.ppermute(value, axes, [(source, source ^ code) for source in range(count)])


def pack_kernel(*refs):
    sources, out_ref, (*held, notes, done) = refs[:7], refs[7], refs[8:]
    size, width = sources[0].shape
    top = sources[3].shape[0]
    targets = [out_ref.at[:, pl.ds(place * width, width)] for place in range(3)] + held
    copies = [
        pltpu.make_async_copy(source, target, done.at[place])
        for place, (source, target) in enumerate(zip(sources, targets))
    ]
    for copy in copies:
        copy.start()
    for copy in copies:
        copy.wait()
    back_routes, back_gates, fore_routes, fore_gates = held
    notes[...] = jnp.zeros_like(notes)
    for place, (routes, gates) in enumerate(((back_routes, back_gates), (fore_routes, fore_gates))):
        first = place * 4 * top
        notes[pl.ds(first, top), 0:size] = routes[...].astype(jnp.float32)
        rest = gates[...]
        for term in range(1, 4):
            part = rest.astype(jnp.bfloat16).astype(jnp.float32)
            notes[pl.ds(first + term * top, top), 0:size] = part
            rest = rest - part
    out_ref[:, pl.ds(3 * width, LANES)] = notes[...].T[:size, :].astype(jnp.bfloat16)


def picks_kernel(count, top, slots, devices, place_ref, *refs):
    blocks, outs, (notes, turned) = refs[:devices], refs[devices:-2], refs[-2:]
    tokens = notes.shape[0]
    for code, block in enumerate(blocks):
        size = block.shape[0]
        rows = pl.ds(pl.multiple_of(place_ref[3 + code], size), size)
        notes[rows, :] = block[...].astype(jnp.float32)
    turned[...] = notes[...].T
    row = lax.broadcasted_iota(jnp.int32, (tokens, tokens), 0)
    column = lax.broadcasted_iota(jnp.int32, (tokens, tokens), 1)
    earlier = jnp.where(row < column, 1.0, 0.0).astype(jnp.bfloat16)
    slot = lax.broadcasted_iota(jnp.int32, (slots, tokens), 0).astype(jnp.float32)

    def find(first, start):
        ids = (first + lax.broadcasted_iota(jnp.int32, (count, tokens), 0)).astype(jnp.float32)
        named = jnp.zeros((count, tokens), jnp.float32)
        gated = jnp.zeros((count, tokens), jnp.float32)
        for column in range(start, start + top):
            same = turned[column : column + 1, :] == ids
            terms = [turned[column + term * top : column + term * top + 1, :] for term in (1, 2, 3)]
            named = named + jnp.where(same, 1.0, 0.0)
            gated = gated + jnp.where(same, terms[0] + terms[1] + terms[2], 0.0)
        place = jnp.dot(named.astype(jnp.bfloat16), earlier, preferred_element_type=jnp.float32)
        return jnp.where(named > 0.0, place, -1.0), gated

    def fill(place, gated, picks, gates, flipped):
        for expert in range(count):
            rows = pl.ds(expert * slots, slots)
            hit = place[expert : expert + 1, :] == slot
            picks[rows, :] = jnp.where(hit, 1.0, 0.0).astype(jnp.bfloat16)
            own = jnp.sum(jnp.where(hit, gated[expert : expert + 1, :], 0.0), axis=1, keepdims=True)
            gates[rows, :] = jnp.broadcast_to(own, (slots, LANES))
        flipped[...] = picks[...].T

    places, gated = find(place_ref[1], 4 * top)
    fill(places, gated, outs[0], outs[1], outs[2])
    places, gated = find(place_ref[1], 0)
    fill(places, gated, outs[3], outs[4], outs[5])
    other_places, other_gated = find(place_ref[2], 0)
    turned[...] = jnp.zeros_like(turned)
    for row, value in enumerate((places, other_places, gated, other_gated)):
        turned[pl.ds(row * count, count), :] = value
    outs[6][...] = turned[...].T


def spread_gate(gates, rows, width):
    gate = gates[rows, 0:1]
    return jnp.broadcast_to(gate, (gate.shape[0], width))


def assemble(place_ref, blocks, columns, tokens):
    for code, block in enumerate(blocks):
        size = block.shape[0]
        rows = pl.ds(pl.multiple_of(place_ref[3 + code], size), size)
        tokens[rows, :] = block[:, columns]


def combine(flipped, results, sums):
    width = sums.shape[1]
    for start in range(0, width, CHUNK):
        columns = pl.ds(start, CHUNK)
        sums[:, columns] = jnp.dot(
            flipped[...], results[:, columns], preferred_element_type=jnp.float32
        ).astype(sums.dtype)


def gather(count, slots, picks, gates, tokens_ref, rows, first, stride):
    width = tokens_ref.shape[1]
    for start in range(0, width, CHUNK):
        columns = pl.ds(start, CHUNK)
        taken = jnp.dot(picks[...], tokens_ref[:, columns], preferred_element_type=jnp.float32)
        if gates is not None:
            taken = taken * spread_gate(gates, pl.ds(0, count * slots), CHUNK)
        taken = taken.astype(rows.dtype)
        for expert in range(count):
            part = slice(expert * slots, (expert + 1) * slots)
            rows[pl.ds(first + expert * stride, slots), columns] = taken[part]


def expert_kernel(count, slots, devices, pair, place_ref, *refs):
    fore_picks, fore_gates, fore_flip, back_picks, back_gates, back_flip = refs[:6]
    weights, blocks = refs[6 : 6 + WEIGHT_CUTS], refs[6 + WEIGHT_CUTS :][:devices]
    groups = devices // pair
    outs = refs[6 + WEIGHT_CUTS + devices :][: 2 * groups + 2]
    inner, turned, *scratch = refs[8 + WEIGHT_CUTS + devices + 2 * groups :]
    tokens, (rows, fore_results, back_results, second) = scratch[:3], scratch[3:]
    total, width = tokens[0].shape
    step = pl.program_id(0)

    @pl.when(step == 0)
    def _():
        taken = ((fore_picks, None), (back_picks, None), (back_picks, back_gates))
        for place, (picks, gates) in enumerate(taken):
            assemble(place_ref, blocks, pl.ds(place * width, width), tokens[place])
            gather(count, slots, picks, gates, tokens[place], rows, place * slots, 3 * slots)

    mine = pl.ds(pl.multiple_of(step * slots, slots), slots)
    three = pl.ds(pl.multiple_of(step * 3 * slots, 3 * slots), 3 * slots)
    cut = width // WEIGHT_CUTS
    product = functools.reduce(
        jnp.add,
        [
            jnp.dot(
                rows[three, pl.ds(place * cut, cut)],
                weight[0],
                preferred_element_type=jnp.float32,
            )
            for place, weight in enumerate(weights)
        ],
    )
    ahead, hidden, active_grads = product[:slots], product[slots : 2 * slots], product[2 * slots :]
    sigma = jax.nn.sigmoid(hidden)
    hidden_grads = (active_grads * sigma * (1.0 + hidden * (1.0 - sigma))).astype(jnp.bfloat16)
    inner[0, :slots, :] = hidden_grads
    inner[0, slots:, :] = (hidden * sigma).astype(jnp.bfloat16)
    gate = spread_gate(fore_gates, mine, ahead.shape[1])
    second[:slots, :] = (ahead * jax.nn.sigmoid(ahead) * gate).astype(jnp.bfloat16)
    second[slots:, :] = hidden_grads
    for place, weight in enumerate(weights):
        columns = pl.ds(place * cut, cut)
        result = lax.dot_general(
            second[...], weight[0], (((1,), (1,)), ((), ())), preferred_element_type=jnp.float32
        ).astype(fore_results.dtype)
        fore_results[mine, columns] = result[:slots]
        back_results[mine, columns] = result[slots:]

    span = turned.shape[0]
    first = place_ref[0] * (width // pair) + step * span
    for place in range(2):
        some = tokens[1 + place][:, pl.ds(pl.multiple_of(first, LANES), span)]
        turned[:, pl.ds(place * total, total)] = some.T

    @pl.when(step == count - 1)
    def _():
        for lead, (flipped, results) in enumerate(
            ((fore_flip, fore_results), (back_flip, back_results))
        ):
            sums = tokens[lead]
            combine(flipped, results, sums)
            *near_outs, far_out = outs[lead * (groups + 1) : (lead + 1) * (groups + 1)]
            size = far_out.shape[1]
            for group, out in enumerate(near_outs):
                near, far = (
                    pl.ds(pl.multiple_of(place_ref[3 + pair * group + code], size), size)
                    for code in range(pair)
                )
                out[...] = sums[near, :]
                far_out[group] = sums[far, :]


def weight_kernel(whose, first, number, count, slots, place_ref, *refs):
    columns, inner, turned = refs[:3]
    out_ref, picks, rows, staged, out_done = refs[-5:]
    total, half = columns.shape[0], turned.shape[0]
    side = place_ref[0]
    owner = side if whose == 0 else 1 - side
    lane = lax.broadcasted_iota(jnp.int32, (total, LANES), 1).astype(jnp.float32)
    is_saved = lax.broadcasted_iota(jnp.int32, (1, LANES), 1) < slots
    scales = []
    for step in range(number):
        column = whose * count + first + step
        slot = jnp.broadcast_to(columns[:, column : column + 1], (total, LANES))
        column += 2 * count
        gate = jnp.broadcast_to(columns[:, column : column + 1], (total, LANES))
        saved, grads = slot == lane, slot == lane - slots
        lanes = pl.ds(step * LANES, LANES)
        picks[pl.ds(0, total), lanes] = jnp.where(saved, 1.0, 0.0).astype(picks.dtype)
        picks[pl.ds(total, total), lanes] = jnp.where(
            jnp.logical_and(grads, lane >= slots), 1.0, 0.0
        ).astype(picks.dtype)
        scale = jnp.sum(jnp.where(grads, gate, 0.0), axis=0, keepdims=True)
        scales.append(jnp.where(is_saved, 1.0, scale))
    for step in range(0, number, 2):
        lanes = pl.ds(step * LANES, 2 * LANES)
        scale = jnp.concatenate(scales[step : step + 2], axis=1)
        rows[:, lanes] = (
            jnp.dot(turned[...], picks[:, lanes], preferred_element_type=jnp.float32) * scale
        ).astype(rows.dtype)

    leaving = []
    for step in range(number):
        for start in range(0, half, CHUNK):
            chunk = pl.ds(start, CHUNK)
            staged[step, chunk, :] = jnp.dot(
                rows[chunk, pl.ds(step * LANES, 2 * slots)],
                inner[first + step],
                preferred_element_type=jnp.float32,
            ).astype(staged.dtype)
            leaving.append(
                pltpu.make_async_copy(
                    staged.at[step, chunk, :],
                    out_ref.at[owner * count + first + step, chunk, :],
                    out_done.at[step, start // CHUNK],
                )
            )
            leaving[-1].start()
    for copy in leaving:
        copy.wait()


def gathered_plan(
    section_inputs,
    saved_inputs,
    output_grads,
    forward_routes,
    backward_routes,
    forward_gates,
    backward_gates,
    expert_weights,
):
    token_count = section_inputs.shape[1]
    top = forward_routes.shape[2]
    _, local_count, width, inner_width = expert_weights.shape
    groups, pair = lax.axis_size("expert"), lax.axis_size("dp")
    devices = groups * pair
    count = local_count // pair
    total = devices * token_count
    slots = -(-devices * CAP // 16) * 16
    rows = count * slots
    half = width // pair
    weights = expert_weights[0]

    side, group = lax.axis_index("dp"), lax.axis_index("expert")
    index = group * pair + side
    base = group * local_count
    place = jnp.stack(
        [side, base + side * count, base + (1 - side) * count]
        + [(index ^ code) * token_count for code in range(devices)]
    ).astype(jnp.int32)
    params = pltpu.CompilerParams(vmem_limit_bytes=VMEM_LIMIT, dimension_semantics=("arbitrary",))

    def whole(shape):
        return pl.BlockSpec(shape, lambda *_: (0,) * len(shape))

    def call(kernel, name, steps, in_specs, out_specs, out_shape, scratch, flops=0, aliases=()):
        return pl.pallas_call(
            kernel,
            grid_spec=pltpu.PrefetchScalarGridSpec(
                num_scalar_prefetch=1,
                grid=(steps,),
                in_specs=in_specs,
                out_specs=out_specs,
                scratch_shapes=scratch,
            ),
            out_shape=out_shape,
            compiler_params=params,
            cost_estimate=pl.CostEstimate(
                flops=flops, bytes_accessed=flops // 512 + 1024, transcendentals=0
            ),
            input_output_aliases=dict(aliases),
            name=name,
        )

    def onward(block):
        return swapped(block, 1)

    def across(parts):
        return [swapped(part, code) for part, code in zip(parts, range(pair, devices, pair))]

    def after(first, then):
        then, _ = lax.optimization_barrier((then, first))
        return then

    def summed(*blocks):
        return functools.reduce(jnp.add, [block.astype(jnp.float32) for block in blocks])

    packed = jax.ShapeDtypeStruct((token_count, 3 * width + LANES), jnp.bfloat16)
    own = pl.pallas_call(
        pack_kernel,
        in_specs=[pl.BlockSpec(memory_space=pl.ANY)] * 7,
        out_specs=pl.BlockSpec(memory_space=pltpu.VMEM),
        out_shape=packed,
        scratch_shapes=[
            pltpu.VMEM((top, token_count), jnp.int32),
            pltpu.VMEM((top, token_count), jnp.float32),
            pltpu.VMEM((top, token_count), jnp.int32),
            pltpu.VMEM((top, token_count), jnp.float32),
            pltpu.VMEM((LANES, LANES), jnp.float32),
            pltpu.SemaphoreType.DMA((7,)),
        ],
        compiler_params=pltpu.CompilerParams(vmem_limit_bytes=VMEM_LIMIT),
        name="pack",
    )(
        *[
            pltpu.with_memory_space_constraint(array, pltpu.HBM)
            for array in (
                section_inputs[0],
                saved_inputs[0],
                output_grads[0],
                backward_routes[0].T,
                backward_gates[0].T,
                forward_routes[0].T,
                forward_gates[0].T,
            )
        ]
    )
    near = [own] + across([own] * (groups - 1))
    blocks = [block for one in near for block in (one, onward(one))]

    pick = jax.ShapeDtypeStruct((rows, total), jnp.bfloat16)
    flip = jax.ShapeDtypeStruct((total, rows), jnp.bfloat16)
    gate = jax.ShapeDtypeStruct((rows, LANES), jnp.float32)
    columns = jax.ShapeDtypeStruct((total, LANES), jnp.float32)
    pick_outs = [pick, gate, flip, pick, gate, flip, columns]
    picks = call(
        functools.partial(picks_kernel, count, top, slots, devices),
        "slot_picks",
        1,
        [pl.BlockSpec((token_count, LANES), lambda *_: (0, 3 * width // LANES))] * devices,
        [whole(out.shape) for out in pick_outs],
        pick_outs,
        [pltpu.VMEM((total, LANES), jnp.float32), pltpu.VMEM((LANES, total), jnp.float32)],
    )(place, *blocks)

    pass_flops = 2 * 2 * count * CHUNK * width * inner_width
    near_part = jax.ShapeDtypeStruct((token_count, width), jnp.bfloat16)
    far_part = jax.ShapeDtypeStruct((groups, token_count, width), jnp.bfloat16)
    inner = jax.ShapeDtypeStruct((count, 2 * slots, inner_width), jnp.bfloat16)
    turned = jax.ShapeDtypeStruct((half, 2 * total), jnp.bfloat16)
    in_smem, in_vmem, anywhere = (
        pl.BlockSpec(memory_space=space) for space in (pltpu.SMEM, pltpu.VMEM, pl.ANY)
    )
    tokens = pltpu.VMEM((total, width), jnp.bfloat16)
    cut = width // WEIGHT_CUTS
    *parts, inner_own, tokens_turned = pl.pallas_call(
        functools.partial(expert_kernel, count, slots, devices, pair),
        grid_spec=pltpu.PrefetchScalarGridSpec(
            num_scalar_prefetch=1,
            grid=(count,),
            in_specs=[whole(array.shape) for array in pick_outs[:6]]
            + [
                pl.BlockSpec(
                    (1, cut, inner_width),
                    lambda step, place, part=part: (place[0] * count + step, part, 0),
                )
                for part in range(WEIGHT_CUTS)
            ]
            + [whole(packed.shape)] * devices,
            out_specs=([whole(near_part.shape)] * groups + [whole(far_part.shape)]) * 2
            + [
                pl.BlockSpec((1, 2 * slots, inner_width), lambda step, place: (step, 0, 0)),
                pl.BlockSpec((half // count, 2 * total), lambda step, place: (step, 0)),
            ],
            scratch_shapes=[tokens] * 3
            + [
                pltpu.VMEM((3 * rows, width), jnp.bfloat16),
                pltpu.VMEM((rows, width), jnp.bfloat16),
                pltpu.VMEM((rows, width), jnp.bfloat16),
                pltpu.VMEM((2 * slots, inner_width), jnp.bfloat16),
            ],
        ),
        out_shape=([near_part] * groups + [far_part]) * 2 + [inner, turned],
        compiler_params=pltpu.CompilerParams(
            vmem_limit_bytes=EXPERTS_LIMIT, dimension_semantics=("arbitrary",)
        ),
        cost_estimate=pl.CostEstimate(
            flops=pass_flops, bytes_accessed=pass_flops // 512, transcendentals=0
        ),
        name="experts",
    )(place, *picks[:6], *[weights] * WEIGHT_CUTS, *blocks)
    *layer_parts, layer_far = parts[: groups + 1]
    *grad_parts, grad_far = parts[groups + 1 :]
    layer_far, grad_far, inner_other = onward(layer_far), onward(grad_far), onward(inner_own)

    def gradient(whose, first, number, inner_rows, earlier):
        earlier = [] if earlier is None else [earlier]
        operands = [picks[6], inner_rows, tokens_turned] + earlier
        return pl.pallas_call(
            functools.partial(weight_kernel, whose, first, number, count, slots),
            in_specs=[in_smem, in_vmem, in_vmem, in_vmem] + [anywhere] * len(earlier),
            out_specs=anywhere,
            out_shape=jax.ShapeDtypeStruct((local_count, half, inner_width), jnp.bfloat16),
            scratch_shapes=[
                pltpu.VMEM((2 * total, number * LANES), jnp.bfloat16),
                pltpu.VMEM((half, number * LANES), jnp.bfloat16),
                pltpu.VMEM((number, half, inner_width), jnp.bfloat16),
                pltpu.SemaphoreType.DMA((number, half // CHUNK)),
            ],
            compiler_params=pltpu.CompilerParams(vmem_limit_bytes=VMEM_LIMIT),
            cost_estimate=pl.CostEstimate(
                flops=number * pass_flops // count // 2,
                bytes_accessed=number * half * inner_width * 4,
                transcendentals=0,
            ),
            input_output_aliases={len(operands): 0} if earlier else {},
            name=f"weight_gradient_{whose}_{first}",
        )(place, *operands)

    def pair_sums(near_parts, far):
        return [summed(part, far[group]).astype(jnp.bfloat16) for group, part in enumerate(near_parts)]

    piece = -(-count // 2)
    done = gradient(0, 0, piece, inner_own, None)
    layer_sums = pair_sums(layer_parts, after(done, layer_far))
    layer_near = across(layer_sums[1:])
    grad_sums = pair_sums(grad_parts, after((layer_sums, inner_other), grad_far))
    grad_near = across(grad_sums[1:])
    done = after(grad_sums, done)
    if piece < count:
        done = gradient(0, piece, count - piece, inner_own, done)
    done = gradient(1, 0, piece, inner_other, after(layer_near[0], done))
    layer_near = after(done, layer_near)
    layer_out = summed(section_inputs[0], layer_sums[0], *layer_near).astype(jnp.bfloat16)
    next_inputs = shifted(layer_out, "pipe", 1)[None]
    done = after(layer_out, done)
    if piece < count:
        done = gradient(1, piece, count - piece, inner_other, done)
    grad_near = after((done, next_inputs), grad_near)
    input_grads = summed(output_grads[0], grad_sums[0], *grad_near).astype(jnp.bfloat16)
    prior_grads = shifted(input_grads, "pipe", -1)[None]
    return (next_inputs, prior_grads, done[None])


def on_device(*arrays):
    token_count = arrays[0].shape[1]
    local_count = arrays[-1].shape[1]
    groups, pair = lax.axis_size("expert"), lax.axis_size("dp")
    gathered = groups * token_count
    packed = groups * local_count * CAP
    paired = pair == 2 and local_count % 8 == 0 and groups & (groups - 1) == 0
    if gathered <= packed and paired and gathered * pair % LANES == 0:
        return gathered_plan(*arrays)
    return packed_plan(*arrays)


def solution(mesh):
    placed = (
        P("pipe", ("expert", "dp"), None),
        P("pipe", ("expert", "dp"), None),
        P("pipe", ("expert", "dp"), None),
        P("pipe", ("expert", "dp"), None),
        P("pipe", ("expert", "dp"), None),
        P("pipe", ("expert", "dp"), None),
        P("pipe", ("expert", "dp"), None),
        P("pipe", "expert", None, None),
    )
    return jax.shard_map(
        on_device,
        mesh=mesh,
        in_specs=placed,
        out_specs=(
            P("pipe", ("expert", "dp"), None),
            P("pipe", ("expert", "dp"), None),
            P("pipe", "expert", "dp", None),
        ),
        check_vma=False,
    )
```

```python
import functools

import jax
import jax.numpy as jnp
from jax import lax
from jax.experimental import pallas as pl
from jax.experimental.pallas import tpu as pltpu
from jax.sharding import PartitionSpec as P

CAP = 5
LANES = 128
CHUNK = 256
VMEM_LIMIT = 24 * 1024 * 1024
EXPERTS_LIMIT = 40 * 1024 * 1024
WEIGHT_CUTS = 4


def shifted(value, axis, steps):
    count = lax.axis_size(axis)
    pairs = [(source, (source + steps) % count) for source in range(count)]
    return lax.ppermute(value, axis, pairs)


def slot_index(routing, experts, capacity):
    one_hot = (routing[..., None] == jnp.arange(experts, dtype=jnp.int32)).astype(jnp.int32)
    before = jnp.cumsum(one_hot, axis=-2) - one_hot
    return routing * capacity + jnp.sum(before * one_hot, axis=-1)


def pack_rows(source, slot_ids, slot_total, spread):
    row_count = slot_ids.shape[0]
    owner_row = (
        jnp.zeros((slot_total,), jnp.int32)
        .at[slot_ids]
        .set(jnp.arange(row_count, dtype=jnp.int32) + 1)
    )
    filled = owner_row > 0
    picked = jnp.take(source, jnp.maximum(owner_row - 1, 0) // spread, axis=0)
    return jnp.where(filled[:, None], picked, jnp.zeros_like(picked))


def expert_forward(slot_rows, weights):
    hidden = jnp.einsum("nlcd,ldh->nlch", slot_rows, weights, preferred_element_type=jnp.float32)
    active = jax.nn.silu(hidden).astype(jnp.bfloat16)
    return jnp.einsum("nlch,ldh->nlcd", active, weights, preferred_element_type=jnp.float32).astype(
        jnp.bfloat16
    )


def expert_backward(saved_rows, slot_grads, weights):
    hidden = jnp.einsum("nlcd,ldh->nlch", saved_rows, weights, preferred_element_type=jnp.float32)
    active = jax.nn.silu(hidden).astype(jnp.bfloat16)
    active_grads = jnp.einsum(
        "nlcd,ldh->nlch", slot_grads, weights, preferred_element_type=jnp.float32
    )
    sigma = jax.nn.sigmoid(hidden)
    hidden_grads = (active_grads * sigma * (1.0 + hidden * (1.0 - sigma))).astype(jnp.bfloat16)
    row_grads = jnp.einsum(
        "nlch,ldh->nlcd", hidden_grads, weights, preferred_element_type=jnp.float32
    ).astype(jnp.bfloat16)
    weight_part = jnp.einsum(
        "nlcd,nlch->ldh", saved_rows, hidden_grads, preferred_element_type=jnp.float32
    )
    weight_part = weight_part + jnp.einsum(
        "nlcd,nlch->ldh", slot_grads, active, preferred_element_type=jnp.float32
    )
    return (row_grads, weight_part)


def packed_plan(
    section_inputs,
    saved_inputs,
    output_grads,
    forward_routes,
    backward_routes,
    forward_gates,
    backward_gates,
    expert_weights,
):
    token_count = section_inputs.shape[1]
    route_count = forward_routes.shape[2]
    local_count = expert_weights.shape[1]
    model_width = expert_weights.shape[2]
    groups = lax.axis_size("expert")
    experts = groups * local_count
    slot_total = experts * CAP
    block_shape = (groups, local_count, CAP, model_width)
    weights = expert_weights[0]
    forward_slot = slot_index(forward_routes[0].reshape(-1), experts, CAP)
    backward_slot = slot_index(backward_routes[0].reshape(-1), experts, CAP)
    forward_rows = pack_rows(section_inputs[0], forward_slot, slot_total, route_count).reshape(
        block_shape
    )
    saved_rows = pack_rows(saved_inputs[0], backward_slot, slot_total, route_count).reshape(
        block_shape
    )
    grad_block = output_grads[0]
    scaled = backward_gates[0][:, :, None] * grad_block.astype(jnp.float32)[:, None, :]
    scaled = scaled.astype(jnp.bfloat16).reshape(token_count * route_count, model_width)
    slot_grads = pack_rows(scaled, backward_slot, slot_total, 1).reshape(block_shape)
    forward_back = lax.all_to_all(
        expert_forward(
            lax.all_to_all(forward_rows, "expert", split_axis=0, concat_axis=0, tiled=True), weights
        ),
        "expert",
        split_axis=0,
        concat_axis=0,
        tiled=True,
    )
    saved_recv, grads_recv = (
        lax.all_to_all(saved_rows, "expert", split_axis=0, concat_axis=0, tiled=True),
        lax.all_to_all(slot_grads, "expert", split_axis=0, concat_axis=0, tiled=True),
    )
    row_grads, weight_part = expert_backward(saved_recv, grads_recv, weights)
    grads_back = lax.all_to_all(row_grads, "expert", split_axis=0, concat_axis=0, tiled=True)
    forward_pick = jnp.take(forward_back.reshape(slot_total, model_width), forward_slot, axis=0)
    forward_pick = forward_pick.reshape(token_count, route_count, model_width).astype(jnp.float32)
    layer_out = section_inputs[0].astype(jnp.float32) + jnp.sum(
        forward_gates[0][:, :, None] * forward_pick, axis=1
    )
    layer_out = layer_out.astype(jnp.bfloat16)
    grads_pick = jnp.take(grads_back.reshape(slot_total, model_width), backward_slot, axis=0)
    grads_pick = grads_pick.reshape(token_count, route_count, model_width).astype(jnp.float32)
    input_grads = (grad_block.astype(jnp.float32) + jnp.sum(grads_pick, axis=1)).astype(
        jnp.bfloat16
    )
    next_inputs = shifted(layer_out, "pipe", 1)[None]
    prior_grads = shifted(input_grads, "pipe", -1)[None]
    weight_grads = lax.psum_scatter(
        weight_part.astype(jnp.bfloat16), "dp", scatter_dimension=1, tiled=True
    )[None]
    return (next_inputs, prior_grads, weight_grads)


def swapped(value, code):
    axes = ("expert", "dp")
    count = lax.axis_size(axes[0]) * lax.axis_size(axes[1])
    return lax.ppermute(value, axes, [(source, source ^ code) for source in range(count)])


def pack_kernel(*refs):
    sources, out_ref, (*held, notes, done) = refs[:7], refs[7], refs[8:]
    size, width = sources[0].shape
    top = sources[3].shape[0]
    targets = [out_ref.at[:, pl.ds(place * width, width)] for place in range(3)] + held
    copies = [
        pltpu.make_async_copy(source, target, done.at[place])
        for place, (source, target) in enumerate(zip(sources, targets))
    ]
    for copy in copies:
        copy.start()
    for copy in copies:
        copy.wait()
    back_routes, back_gates, fore_routes, fore_gates = held
    notes[...] = jnp.zeros_like(notes)
    for place, (routes, gates) in enumerate(((back_routes, back_gates), (fore_routes, fore_gates))):
        first = place * 4 * top
        notes[pl.ds(first, top), 0:size] = routes[...].astype(jnp.float32)
        rest = gates[...]
        for term in range(1, 4):
            part = rest.astype(jnp.bfloat16).astype(jnp.float32)
            notes[pl.ds(first + term * top, top), 0:size] = part
            rest = rest - part
    out_ref[:, pl.ds(3 * width, LANES)] = notes[...].T[:size, :].astype(jnp.bfloat16)


def picks_kernel(count, top, slots, devices, place_ref, *refs):
    blocks, outs, (notes, turned) = refs[:devices], refs[devices:-2], refs[-2:]
    tokens = notes.shape[0]
    for code, block in enumerate(blocks):
        size = block.shape[0]
        rows = pl.ds(pl.multiple_of(place_ref[3 + code], size), size)
        notes[rows, :] = block[...].astype(jnp.float32)
    turned[...] = notes[...].T
    row = lax.broadcasted_iota(jnp.int32, (tokens, tokens), 0)
    column = lax.broadcasted_iota(jnp.int32, (tokens, tokens), 1)
    earlier = jnp.where(row < column, 1.0, 0.0).astype(jnp.bfloat16)
    slot = lax.broadcasted_iota(jnp.int32, (slots, tokens), 0).astype(jnp.float32)

    def find(first, start):
        ids = (first + lax.broadcasted_iota(jnp.int32, (count, tokens), 0)).astype(jnp.float32)
        named = jnp.zeros((count, tokens), jnp.float32)
        gated = jnp.zeros((count, tokens), jnp.float32)
        for column in range(start, start + top):
            same = turned[column : column + 1, :] == ids
            terms = [turned[column + term * top : column + term * top + 1, :] for term in (1, 2, 3)]
            named = named + jnp.where(same, 1.0, 0.0)
            gated = gated + jnp.where(same, terms[0] + terms[1] + terms[2], 0.0)
        place = jnp.dot(named.astype(jnp.bfloat16), earlier, preferred_element_type=jnp.float32)
        return jnp.where(named > 0.0, place, -1.0), gated

    def fill(place, gated, picks, gates, flipped):
        for expert in range(count):
            rows = pl.ds(expert * slots, slots)
            hit = place[expert : expert + 1, :] == slot
            picks[rows, :] = jnp.where(hit, 1.0, 0.0).astype(jnp.bfloat16)
            own = jnp.sum(jnp.where(hit, gated[expert : expert + 1, :], 0.0), axis=1, keepdims=True)
            gates[rows, :] = jnp.broadcast_to(own, (slots, LANES))
        flipped[...] = picks[...].T

    places, gated = find(place_ref[1], 4 * top)
    fill(places, gated, outs[0], outs[1], outs[2])
    places, gated = find(place_ref[1], 0)
    fill(places, gated, outs[3], outs[4], outs[5])
    other_places, other_gated = find(place_ref[2], 0)
    turned[...] = jnp.zeros_like(turned)
    for row, value in enumerate((places, other_places, gated, other_gated)):
        turned[pl.ds(row * count, count), :] = value
    outs[6][...] = turned[...].T


def spread_gate(gates, rows, width):
    gate = gates[rows, 0:1]
    return jnp.broadcast_to(gate, (gate.shape[0], width))


def assemble(place_ref, blocks, columns, tokens):
    for code, block in enumerate(blocks):
        size = block.shape[0]
        rows = pl.ds(pl.multiple_of(place_ref[3 + code], size), size)
        tokens[rows, :] = block[:, columns]


def combine(flipped, results, sums):
    width = sums.shape[1]
    for start in range(0, width, CHUNK):
        columns = pl.ds(start, CHUNK)
        sums[:, columns] = jnp.dot(
            flipped[...], results[:, columns], preferred_element_type=jnp.float32
        ).astype(sums.dtype)


def gather(count, slots, picks, gates, tokens_ref, rows, first, stride):
    width = tokens_ref.shape[1]
    for start in range(0, width, CHUNK):
        columns = pl.ds(start, CHUNK)
        taken = jnp.dot(picks[...], tokens_ref[:, columns], preferred_element_type=jnp.float32)
        if gates is not None:
            taken = taken * spread_gate(gates, pl.ds(0, count * slots), CHUNK)
        taken = taken.astype(rows.dtype)
        for expert in range(count):
            part = slice(expert * slots, (expert + 1) * slots)
            rows[pl.ds(first + expert * stride, slots), columns] = taken[part]


def expert_kernel(count, slots, devices, pair, place_ref, *refs):
    fore_picks, fore_gates, fore_flip, back_picks, back_gates, back_flip = refs[:6]
    weights, blocks = refs[6 : 6 + WEIGHT_CUTS], refs[6 + WEIGHT_CUTS :][:devices]
    groups = devices // pair
    outs = refs[6 + WEIGHT_CUTS + devices :][: 2 * groups + 2]
    inner, turned, *scratch = refs[8 + WEIGHT_CUTS + devices + 2 * groups :]
    tokens, (rows, fore_results, back_results, second) = scratch[:3], scratch[3:]
    total, width = tokens[0].shape
    step = pl.program_id(0)

    @pl.when(step == 0)
    def _():
        taken = ((fore_picks, None), (back_picks, None), (back_picks, back_gates))
        for place, (picks, gates) in enumerate(taken):
            assemble(place_ref, blocks, pl.ds(place * width, width), tokens[place])
            gather(count, slots, picks, gates, tokens[place], rows, place * slots, 3 * slots)

    mine = pl.ds(pl.multiple_of(step * slots, slots), slots)
    three = pl.ds(pl.multiple_of(step * 3 * slots, 3 * slots), 3 * slots)
    cut = width // WEIGHT_CUTS
    for start in range(0, inner.shape[2], CHUNK):
        lanes = pl.ds(start, CHUNK)
        product = functools.reduce(
            jnp.add,
            [
                jnp.dot(
                    rows[three, pl.ds(place * cut, cut)],
                    weight[0, :, lanes],
                    preferred_element_type=jnp.float32,
                )
                for place, weight in enumerate(weights)
            ],
        )
        ahead, hidden, active_grads = (
            product[:slots],
            product[slots : 2 * slots],
            product[2 * slots :],
        )
        sigma = jax.nn.sigmoid(hidden)
        hidden_grads = (active_grads * sigma * (1.0 + hidden * (1.0 - sigma))).astype(jnp.bfloat16)
        inner[0, :slots, lanes] = hidden_grads
        inner[0, slots:, lanes] = (hidden * sigma).astype(jnp.bfloat16)
        gate = spread_gate(fore_gates, mine, CHUNK)
        second[:slots, lanes] = (ahead * jax.nn.sigmoid(ahead) * gate).astype(jnp.bfloat16)
        second[slots:, lanes] = hidden_grads
    for start in range(0, width, CHUNK):
        columns = pl.ds(start, CHUNK)
        result = lax.dot_general(
            second[...],
            weights[start // cut][0, pl.ds(start % cut, CHUNK), :],
            (((1,), (1,)), ((), ())),
            preferred_element_type=jnp.float32,
        ).astype(fore_results.dtype)
        fore_results[mine, columns] = result[:slots]
        back_results[mine, columns] = result[slots:]

    span = turned.shape[0]
    first = place_ref[0] * (width // pair) + step * span
    for place in range(2):
        some = tokens[1 + place][:, pl.ds(pl.multiple_of(first, LANES), span)]
        turned[:, pl.ds(place * total, total)] = some.T

    @pl.when(step == count - 1)
    def _():
        for lead, (flipped, results) in enumerate(
            ((fore_flip, fore_results), (back_flip, back_results))
        ):
            sums = tokens[lead]
            combine(flipped, results, sums)
            *near_outs, far_out = outs[lead * (groups + 1) : (lead + 1) * (groups + 1)]
            size = far_out.shape[1]
            for group, out in enumerate(near_outs):
                near, far = (
                    pl.ds(pl.multiple_of(place_ref[3 + pair * group + code], size), size)
                    for code in range(pair)
                )
                out[...] = sums[near, :]
                far_out[group] = sums[far, :]


def weight_kernel(whose, first, number, count, slots, place_ref, *refs):
    columns, inner, turned = refs[:3]
    out_ref, picks, rows, staged, out_done = refs[-5:]
    total, half = columns.shape[0], turned.shape[0]
    side = place_ref[0]
    owner = side if whose == 0 else 1 - side
    lane = lax.broadcasted_iota(jnp.int32, (total, LANES), 1).astype(jnp.float32)
    is_saved = lax.broadcasted_iota(jnp.int32, (1, LANES), 1) < slots
    scales = []
    for step in range(number):
        column = whose * count + first + step
        slot = jnp.broadcast_to(columns[:, column : column + 1], (total, LANES))
        column += 2 * count
        gate = jnp.broadcast_to(columns[:, column : column + 1], (total, LANES))
        saved, grads = slot == lane, slot == lane - slots
        lanes = pl.ds(step * LANES, LANES)
        picks[pl.ds(0, total), lanes] = jnp.where(saved, 1.0, 0.0).astype(picks.dtype)
        picks[pl.ds(total, total), lanes] = jnp.where(
            jnp.logical_and(grads, lane >= slots), 1.0, 0.0
        ).astype(picks.dtype)
        scale = jnp.sum(jnp.where(grads, gate, 0.0), axis=0, keepdims=True)
        scales.append(jnp.where(is_saved, 1.0, scale))
    for step in range(0, number, 2):
        lanes = pl.ds(step * LANES, 2 * LANES)
        scale = jnp.concatenate(scales[step : step + 2], axis=1)
        rows[:, lanes] = (
            jnp.dot(turned[...], picks[:, lanes], preferred_element_type=jnp.float32) * scale
        ).astype(rows.dtype)

    leaving = []
    for step in range(number):
        for start in range(0, half, CHUNK):
            chunk = pl.ds(start, CHUNK)
            for corner in range(start, start + CHUNK, LANES):
                for column in range(0, inner.shape[2], CHUNK):
                    tile = (step, pl.ds(corner, LANES), pl.ds(column, CHUNK))
                    staged[tile] = jnp.dot(
                        rows[tile[1], pl.ds(step * LANES, 2 * slots)],
                        inner[first + step, :, tile[2]],
                        preferred_element_type=jnp.float32,
                    ).astype(staged.dtype)
            leaving.append(
                pltpu.make_async_copy(
                    staged.at[step, chunk, :],
                    out_ref.at[owner * count + first + step, chunk, :],
                    out_done.at[step, start // CHUNK],
                )
            )
            leaving[-1].start()
    for copy in leaving:
        copy.wait()


def gathered_plan(
    section_inputs,
    saved_inputs,
    output_grads,
    forward_routes,
    backward_routes,
    forward_gates,
    backward_gates,
    expert_weights,
):
    token_count = section_inputs.shape[1]
    top = forward_routes.shape[2]
    _, local_count, width, inner_width = expert_weights.shape
    groups, pair = lax.axis_size("expert"), lax.axis_size("dp")
    devices = groups * pair
    count = local_count // pair
    total = devices * token_count
    slots = -(-devices * CAP // 16) * 16
    rows = count * slots
    half = width // pair
    weights = expert_weights[0]

    side, group = lax.axis_index("dp"), lax.axis_index("expert")
    index = group * pair + side
    base = group * local_count
    place = jnp.stack(
        [side, base + side * count, base + (1 - side) * count]
        + [(index ^ code) * token_count for code in range(devices)]
    ).astype(jnp.int32)
    params = pltpu.CompilerParams(vmem_limit_bytes=VMEM_LIMIT, dimension_semantics=("arbitrary",))

    def whole(shape):
        return pl.BlockSpec(shape, lambda *_: (0,) * len(shape))

    def call(kernel, name, steps, in_specs, out_specs, out_shape, scratch, flops=0, aliases=()):
        return pl.pallas_call(
            kernel,
            grid_spec=pltpu.PrefetchScalarGridSpec(
                num_scalar_prefetch=1,
                grid=(steps,),
                in_specs=in_specs,
                out_specs=out_specs,
                scratch_shapes=scratch,
            ),
            out_shape=out_shape,
            compiler_params=params,
            cost_estimate=pl.CostEstimate(
                flops=flops, bytes_accessed=flops // 512 + 1024, transcendentals=0
            ),
            input_output_aliases=dict(aliases),
            name=name,
        )

    def onward(block):
        return swapped(block, 1)

    def across(parts):
        return [swapped(part, code) for part, code in zip(parts, range(pair, devices, pair))]

    def after(first, then):
        then, _ = lax.optimization_barrier((then, first))
        return then

    def summed(*blocks):
        return functools.reduce(jnp.add, [block.astype(jnp.float32) for block in blocks])

    packed = jax.ShapeDtypeStruct((token_count, 3 * width + LANES), jnp.bfloat16)
    own = pl.pallas_call(
        pack_kernel,
        in_specs=[pl.BlockSpec(memory_space=pl.ANY)] * 7,
        out_specs=pl.BlockSpec(memory_space=pltpu.VMEM),
        out_shape=packed,
        scratch_shapes=[
            pltpu.VMEM((top, token_count), jnp.int32),
            pltpu.VMEM((top, token_count), jnp.float32),
            pltpu.VMEM((top, token_count), jnp.int32),
            pltpu.VMEM((top, token_count), jnp.float32),
            pltpu.VMEM((LANES, LANES), jnp.float32),
            pltpu.SemaphoreType.DMA((7,)),
        ],
        compiler_params=pltpu.CompilerParams(vmem_limit_bytes=VMEM_LIMIT),
        name="pack",
    )(
        *[
            pltpu.with_memory_space_constraint(array, pltpu.HBM)
            for array in (
                section_inputs[0],
                saved_inputs[0],
                output_grads[0],
                backward_routes[0].T,
                backward_gates[0].T,
                forward_routes[0].T,
                forward_gates[0].T,
            )
        ]
    )
    near = [own] + across([own] * (groups - 1))
    blocks = [block for one in near for block in (one, onward(one))]

    pick = jax.ShapeDtypeStruct((rows, total), jnp.bfloat16)
    flip = jax.ShapeDtypeStruct((total, rows), jnp.bfloat16)
    gate = jax.ShapeDtypeStruct((rows, LANES), jnp.float32)
    columns = jax.ShapeDtypeStruct((total, LANES), jnp.float32)
    pick_outs = [pick, gate, flip, pick, gate, flip, columns]
    picks = call(
        functools.partial(picks_kernel, count, top, slots, devices),
        "slot_picks",
        1,
        [pl.BlockSpec((token_count, LANES), lambda *_: (0, 3 * width // LANES))] * devices,
        [whole(out.shape) for out in pick_outs],
        pick_outs,
        [pltpu.VMEM((total, LANES), jnp.float32), pltpu.VMEM((LANES, total), jnp.float32)],
    )(place, *blocks)

    pass_flops = 2 * 2 * count * CHUNK * width * inner_width
    near_part = jax.ShapeDtypeStruct((token_count, width), jnp.bfloat16)
    far_part = jax.ShapeDtypeStruct((groups, token_count, width), jnp.bfloat16)
    inner = jax.ShapeDtypeStruct((count, 2 * slots, inner_width), jnp.bfloat16)
    turned = jax.ShapeDtypeStruct((half, 2 * total), jnp.bfloat16)
    in_smem, in_vmem, anywhere = (
        pl.BlockSpec(memory_space=space) for space in (pltpu.SMEM, pltpu.VMEM, pl.ANY)
    )
    tokens = pltpu.VMEM((total, width), jnp.bfloat16)
    cut = width // WEIGHT_CUTS
    *parts, inner_own, tokens_turned = pl.pallas_call(
        functools.partial(expert_kernel, count, slots, devices, pair),
        grid_spec=pltpu.PrefetchScalarGridSpec(
            num_scalar_prefetch=1,
            grid=(count,),
            in_specs=[whole(array.shape) for array in pick_outs[:6]]
            + [
                pl.BlockSpec(
                    (1, cut, inner_width),
                    lambda step, place, part=part: (place[0] * count + step, part, 0),
                )
                for part in range(WEIGHT_CUTS)
            ]
            + [whole(packed.shape)] * devices,
            out_specs=([whole(near_part.shape)] * groups + [whole(far_part.shape)]) * 2
            + [
                pl.BlockSpec((1, 2 * slots, inner_width), lambda step, place: (step, 0, 0)),
                pl.BlockSpec((half // count, 2 * total), lambda step, place: (step, 0)),
            ],
            scratch_shapes=[tokens] * 3
            + [
                pltpu.VMEM((3 * rows, width), jnp.bfloat16),
                pltpu.VMEM((rows, width), jnp.bfloat16),
                pltpu.VMEM((rows, width), jnp.bfloat16),
                pltpu.VMEM((2 * slots, inner_width), jnp.bfloat16),
            ],
        ),
        out_shape=([near_part] * groups + [far_part]) * 2 + [inner, turned],
        compiler_params=pltpu.CompilerParams(
            vmem_limit_bytes=EXPERTS_LIMIT, dimension_semantics=("arbitrary",)
        ),
        cost_estimate=pl.CostEstimate(
            flops=pass_flops, bytes_accessed=pass_flops // 512, transcendentals=0
        ),
        name="experts",
    )(place, *picks[:6], *[weights] * WEIGHT_CUTS, *blocks)
    *layer_parts, layer_far = parts[: groups + 1]
    *grad_parts, grad_far = parts[groups + 1 :]
    layer_far, grad_far, inner_other = onward(layer_far), onward(grad_far), onward(inner_own)

    def gradient(whose, first, number, inner_rows, earlier):
        earlier = [] if earlier is None else [earlier]
        operands = [picks[6], inner_rows, tokens_turned] + earlier
        return pl.pallas_call(
            functools.partial(weight_kernel, whose, first, number, count, slots),
            in_specs=[in_smem, in_vmem, in_vmem, in_vmem] + [anywhere] * len(earlier),
            out_specs=anywhere,
            out_shape=jax.ShapeDtypeStruct((local_count, half, inner_width), jnp.bfloat16),
            scratch_shapes=[
                pltpu.VMEM((2 * total, number * LANES), jnp.bfloat16),
                pltpu.VMEM((half, number * LANES), jnp.bfloat16),
                pltpu.VMEM((number, half, inner_width), jnp.bfloat16),
                pltpu.SemaphoreType.DMA((number, half // CHUNK)),
            ],
            compiler_params=pltpu.CompilerParams(vmem_limit_bytes=VMEM_LIMIT),
            cost_estimate=pl.CostEstimate(
                flops=number * pass_flops // count // 2,
                bytes_accessed=number * half * inner_width * 4,
                transcendentals=0,
            ),
            input_output_aliases={len(operands): 0} if earlier else {},
            name=f"weight_gradient_{whose}_{first}",
        )(place, *operands)

    def pair_sums(near_parts, far):
        return [summed(part, far[group]).astype(jnp.bfloat16) for group, part in enumerate(near_parts)]

    piece = -(-count // 2)
    done = gradient(0, 0, piece, inner_own, None)
    layer_sums = pair_sums(layer_parts, after(done, layer_far))
    layer_near = across(layer_sums[1:])
    grad_sums = pair_sums(grad_parts, after((layer_sums, inner_other), grad_far))
    grad_near = across(grad_sums[1:])
    done = after(grad_sums, done)
    if piece < count:
        done = gradient(0, piece, count - piece, inner_own, done)
    done = gradient(1, 0, piece, inner_other, after(layer_near[0], done))
    layer_near = after(done, layer_near)
    layer_out = summed(section_inputs[0], layer_sums[0], *layer_near).astype(jnp.bfloat16)
    next_inputs = shifted(layer_out, "pipe", 1)[None]
    done = after(layer_out, done)
    if piece < count:
        done = gradient(1, piece, count - piece, inner_other, done)
    grad_near = after((done, next_inputs), grad_near)
    input_grads = summed(output_grads[0], grad_sums[0], *grad_near).astype(jnp.bfloat16)
    prior_grads = shifted(input_grads, "pipe", -1)[None]
    return (next_inputs, prior_grads, done[None])


def on_device(*arrays):
    token_count = arrays[0].shape[1]
    local_count = arrays[-1].shape[1]
    groups, pair = lax.axis_size("expert"), lax.axis_size("dp")
    gathered = groups * token_count
    packed = groups * local_count * CAP
    paired = pair == 2 and local_count % 8 == 0 and groups & (groups - 1) == 0
    if gathered <= packed and paired and gathered * pair % LANES == 0:
        return gathered_plan(*arrays)
    return packed_plan(*arrays)


def solution(mesh):
    placed = (
        P("pipe", ("expert", "dp"), None),
        P("pipe", ("expert", "dp"), None),
        P("pipe", ("expert", "dp"), None),
        P("pipe", ("expert", "dp"), None),
        P("pipe", ("expert", "dp"), None),
        P("pipe", ("expert", "dp"), None),
        P("pipe", ("expert", "dp"), None),
        P("pipe", "expert", None, None),
    )
    return jax.shard_map(
        on_device,
        mesh=mesh,
        in_specs=placed,
        out_specs=(
            P("pipe", ("expert", "dp"), None),
            P("pipe", ("expert", "dp"), None),
            P("pipe", "expert", "dp", None),
        ),
        check_vma=False,
    )
```

```python
import functools

import jax
import jax.numpy as jnp
from jax import lax
from jax.experimental import pallas as pl
from jax.experimental.pallas import tpu as pltpu
from jax.sharding import PartitionSpec as P

CAP = 5
LANES = 128
CHUNK = 256
VMEM_LIMIT = 24 * 1024 * 1024
EXPERTS_LIMIT = 40 * 1024 * 1024
WEIGHT_CUTS = 4


def shifted(value, axis, steps):
    count = lax.axis_size(axis)
    pairs = [(source, (source + steps) % count) for source in range(count)]
    return lax.ppermute(value, axis, pairs)


def slot_index(routing, experts, capacity):
    one_hot = (routing[..., None] == jnp.arange(experts, dtype=jnp.int32)).astype(jnp.int32)
    before = jnp.cumsum(one_hot, axis=-2) - one_hot
    return routing * capacity + jnp.sum(before * one_hot, axis=-1)


def pack_rows(source, slot_ids, slot_total, spread):
    row_count = slot_ids.shape[0]
    owner_row = (
        jnp.zeros((slot_total,), jnp.int32)
        .at[slot_ids]
        .set(jnp.arange(row_count, dtype=jnp.int32) + 1)
    )
    filled = owner_row > 0
    picked = jnp.take(source, jnp.maximum(owner_row - 1, 0) // spread, axis=0)
    return jnp.where(filled[:, None], picked, jnp.zeros_like(picked))


def expert_forward(slot_rows, weights):
    hidden = jnp.einsum("nlcd,ldh->nlch", slot_rows, weights, preferred_element_type=jnp.float32)
    active = jax.nn.silu(hidden).astype(jnp.bfloat16)
    return jnp.einsum("nlch,ldh->nlcd", active, weights, preferred_element_type=jnp.float32).astype(
        jnp.bfloat16
    )


def expert_backward(saved_rows, slot_grads, weights):
    hidden = jnp.einsum("nlcd,ldh->nlch", saved_rows, weights, preferred_element_type=jnp.float32)
    active = jax.nn.silu(hidden).astype(jnp.bfloat16)
    active_grads = jnp.einsum(
        "nlcd,ldh->nlch", slot_grads, weights, preferred_element_type=jnp.float32
    )
    sigma = jax.nn.sigmoid(hidden)
    hidden_grads = (active_grads * sigma * (1.0 + hidden * (1.0 - sigma))).astype(jnp.bfloat16)
    row_grads = jnp.einsum(
        "nlch,ldh->nlcd", hidden_grads, weights, preferred_element_type=jnp.float32
    ).astype(jnp.bfloat16)
    weight_part = jnp.einsum(
        "nlcd,nlch->ldh", saved_rows, hidden_grads, preferred_element_type=jnp.float32
    )
    weight_part = weight_part + jnp.einsum(
        "nlcd,nlch->ldh", slot_grads, active, preferred_element_type=jnp.float32
    )
    return (row_grads, weight_part)


def packed_plan(
    section_inputs,
    saved_inputs,
    output_grads,
    forward_routes,
    backward_routes,
    forward_gates,
    backward_gates,
    expert_weights,
):
    token_count = section_inputs.shape[1]
    route_count = forward_routes.shape[2]
    local_count = expert_weights.shape[1]
    model_width = expert_weights.shape[2]
    groups = lax.axis_size("expert")
    experts = groups * local_count
    slot_total = experts * CAP
    block_shape = (groups, local_count, CAP, model_width)
    weights = expert_weights[0]
    forward_slot = slot_index(forward_routes[0].reshape(-1), experts, CAP)
    backward_slot = slot_index(backward_routes[0].reshape(-1), experts, CAP)
    forward_rows = pack_rows(section_inputs[0], forward_slot, slot_total, route_count).reshape(
        block_shape
    )
    saved_rows = pack_rows(saved_inputs[0], backward_slot, slot_total, route_count).reshape(
        block_shape
    )
    grad_block = output_grads[0]
    scaled = backward_gates[0][:, :, None] * grad_block.astype(jnp.float32)[:, None, :]
    scaled = scaled.astype(jnp.bfloat16).reshape(token_count * route_count, model_width)
    slot_grads = pack_rows(scaled, backward_slot, slot_total, 1).reshape(block_shape)
    forward_back = lax.all_to_all(
        expert_forward(
            lax.all_to_all(forward_rows, "expert", split_axis=0, concat_axis=0, tiled=True), weights
        ),
        "expert",
        split_axis=0,
        concat_axis=0,
        tiled=True,
    )
    saved_recv, grads_recv = (
        lax.all_to_all(saved_rows, "expert", split_axis=0, concat_axis=0, tiled=True),
        lax.all_to_all(slot_grads, "expert", split_axis=0, concat_axis=0, tiled=True),
    )
    row_grads, weight_part = expert_backward(saved_recv, grads_recv, weights)
    grads_back = lax.all_to_all(row_grads, "expert", split_axis=0, concat_axis=0, tiled=True)
    forward_pick = jnp.take(forward_back.reshape(slot_total, model_width), forward_slot, axis=0)
    forward_pick = forward_pick.reshape(token_count, route_count, model_width).astype(jnp.float32)
    layer_out = section_inputs[0].astype(jnp.float32) + jnp.sum(
        forward_gates[0][:, :, None] * forward_pick, axis=1
    )
    layer_out = layer_out.astype(jnp.bfloat16)
    grads_pick = jnp.take(grads_back.reshape(slot_total, model_width), backward_slot, axis=0)
    grads_pick = grads_pick.reshape(token_count, route_count, model_width).astype(jnp.float32)
    input_grads = (grad_block.astype(jnp.float32) + jnp.sum(grads_pick, axis=1)).astype(
        jnp.bfloat16
    )
    next_inputs = shifted(layer_out, "pipe", 1)[None]
    prior_grads = shifted(input_grads, "pipe", -1)[None]
    weight_grads = lax.psum_scatter(
        weight_part.astype(jnp.bfloat16), "dp", scatter_dimension=1, tiled=True
    )[None]
    return (next_inputs, prior_grads, weight_grads)


def swapped(value, code):
    axes = ("expert", "dp")
    count = lax.axis_size(axes[0]) * lax.axis_size(axes[1])
    return lax.ppermute(value, axes, [(source, source ^ code) for source in range(count)])


def pack_kernel(*refs):
    sources, (one, two), (*held, notes, done) = list(refs[:7]), refs[7:9], refs[9:]
    size, width = sources[0].shape
    half = width // 2
    top = sources[3].shape[0]
    targets = [one.at[:, pl.ds(0, width)], one.at[:, pl.ds(width, half)]]
    targets += [two.at[:, pl.ds(0, half)], two.at[:, pl.ds(half, width)]] + held
    sources[1:2] = [sources[1].at[:, pl.ds(0, half)], sources[1].at[:, pl.ds(half, half)]]
    copies = [
        pltpu.make_async_copy(source, target, done.at[place])
        for place, (source, target) in enumerate(zip(sources, targets))
    ]
    for copy in copies:
        copy.start()
    for copy in copies:
        copy.wait()
    back_routes, back_gates, fore_routes, fore_gates = held
    notes[...] = jnp.zeros_like(notes)
    for place, (routes, gates) in enumerate(((back_routes, back_gates), (fore_routes, fore_gates))):
        first = place * 4 * top
        notes[pl.ds(first, top), 0:size] = routes[...].astype(jnp.float32)
        rest = gates[...]
        for term in range(1, 4):
            part = rest.astype(jnp.bfloat16).astype(jnp.float32)
            notes[pl.ds(first + term * top, top), 0:size] = part
            rest = rest - part
    one[:, pl.ds(width + half, LANES)] = notes[...].T[:size, :].astype(jnp.bfloat16)


def picks_kernel(count, top, slots, devices, place_ref, *refs):
    blocks, outs, (notes, turned) = refs[:devices], refs[devices:-2], refs[-2:]
    tokens = notes.shape[0]
    for code, block in enumerate(blocks):
        size = block.shape[0]
        rows = pl.ds(pl.multiple_of(place_ref[3 + code], size), size)
        notes[rows, :] = block[...].astype(jnp.float32)
    turned[...] = notes[...].T
    row = lax.broadcasted_iota(jnp.int32, (tokens, tokens), 0)
    column = lax.broadcasted_iota(jnp.int32, (tokens, tokens), 1)
    earlier = jnp.where(row < column, 1.0, 0.0).astype(jnp.bfloat16)
    slot = lax.broadcasted_iota(jnp.int32, (slots, tokens), 0).astype(jnp.float32)

    def find(first, start):
        ids = (first + lax.broadcasted_iota(jnp.int32, (count, tokens), 0)).astype(jnp.float32)
        named = jnp.zeros((count, tokens), jnp.float32)
        gated = jnp.zeros((count, tokens), jnp.float32)
        for column in range(start, start + top):
            same = turned[column : column + 1, :] == ids
            terms = [turned[column + term * top : column + term * top + 1, :] for term in (1, 2, 3)]
            named = named + jnp.where(same, 1.0, 0.0)
            gated = gated + jnp.where(same, terms[0] + terms[1] + terms[2], 0.0)
        place = jnp.dot(named.astype(jnp.bfloat16), earlier, preferred_element_type=jnp.float32)
        return jnp.where(named > 0.0, place, -1.0), gated

    def fill(place, gated, picks, gates, flipped):
        for expert in range(count):
            rows = pl.ds(expert * slots, slots)
            hit = place[expert : expert + 1, :] == slot
            picks[rows, :] = jnp.where(hit, 1.0, 0.0).astype(jnp.bfloat16)
            own = jnp.sum(jnp.where(hit, gated[expert : expert + 1, :], 0.0), axis=1, keepdims=True)
            gates[rows, :] = jnp.broadcast_to(own, (slots, LANES))
        flipped[...] = picks[...].T

    places, gated = find(place_ref[1], 4 * top)
    fill(places, gated, outs[0], outs[1], outs[2])
    places, gated = find(place_ref[1], 0)
    fill(places, gated, outs[3], outs[4], outs[5])
    other_places, other_gated = find(place_ref[2], 0)
    turned[...] = jnp.zeros_like(turned)
    for row, value in enumerate((places, other_places, gated, other_gated)):
        turned[pl.ds(row * count, count), :] = value
    outs[6][...] = turned[...].T


def spread_gate(gates, rows, width):
    gate = gates[rows, 0:1]
    return jnp.broadcast_to(gate, (gate.shape[0], width))


def assemble(place_ref, first, second, tokens):
    width = tokens[0].shape[1]
    half = width // 2
    for code, (one, two) in enumerate(zip(first, second)):
        size = one.shape[0]
        rows = pl.ds(pl.multiple_of(place_ref[3 + code], size), size)
        tokens[0][rows, :] = one[:, pl.ds(0, width)]
        tokens[1][rows, pl.ds(0, half)] = one[:, pl.ds(width, half)]
        tokens[1][rows, pl.ds(half, half)] = two[:, pl.ds(0, half)]
        tokens[2][rows, :] = two[:, pl.ds(half, width)]


def combine(flipped, results, sums):
    width = sums.shape[1]
    for start in range(0, width, CHUNK):
        columns = pl.ds(start, CHUNK)
        sums[:, columns] = jnp.dot(
            flipped[...], results[:, columns], preferred_element_type=jnp.float32
        ).astype(sums.dtype)


def gather(count, slots, picks, gates, tokens_ref, rows, first, stride):
    width = tokens_ref.shape[1]
    for start in range(0, width, CHUNK):
        columns = pl.ds(start, CHUNK)
        taken = jnp.dot(picks[...], tokens_ref[:, columns], preferred_element_type=jnp.float32)
        if gates is not None:
            taken = taken * spread_gate(gates, pl.ds(0, count * slots), CHUNK)
        taken = taken.astype(rows.dtype)
        for expert in range(count):
            part = slice(expert * slots, (expert + 1) * slots)
            rows[pl.ds(first + expert * stride, slots), columns] = taken[part]


def expert_kernel(count, slots, devices, pair, place_ref, *refs):
    fore_picks, fore_gates, fore_flip, back_picks, back_gates, back_flip = refs[:6]
    weights, blocks = refs[6 : 6 + WEIGHT_CUTS], refs[6 + WEIGHT_CUTS :][: 2 * devices]
    groups = devices // pair
    outs = refs[6 + WEIGHT_CUTS + 2 * devices :][: 2 * groups + 2]
    inner, turned, gradient, *scratch = refs[8 + WEIGHT_CUTS + 2 * devices + 2 * groups :]
    tokens, (rows, fore_results, back_results, second) = scratch[:3], scratch[3:]
    total, width = tokens[0].shape
    step = pl.program_id(0)

    @pl.when(step == 0)
    def _():
        taken = ((fore_picks, None), (back_picks, None), (back_picks, back_gates))
        assemble(place_ref, blocks[:devices], blocks[devices:], tokens)
        for place, (picks, gates) in enumerate(taken):
            gather(count, slots, picks, gates, tokens[place], rows, place * slots, 3 * slots)

    mine = pl.ds(pl.multiple_of(step * slots, slots), slots)
    three = pl.ds(pl.multiple_of(step * 3 * slots, 3 * slots), 3 * slots)
    cut = width // WEIGHT_CUTS
    for start in range(0, inner.shape[2], CHUNK):
        lanes = pl.ds(start, CHUNK)
        product = functools.reduce(
            jnp.add,
            [
                jnp.dot(
                    rows[three, pl.ds(place * cut, cut)],
                    weight[0, :, lanes],
                    preferred_element_type=jnp.float32,
                )
                for place, weight in enumerate(weights)
            ],
        )
        ahead, hidden, active_grads = (
            product[:slots],
            product[slots : 2 * slots],
            product[2 * slots :],
        )
        sigma = jax.nn.sigmoid(hidden)
        hidden_grads = (active_grads * sigma * (1.0 + hidden * (1.0 - sigma))).astype(jnp.bfloat16)
        inner[0, :slots, lanes] = hidden_grads
        inner[0, slots:, lanes] = (hidden * sigma).astype(jnp.bfloat16)
        gate = spread_gate(fore_gates, mine, CHUNK)
        second[:slots, lanes] = (ahead * jax.nn.sigmoid(ahead) * gate).astype(jnp.bfloat16)
        second[slots:, lanes] = hidden_grads
    for start in range(0, width, CHUNK):
        columns = pl.ds(start, CHUNK)
        result = lax.dot_general(
            second[...],
            weights[start // cut][0, pl.ds(start % cut, CHUNK), :],
            (((1,), (1,)), ((), ())),
            preferred_element_type=jnp.float32,
        ).astype(fore_results.dtype)
        fore_results[mine, columns] = result[:slots]
        back_results[mine, columns] = result[slots:]

    half = gradient.shape[1]
    two = pl.ds(pl.multiple_of(step * 3 * slots + slots, slots), 2 * slots)
    flat = rows[two, pl.ds(pl.multiple_of(place_ref[0] * half, LANES), half)].T
    for start in range(0, gradient.shape[2], CHUNK):
        columns = pl.ds(start, CHUNK)
        gradient[0, :, columns] = jnp.dot(
            flat, inner[0, :, columns], preferred_element_type=jnp.float32
        ).astype(gradient.dtype)

    span = turned.shape[0]
    first = place_ref[0] * half + step * span
    for place in range(2):
        some = tokens[1 + place][:, pl.ds(pl.multiple_of(first, LANES), span)]
        turned[:, pl.ds(place * total, total)] = some.T

    @pl.when(step == count - 1)
    def _():
        for lead, (flipped, results) in enumerate(
            ((fore_flip, fore_results), (back_flip, back_results))
        ):
            sums = tokens[lead]
            combine(flipped, results, sums)
            *near_outs, far_out = outs[lead * (groups + 1) : (lead + 1) * (groups + 1)]
            size = far_out.shape[1]
            for group, out in enumerate(near_outs):
                near, far = (
                    pl.ds(pl.multiple_of(place_ref[3 + pair * group + code], size), size)
                    for code in range(pair)
                )
                out[...] = sums[near, :]
                far_out[group] = sums[far, :]


def weight_kernel(first, number, count, slots, place_ref, *refs):
    columns, inner, turned = refs[:3]
    out_ref, picks, rows, staged, out_done = refs[-5:]
    total, half = columns.shape[0], turned.shape[0]
    owner = 1 - place_ref[0]
    lane = lax.broadcasted_iota(jnp.int32, (total, LANES), 1).astype(jnp.float32)
    is_saved = lax.broadcasted_iota(jnp.int32, (1, LANES), 1) < slots
    scales = []
    for step in range(number):
        column = count + first + step
        slot = jnp.broadcast_to(columns[:, column : column + 1], (total, LANES))
        column += 2 * count
        gate = jnp.broadcast_to(columns[:, column : column + 1], (total, LANES))
        saved, grads = slot == lane, slot == lane - slots
        lanes = pl.ds(step * LANES, LANES)
        picks[pl.ds(0, total), lanes] = jnp.where(saved, 1.0, 0.0).astype(picks.dtype)
        picks[pl.ds(total, total), lanes] = jnp.where(
            jnp.logical_and(grads, lane >= slots), 1.0, 0.0
        ).astype(picks.dtype)
        scale = jnp.sum(jnp.where(grads, gate, 0.0), axis=0, keepdims=True)
        scales.append(jnp.where(is_saved, 1.0, scale))
    for step in range(0, number, 2):
        lanes = pl.ds(step * LANES, 2 * LANES)
        scale = jnp.concatenate(scales[step : step + 2], axis=1)
        rows[:, lanes] = (
            jnp.dot(turned[...], picks[:, lanes], preferred_element_type=jnp.float32) * scale
        ).astype(rows.dtype)

    leaving = []
    for step in range(number):
        for start in range(0, half, CHUNK):
            chunk = pl.ds(start, CHUNK)
            for corner in range(start, start + CHUNK, LANES):
                for column in range(0, inner.shape[2], CHUNK):
                    tile = (step, pl.ds(corner, LANES), pl.ds(column, CHUNK))
                    staged[tile] = jnp.dot(
                        rows[tile[1], pl.ds(step * LANES, 2 * slots)],
                        inner[first + step, :, tile[2]],
                        preferred_element_type=jnp.float32,
                    ).astype(staged.dtype)
            leaving.append(
                pltpu.make_async_copy(
                    staged.at[step, chunk, :],
                    out_ref.at[owner * count + first + step, chunk, :],
                    out_done.at[step, start // CHUNK],
                )
            )
            leaving[-1].start()
    for copy in leaving:
        copy.wait()


def gathered_plan(
    section_inputs,
    saved_inputs,
    output_grads,
    forward_routes,
    backward_routes,
    forward_gates,
    backward_gates,
    expert_weights,
):
    token_count = section_inputs.shape[1]
    top = forward_routes.shape[2]
    _, local_count, width, inner_width = expert_weights.shape
    groups, pair = lax.axis_size("expert"), lax.axis_size("dp")
    devices = groups * pair
    count = local_count // pair
    total = devices * token_count
    slots = -(-devices * CAP // 16) * 16
    rows = count * slots
    half = width // pair
    weights = expert_weights[0]

    side, group = lax.axis_index("dp"), lax.axis_index("expert")
    index = group * pair + side
    base = group * local_count
    place = jnp.stack(
        [side, base + side * count, base + (1 - side) * count]
        + [(index ^ code) * token_count for code in range(devices)]
    ).astype(jnp.int32)
    params = pltpu.CompilerParams(vmem_limit_bytes=VMEM_LIMIT, dimension_semantics=("arbitrary",))

    def whole(shape):
        return pl.BlockSpec(shape, lambda *_: (0,) * len(shape))

    def call(kernel, name, steps, in_specs, out_specs, out_shape, scratch, flops=0, aliases=()):
        return pl.pallas_call(
            kernel,
            grid_spec=pltpu.PrefetchScalarGridSpec(
                num_scalar_prefetch=1,
                grid=(steps,),
                in_specs=in_specs,
                out_specs=out_specs,
                scratch_shapes=scratch,
            ),
            out_shape=out_shape,
            compiler_params=params,
            cost_estimate=pl.CostEstimate(
                flops=flops, bytes_accessed=flops // 512 + 1024, transcendentals=0
            ),
            input_output_aliases=dict(aliases),
            name=name,
        )

    def onward(block):
        return swapped(block, 1)

    def across(parts):
        return [swapped(part, code) for part, code in zip(parts, range(pair, devices, pair))]

    def after(first, then):
        then, _ = lax.optimization_barrier((then, first))
        return then

    def summed(*blocks):
        return functools.reduce(jnp.add, [block.astype(jnp.float32) for block in blocks])

    packed = [
        jax.ShapeDtypeStruct((token_count, 3 * width // 2 + extra), jnp.bfloat16)
        for extra in (LANES, 0)
    ]
    own = pl.pallas_call(
        pack_kernel,
        in_specs=[pl.BlockSpec(memory_space=pl.ANY)] * 7,
        out_specs=[pl.BlockSpec(memory_space=pltpu.VMEM)] * 2,
        out_shape=packed,
        scratch_shapes=[
            pltpu.VMEM((top, token_count), jnp.int32),
            pltpu.VMEM((top, token_count), jnp.float32),
            pltpu.VMEM((top, token_count), jnp.int32),
            pltpu.VMEM((top, token_count), jnp.float32),
            pltpu.VMEM((LANES, LANES), jnp.float32),
            pltpu.SemaphoreType.DMA((8,)),
        ],
        compiler_params=pltpu.CompilerParams(vmem_limit_bytes=VMEM_LIMIT),
        name="pack",
    )(
        *[
            pltpu.with_memory_space_constraint(array, pltpu.HBM)
            for array in (
                section_inputs[0],
                saved_inputs[0],
                output_grads[0],
                backward_routes[0].T,
                backward_gates[0].T,
                forward_routes[0].T,
                forward_gates[0].T,
            )
        ]
    )
    near = [[half_block] for half_block in own]
    code = pair
    while code < devices:
        near[0] += [swapped(block, code) for block in near[0]]
        near[1] += [swapped(block, devices // code) for block in near[1]]
        code *= 2
    bits = groups.bit_length() - 1
    near[1] = [
        near[1][int(f"{group:0{bits}b}"[::-1], 2) if bits else 0] for group in range(groups)
    ]
    blocks = [block for half_blocks in near for one in half_blocks for block in (one, onward(one))]

    pick = jax.ShapeDtypeStruct((rows, total), jnp.bfloat16)
    flip = jax.ShapeDtypeStruct((total, rows), jnp.bfloat16)
    gate = jax.ShapeDtypeStruct((rows, LANES), jnp.float32)
    columns = jax.ShapeDtypeStruct((total, LANES), jnp.float32)
    pick_outs = [pick, gate, flip, pick, gate, flip, columns]
    picks = call(
        functools.partial(picks_kernel, count, top, slots, devices),
        "slot_picks",
        1,
        [pl.BlockSpec((token_count, LANES), lambda *_: (0, 3 * width // 2 // LANES))] * devices,
        [whole(out.shape) for out in pick_outs],
        pick_outs,
        [pltpu.VMEM((total, LANES), jnp.float32), pltpu.VMEM((LANES, total), jnp.float32)],
    )(place, *blocks[:devices])

    pass_flops = 2 * 2 * count * CHUNK * width * inner_width
    near_part = jax.ShapeDtypeStruct((token_count, width), jnp.bfloat16)
    far_part = jax.ShapeDtypeStruct((groups, token_count, width), jnp.bfloat16)
    inner = jax.ShapeDtypeStruct((count, 2 * slots, inner_width), jnp.bfloat16)
    turned = jax.ShapeDtypeStruct((half, 2 * total), jnp.bfloat16)
    in_smem, in_vmem, anywhere = (
        pl.BlockSpec(memory_space=space) for space in (pltpu.SMEM, pltpu.VMEM, pl.ANY)
    )
    tokens = pltpu.VMEM((total, width), jnp.bfloat16)
    cut = width // WEIGHT_CUTS
    whole_gradient = jax.ShapeDtypeStruct((local_count, half, inner_width), jnp.bfloat16)
    *parts, inner_own, tokens_turned, done = pl.pallas_call(
        functools.partial(expert_kernel, count, slots, devices, pair),
        grid_spec=pltpu.PrefetchScalarGridSpec(
            num_scalar_prefetch=1,
            grid=(count,),
            in_specs=[whole(array.shape) for array in pick_outs[:6]]
            + [
                pl.BlockSpec(
                    (1, cut, inner_width),
                    lambda step, place, part=part: (place[0] * count + step, part, 0),
                )
                for part in range(WEIGHT_CUTS)
            ]
            + [whole(one.shape) for one in packed for _ in range(devices)],
            out_specs=([whole(near_part.shape)] * groups + [whole(far_part.shape)]) * 2
            + [
                pl.BlockSpec((1, 2 * slots, inner_width), lambda step, place: (step, 0, 0)),
                pl.BlockSpec((half // count, 2 * total), lambda step, place: (step, 0)),
                pl.BlockSpec(
                    (1, half, inner_width), lambda step, place: (place[0] * count + step, 0, 0)
                ),
            ],
            scratch_shapes=[tokens] * 3
            + [
                pltpu.VMEM((3 * rows, width), jnp.bfloat16),
                pltpu.VMEM((rows, width), jnp.bfloat16),
                pltpu.VMEM((rows, width), jnp.bfloat16),
                pltpu.VMEM((2 * slots, inner_width), jnp.bfloat16),
            ],
        ),
        out_shape=([near_part] * groups + [far_part]) * 2 + [inner, turned, whole_gradient],
        compiler_params=pltpu.CompilerParams(
            vmem_limit_bytes=EXPERTS_LIMIT, dimension_semantics=("arbitrary",)
        ),
        cost_estimate=pl.CostEstimate(
            flops=pass_flops, bytes_accessed=pass_flops // 512, transcendentals=0
        ),
        name="experts",
    )(place, *picks[:6], *[weights] * WEIGHT_CUTS, *blocks)
    *layer_parts, layer_far = parts[: groups + 1]
    *grad_parts, grad_far = parts[groups + 1 :]
    layer_far, grad_far, inner_other = onward(layer_far), onward(grad_far), onward(inner_own)

    def gradient(first, number, earlier):
        operands = [picks[6], inner_other, tokens_turned, earlier]
        return pl.pallas_call(
            functools.partial(weight_kernel, first, number, count, slots),
            in_specs=[in_smem, in_vmem, in_vmem, in_vmem, anywhere],
            out_specs=anywhere,
            out_shape=whole_gradient,
            scratch_shapes=[
                pltpu.VMEM((2 * total, number * LANES), jnp.bfloat16),
                pltpu.VMEM((half, number * LANES), jnp.bfloat16),
                pltpu.VMEM((number, half, inner_width), jnp.bfloat16),
                pltpu.SemaphoreType.DMA((number, half // CHUNK)),
            ],
            compiler_params=pltpu.CompilerParams(vmem_limit_bytes=VMEM_LIMIT),
            cost_estimate=pl.CostEstimate(
                flops=number * pass_flops // count // 2,
                bytes_accessed=number * half * inner_width * 4,
                transcendentals=0,
            ),
            input_output_aliases={len(operands): 0},
            name=f"weight_gradient_{first}",
        )(place, *operands)

    def pair_sums(near_parts, far):
        return [summed(part, far[group]).astype(jnp.bfloat16) for group, part in enumerate(near_parts)]

    piece = count // 2
    layer_sums = pair_sums(layer_parts, layer_far)
    layer_near = across(layer_sums[1:])
    grad_sums = pair_sums(grad_parts, after((layer_sums, inner_other), grad_far))
    grad_near = across(grad_sums[1:])
    done = gradient(0, piece, after(grad_sums, done))
    layer_near = after((done, grad_near[:-1]), layer_near)
    layer_out = summed(section_inputs[0], layer_sums[0], *layer_near).astype(jnp.bfloat16)
    next_inputs = shifted(layer_out, "pipe", 1)[None]
    done = gradient(piece, count - piece, after(layer_out, done))
    grad_near = after((done, next_inputs), grad_near)
    input_grads = summed(output_grads[0], grad_sums[0], *grad_near).astype(jnp.bfloat16)
    prior_grads = shifted(input_grads, "pipe", -1)[None]
    return (next_inputs, prior_grads, done[None])


def on_device(*arrays):
    token_count = arrays[0].shape[1]
    local_count = arrays[-1].shape[1]
    groups, pair = lax.axis_size("expert"), lax.axis_size("dp")
    gathered = groups * token_count
    packed = groups * local_count * CAP
    paired = pair == 2 and local_count % 8 == 0 and groups & (groups - 1) == 0
    if gathered <= packed and paired and gathered * pair % LANES == 0:
        return gathered_plan(*arrays)
    return packed_plan(*arrays)


def solution(mesh):
    placed = (
        P("pipe", ("expert", "dp"), None),
        P("pipe", ("expert", "dp"), None),
        P("pipe", ("expert", "dp"), None),
        P("pipe", ("expert", "dp"), None),
        P("pipe", ("expert", "dp"), None),
        P("pipe", ("expert", "dp"), None),
        P("pipe", ("expert", "dp"), None),
        P("pipe", "expert", None, None),
    )
    return jax.shard_map(
        on_device,
        mesh=mesh,
        in_specs=placed,
        out_specs=(
            P("pipe", ("expert", "dp"), None),
            P("pipe", ("expert", "dp"), None),
            P("pipe", "expert", "dp", None),
        ),
        check_vma=False,
    )
```

```python
import functools

import jax
import jax.numpy as jnp
from jax import lax
from jax.experimental import pallas as pl
from jax.experimental.pallas import tpu as pltpu
from jax.sharding import PartitionSpec as P

CAP = 5
LANES = 128
CHUNK = 256
VMEM_LIMIT = 24 * 1024 * 1024
EXPERTS_LIMIT = 40 * 1024 * 1024
WEIGHT_CUTS = 4


def shifted(value, axis, steps):
    count = lax.axis_size(axis)
    pairs = [(source, (source + steps) % count) for source in range(count)]
    return lax.ppermute(value, axis, pairs)


def slot_index(routing, experts, capacity):
    one_hot = (routing[..., None] == jnp.arange(experts, dtype=jnp.int32)).astype(jnp.int32)
    before = jnp.cumsum(one_hot, axis=-2) - one_hot
    return routing * capacity + jnp.sum(before * one_hot, axis=-1)


def pack_rows(source, slot_ids, slot_total, spread):
    row_count = slot_ids.shape[0]
    owner_row = (
        jnp.zeros((slot_total,), jnp.int32)
        .at[slot_ids]
        .set(jnp.arange(row_count, dtype=jnp.int32) + 1)
    )
    filled = owner_row > 0
    picked = jnp.take(source, jnp.maximum(owner_row - 1, 0) // spread, axis=0)
    return jnp.where(filled[:, None], picked, jnp.zeros_like(picked))


def expert_forward(slot_rows, weights):
    hidden = jnp.einsum("nlcd,ldh->nlch", slot_rows, weights, preferred_element_type=jnp.float32)
    active = jax.nn.silu(hidden).astype(jnp.bfloat16)
    return jnp.einsum("nlch,ldh->nlcd", active, weights, preferred_element_type=jnp.float32).astype(
        jnp.bfloat16
    )


def expert_backward(saved_rows, slot_grads, weights):
    hidden = jnp.einsum("nlcd,ldh->nlch", saved_rows, weights, preferred_element_type=jnp.float32)
    active = jax.nn.silu(hidden).astype(jnp.bfloat16)
    active_grads = jnp.einsum(
        "nlcd,ldh->nlch", slot_grads, weights, preferred_element_type=jnp.float32
    )
    sigma = jax.nn.sigmoid(hidden)
    hidden_grads = (active_grads * sigma * (1.0 + hidden * (1.0 - sigma))).astype(jnp.bfloat16)
    row_grads = jnp.einsum(
        "nlch,ldh->nlcd", hidden_grads, weights, preferred_element_type=jnp.float32
    ).astype(jnp.bfloat16)
    weight_part = jnp.einsum(
        "nlcd,nlch->ldh", saved_rows, hidden_grads, preferred_element_type=jnp.float32
    )
    weight_part = weight_part + jnp.einsum(
        "nlcd,nlch->ldh", slot_grads, active, preferred_element_type=jnp.float32
    )
    return (row_grads, weight_part)


def packed_plan(
    section_inputs,
    saved_inputs,
    output_grads,
    forward_routes,
    backward_routes,
    forward_gates,
    backward_gates,
    expert_weights,
):
    token_count = section_inputs.shape[1]
    route_count = forward_routes.shape[2]
    local_count = expert_weights.shape[1]
    model_width = expert_weights.shape[2]
    groups = lax.axis_size("expert")
    experts = groups * local_count
    slot_total = experts * CAP
    block_shape = (groups, local_count, CAP, model_width)
    weights = expert_weights[0]
    forward_slot = slot_index(forward_routes[0].reshape(-1), experts, CAP)
    backward_slot = slot_index(backward_routes[0].reshape(-1), experts, CAP)
    forward_rows = pack_rows(section_inputs[0], forward_slot, slot_total, route_count).reshape(
        block_shape
    )
    saved_rows = pack_rows(saved_inputs[0], backward_slot, slot_total, route_count).reshape(
        block_shape
    )
    grad_block = output_grads[0]
    scaled = backward_gates[0][:, :, None] * grad_block.astype(jnp.float32)[:, None, :]
    scaled = scaled.astype(jnp.bfloat16).reshape(token_count * route_count, model_width)
    slot_grads = pack_rows(scaled, backward_slot, slot_total, 1).reshape(block_shape)
    forward_back = lax.all_to_all(
        expert_forward(
            lax.all_to_all(forward_rows, "expert", split_axis=0, concat_axis=0, tiled=True), weights
        ),
        "expert",
        split_axis=0,
        concat_axis=0,
        tiled=True,
    )
    saved_recv, grads_recv = (
        lax.all_to_all(saved_rows, "expert", split_axis=0, concat_axis=0, tiled=True),
        lax.all_to_all(slot_grads, "expert", split_axis=0, concat_axis=0, tiled=True),
    )
    row_grads, weight_part = expert_backward(saved_recv, grads_recv, weights)
    grads_back = lax.all_to_all(row_grads, "expert", split_axis=0, concat_axis=0, tiled=True)
    forward_pick = jnp.take(forward_back.reshape(slot_total, model_width), forward_slot, axis=0)
    forward_pick = forward_pick.reshape(token_count, route_count, model_width).astype(jnp.float32)
    layer_out = section_inputs[0].astype(jnp.float32) + jnp.sum(
        forward_gates[0][:, :, None] * forward_pick, axis=1
    )
    layer_out = layer_out.astype(jnp.bfloat16)
    grads_pick = jnp.take(grads_back.reshape(slot_total, model_width), backward_slot, axis=0)
    grads_pick = grads_pick.reshape(token_count, route_count, model_width).astype(jnp.float32)
    input_grads = (grad_block.astype(jnp.float32) + jnp.sum(grads_pick, axis=1)).astype(
        jnp.bfloat16
    )
    next_inputs = shifted(layer_out, "pipe", 1)[None]
    prior_grads = shifted(input_grads, "pipe", -1)[None]
    weight_grads = lax.psum_scatter(
        weight_part.astype(jnp.bfloat16), "dp", scatter_dimension=1, tiled=True
    )[None]
    return (next_inputs, prior_grads, weight_grads)


def swapped(value, code):
    axes = ("expert", "dp")
    count = lax.axis_size(axes[0]) * lax.axis_size(axes[1])
    return lax.ppermute(value, axes, [(source, source ^ code) for source in range(count)])


def pack_kernel(*refs):
    sources, (one, two), (*held, notes, done) = list(refs[:7]), refs[7:9], refs[9:]
    size, width = sources[0].shape
    half = width // 2
    top = sources[3].shape[0]
    targets = [one.at[:, pl.ds(0, width)], one.at[:, pl.ds(width, half)]]
    targets += [two.at[:, pl.ds(0, half)], two.at[:, pl.ds(half, width)]] + held
    sources[1:2] = [sources[1].at[:, pl.ds(0, half)], sources[1].at[:, pl.ds(half, half)]]
    copies = [
        pltpu.make_async_copy(source, target, done.at[place])
        for place, (source, target) in enumerate(zip(sources, targets))
    ]
    for copy in copies:
        copy.start()
    for copy in copies:
        copy.wait()
    back_routes, back_gates, fore_routes, fore_gates = held
    notes[...] = jnp.zeros_like(notes)
    for place, (routes, gates) in enumerate(((back_routes, back_gates), (fore_routes, fore_gates))):
        first = place * 4 * top
        notes[pl.ds(first, top), 0:size] = routes[...].astype(jnp.float32)
        rest = gates[...]
        for term in range(1, 4):
            part = rest.astype(jnp.bfloat16).astype(jnp.float32)
            notes[pl.ds(first + term * top, top), 0:size] = part
            rest = rest - part
    one[:, pl.ds(width + half, LANES)] = notes[...].T[:size, :].astype(jnp.bfloat16)


def picks_kernel(count, top, slots, devices, place_ref, *refs):
    blocks, outs, (notes, turned) = refs[:devices], refs[devices:-2], refs[-2:]
    tokens = notes.shape[0]
    for code, block in enumerate(blocks):
        size = block.shape[0]
        rows = pl.ds(pl.multiple_of(place_ref[3 + code], size), size)
        notes[rows, :] = block[...].astype(jnp.float32)
    turned[...] = notes[...].T
    row = lax.broadcasted_iota(jnp.int32, (tokens, tokens), 0)
    column = lax.broadcasted_iota(jnp.int32, (tokens, tokens), 1)
    earlier = jnp.where(row < column, 1.0, 0.0).astype(jnp.bfloat16)
    slot = lax.broadcasted_iota(jnp.int32, (slots, tokens), 0).astype(jnp.float32)

    def find(first, start):
        ids = (first + lax.broadcasted_iota(jnp.int32, (count, tokens), 0)).astype(jnp.float32)
        named = jnp.zeros((count, tokens), jnp.float32)
        gated = jnp.zeros((count, tokens), jnp.float32)
        for column in range(start, start + top):
            same = turned[column : column + 1, :] == ids
            terms = [turned[column + term * top : column + term * top + 1, :] for term in (1, 2, 3)]
            named = named + jnp.where(same, 1.0, 0.0)
            gated = gated + jnp.where(same, terms[0] + terms[1] + terms[2], 0.0)
        place = jnp.dot(named.astype(jnp.bfloat16), earlier, preferred_element_type=jnp.float32)
        return jnp.where(named > 0.0, place, -1.0), gated

    def fill(place, gated, picks, gates, flipped):
        for expert in range(count):
            rows = pl.ds(expert * slots, slots)
            hit = place[expert : expert + 1, :] == slot
            picks[rows, :] = jnp.where(hit, 1.0, 0.0).astype(jnp.bfloat16)
            own = jnp.sum(jnp.where(hit, gated[expert : expert + 1, :], 0.0), axis=1, keepdims=True)
            gates[rows, :] = jnp.broadcast_to(own, (slots, LANES))
        flipped[...] = picks[...].T

    places, gated = find(place_ref[1], 4 * top)
    fill(places, gated, outs[0], outs[1], outs[2])
    places, gated = find(place_ref[1], 0)
    fill(places, gated, outs[3], outs[4], outs[5])
    other_places, other_gated = find(place_ref[2], 0)
    turned[...] = jnp.zeros_like(turned)
    for row, value in enumerate((places, other_places, gated, other_gated)):
        turned[pl.ds(row * count, count), :] = value
    outs[6][...] = turned[...].T


def spread_gate(gates, rows, width):
    gate = gates[rows, 0:1]
    return jnp.broadcast_to(gate, (gate.shape[0], width))


def assemble(place_ref, first, second, tokens):
    width = tokens[0].shape[1]
    half = width // 2
    for code, (one, two) in enumerate(zip(first, second)):
        size = one.shape[0]
        rows = pl.ds(pl.multiple_of(place_ref[3 + code], size), size)
        tokens[0][rows, :] = one[:, pl.ds(0, width)]
        tokens[1][rows, pl.ds(0, half)] = one[:, pl.ds(width, half)]
        tokens[1][rows, pl.ds(half, half)] = two[:, pl.ds(0, half)]
        tokens[2][rows, :] = two[:, pl.ds(half, width)]


def combine(flipped, results, sums):
    width = sums.shape[1]
    for start in range(0, width, CHUNK):
        columns = pl.ds(start, CHUNK)
        sums[:, columns] = jnp.dot(
            flipped[...], results[:, columns], preferred_element_type=jnp.float32
        ).astype(sums.dtype)


def gather(count, slots, picks, gates, tokens_ref, rows, first, stride):
    width = tokens_ref.shape[1]
    for start in range(0, width, CHUNK):
        columns = pl.ds(start, CHUNK)
        taken = jnp.dot(picks[...], tokens_ref[:, columns], preferred_element_type=jnp.float32)
        if gates is not None:
            taken = taken * spread_gate(gates, pl.ds(0, count * slots), CHUNK)
        taken = taken.astype(rows.dtype)
        for expert in range(count):
            part = slice(expert * slots, (expert + 1) * slots)
            rows[pl.ds(first + expert * stride, slots), columns] = taken[part]


def expert_kernel(count, slots, devices, pair, place_ref, *refs):
    fore_picks, fore_gates, fore_flip, back_picks, back_gates, back_flip = refs[:6]
    weights, blocks = refs[6 : 6 + WEIGHT_CUTS], refs[6 + WEIGHT_CUTS :][: 2 * devices]
    groups = devices // pair
    outs = refs[6 + WEIGHT_CUTS + 2 * devices :][: 2 * groups + 2]
    inner, turned, gradient, *scratch = refs[8 + WEIGHT_CUTS + 2 * devices + 2 * groups :]
    tokens, (rows, fore_results, back_results, second) = scratch[:3], scratch[3:]
    total, width = tokens[0].shape
    step = pl.program_id(0)

    @pl.when(step == 0)
    def _():
        taken = ((fore_picks, None), (back_picks, None), (back_picks, back_gates))
        assemble(place_ref, blocks[:devices], blocks[devices:], tokens)
        for place, (picks, gates) in enumerate(taken):
            gather(count, slots, picks, gates, tokens[place], rows, place * slots, 3 * slots)

    mine = pl.ds(pl.multiple_of(step * slots, slots), slots)
    three = pl.ds(pl.multiple_of(step * 3 * slots, 3 * slots), 3 * slots)
    cut = width // WEIGHT_CUTS
    for start in range(0, inner.shape[2], CHUNK):
        lanes = pl.ds(start, CHUNK)
        product = functools.reduce(
            jnp.add,
            [
                jnp.dot(
                    rows[three, pl.ds(place * cut, cut)],
                    weight[0, :, lanes],
                    preferred_element_type=jnp.float32,
                )
                for place, weight in enumerate(weights)
            ],
        )
        ahead, hidden, active_grads = (
            product[:slots],
            product[slots : 2 * slots],
            product[2 * slots :],
        )
        sigma = jax.nn.sigmoid(hidden)
        hidden_grads = (active_grads * sigma * (1.0 + hidden * (1.0 - sigma))).astype(jnp.bfloat16)
        inner[0, :slots, lanes] = hidden_grads
        inner[0, slots:, lanes] = (hidden * sigma).astype(jnp.bfloat16)
        gate = spread_gate(fore_gates, mine, CHUNK)
        second[:slots, lanes] = (ahead * jax.nn.sigmoid(ahead) * gate).astype(jnp.bfloat16)
        second[slots:, lanes] = hidden_grads
    for start in range(0, width, CHUNK):
        columns = pl.ds(start, CHUNK)
        result = lax.dot_general(
            second[...],
            weights[start // cut][0, pl.ds(start % cut, CHUNK), :],
            (((1,), (1,)), ((), ())),
            preferred_element_type=jnp.float32,
        ).astype(fore_results.dtype)
        fore_results[mine, columns] = result[:slots]
        back_results[mine, columns] = result[slots:]

    half = gradient.shape[1]
    two = pl.ds(pl.multiple_of(step * 3 * slots + slots, slots), 2 * slots)
    flat = rows[two, pl.ds(pl.multiple_of(place_ref[0] * half, LANES), half)].T
    for start in range(0, gradient.shape[2], CHUNK):
        columns = pl.ds(start, CHUNK)
        gradient[0, :, columns] = jnp.dot(
            flat, inner[0, :, columns], preferred_element_type=jnp.float32
        ).astype(gradient.dtype)

    span = turned.shape[0]
    first = place_ref[0] * half + step * span
    for place in range(2):
        some = tokens[1 + place][:, pl.ds(pl.multiple_of(first, LANES), span)]
        turned[:, pl.ds(place * total, total)] = some.T

    @pl.when(step == count - 1)
    def _():
        for lead, (flipped, results) in enumerate(
            ((fore_flip, fore_results), (back_flip, back_results))
        ):
            sums = tokens[lead]
            combine(flipped, results, sums)
            *near_outs, far_out = outs[lead * (groups + 1) : (lead + 1) * (groups + 1)]
            size = far_out.shape[1]
            for group, out in enumerate(near_outs):
                near, far = (
                    pl.ds(pl.multiple_of(place_ref[3 + pair * group + code], size), size)
                    for code in range(pair)
                )
                out[...] = sums[near, :]
                far_out[group] = sums[far, :]


def weight_kernel(first, number, count, slots, place_ref, *refs):
    columns, inner, turned = refs[:3]
    out_ref, picks, rows, staged, out_done = refs[-5:]
    total, half = columns.shape[0], turned.shape[0]
    owner = 1 - place_ref[0]
    lane = lax.broadcasted_iota(jnp.int32, (total, LANES), 1).astype(jnp.float32)
    is_saved = lax.broadcasted_iota(jnp.int32, (1, LANES), 1) < slots
    scales = []
    for step in range(number):
        column = count + first + step
        slot = jnp.broadcast_to(columns[:, column : column + 1], (total, LANES))
        column += 2 * count
        gate = jnp.broadcast_to(columns[:, column : column + 1], (total, LANES))
        saved, grads = slot == lane, slot == lane - slots
        lanes = pl.ds(step * LANES, LANES)
        picks[pl.ds(0, total), lanes] = jnp.where(saved, 1.0, 0.0).astype(picks.dtype)
        picks[pl.ds(total, total), lanes] = jnp.where(
            jnp.logical_and(grads, lane >= slots), 1.0, 0.0
        ).astype(picks.dtype)
        scale = jnp.sum(jnp.where(grads, gate, 0.0), axis=0, keepdims=True)
        scales.append(jnp.where(is_saved, 1.0, scale))
    for step in range(0, number, 2):
        lanes = pl.ds(step * LANES, 2 * LANES)
        scale = jnp.concatenate(scales[step : step + 2], axis=1)
        rows[:, lanes] = (
            jnp.dot(turned[...], picks[:, lanes], preferred_element_type=jnp.float32) * scale
        ).astype(rows.dtype)

    leaving = []
    for step in range(number):
        for start in range(0, half, CHUNK):
            chunk = pl.ds(start, CHUNK)
            for corner in range(start, start + CHUNK, LANES):
                for column in range(0, inner.shape[2], CHUNK):
                    tile = (step, pl.ds(corner, LANES), pl.ds(column, CHUNK))
                    staged[tile] = jnp.dot(
                        rows[tile[1], pl.ds(step * LANES, 2 * slots)],
                        inner[first + step, :, tile[2]],
                        preferred_element_type=jnp.float32,
                    ).astype(staged.dtype)
            leaving.append(
                pltpu.make_async_copy(
                    staged.at[step, chunk, :],
                    out_ref.at[owner * count + first + step, chunk, :],
                    out_done.at[step, start // CHUNK],
                )
            )
            leaving[-1].start()
    for copy in leaving:
        copy.wait()


def gathered_plan(
    section_inputs,
    saved_inputs,
    output_grads,
    forward_routes,
    backward_routes,
    forward_gates,
    backward_gates,
    expert_weights,
):
    token_count = section_inputs.shape[1]
    top = forward_routes.shape[2]
    _, local_count, width, inner_width = expert_weights.shape
    groups, pair = lax.axis_size("expert"), lax.axis_size("dp")
    devices = groups * pair
    count = local_count // pair
    total = devices * token_count
    slots = -(-devices * CAP // 16) * 16
    rows = count * slots
    half = width // pair
    weights = expert_weights[0]

    side, group = lax.axis_index("dp"), lax.axis_index("expert")
    index = group * pair + side
    base = group * local_count
    place = jnp.stack(
        [side, base + side * count, base + (1 - side) * count]
        + [(index ^ code) * token_count for code in range(devices)]
    ).astype(jnp.int32)
    params = pltpu.CompilerParams(vmem_limit_bytes=VMEM_LIMIT, dimension_semantics=("arbitrary",))

    def whole(shape):
        return pl.BlockSpec(shape, lambda *_: (0,) * len(shape))

    def call(kernel, name, steps, in_specs, out_specs, out_shape, scratch, flops=0, aliases=()):
        return pl.pallas_call(
            kernel,
            grid_spec=pltpu.PrefetchScalarGridSpec(
                num_scalar_prefetch=1,
                grid=(steps,),
                in_specs=in_specs,
                out_specs=out_specs,
                scratch_shapes=scratch,
            ),
            out_shape=out_shape,
            compiler_params=params,
            cost_estimate=pl.CostEstimate(
                flops=flops, bytes_accessed=flops // 512 + 1024, transcendentals=0
            ),
            input_output_aliases=dict(aliases),
            name=name,
        )

    def onward(block):
        return swapped(block, 1)

    def across(parts):
        return [swapped(part, code) for part, code in zip(parts, range(pair, devices, pair))]

    def after(first, then):
        then, _ = lax.optimization_barrier((then, first))
        return then

    def summed(*blocks):
        return functools.reduce(jnp.add, [block.astype(jnp.float32) for block in blocks])

    packed = [
        jax.ShapeDtypeStruct((token_count, 3 * width // 2 + extra), jnp.bfloat16)
        for extra in (LANES, 0)
    ]
    own = pl.pallas_call(
        pack_kernel,
        in_specs=[pl.BlockSpec(memory_space=pl.ANY)] * 7,
        out_specs=[pl.BlockSpec(memory_space=pltpu.VMEM)] * 2,
        out_shape=packed,
        scratch_shapes=[
            pltpu.VMEM((top, token_count), jnp.int32),
            pltpu.VMEM((top, token_count), jnp.float32),
            pltpu.VMEM((top, token_count), jnp.int32),
            pltpu.VMEM((top, token_count), jnp.float32),
            pltpu.VMEM((LANES, LANES), jnp.float32),
            pltpu.SemaphoreType.DMA((8,)),
        ],
        compiler_params=pltpu.CompilerParams(vmem_limit_bytes=VMEM_LIMIT),
        name="pack",
    )(
        *[
            pltpu.with_memory_space_constraint(array, pltpu.HBM)
            for array in (
                section_inputs[0],
                saved_inputs[0],
                output_grads[0],
                backward_routes[0].T,
                backward_gates[0].T,
                forward_routes[0].T,
                forward_gates[0].T,
            )
        ]
    )
    bits = groups.bit_length() - 1
    far_own = [onward(block) for block in own]
    near = []
    for way, (block, far) in enumerate(zip(own, far_own)):
        held = {0: block}
        for bit in range(bits):
            step = 1 << (bit if way == 0 else bits - 1 - bit)
            sources = dict(held) if bit == 0 else {0: block} | after(far, {k: v for k, v in held.items() if k})
            held |= {group ^ step: swapped(source, step * pair) for group, source in sources.items()}
        near.append([held[group] for group in range(groups)])
    direct = [1 << bit for bit in range(bits)]
    settled = lax.optimization_barrier([[half_blocks[group] for group in direct] for half_blocks in near])
    blocks = []
    for half_blocks, far, firm in zip(near, far_own, settled):
        ready = list(half_blocks)
        for group, block in zip(direct, firm):
            ready[group] = block
        distant = [far] + [onward(block) for block in ready[1:]]
        blocks += [block for both in zip(half_blocks, distant) for block in both]

    pick = jax.ShapeDtypeStruct((rows, total), jnp.bfloat16)
    flip = jax.ShapeDtypeStruct((total, rows), jnp.bfloat16)
    gate = jax.ShapeDtypeStruct((rows, LANES), jnp.float32)
    columns = jax.ShapeDtypeStruct((total, LANES), jnp.float32)
    pick_outs = [pick, gate, flip, pick, gate, flip, columns]
    picks = call(
        functools.partial(picks_kernel, count, top, slots, devices),
        "slot_picks",
        1,
        [pl.BlockSpec((token_count, LANES), lambda *_: (0, 3 * width // 2 // LANES))] * devices,
        [whole(out.shape) for out in pick_outs],
        pick_outs,
        [pltpu.VMEM((total, LANES), jnp.float32), pltpu.VMEM((LANES, total), jnp.float32)],
    )(place, *blocks[:devices])

    pass_flops = 2 * 2 * count * CHUNK * width * inner_width
    near_part = jax.ShapeDtypeStruct((token_count, width), jnp.bfloat16)
    far_part = jax.ShapeDtypeStruct((groups, token_count, width), jnp.bfloat16)
    inner = jax.ShapeDtypeStruct((count, 2 * slots, inner_width), jnp.bfloat16)
    turned = jax.ShapeDtypeStruct((half, 2 * total), jnp.bfloat16)
    in_smem, in_vmem, anywhere = (
        pl.BlockSpec(memory_space=space) for space in (pltpu.SMEM, pltpu.VMEM, pl.ANY)
    )
    tokens = pltpu.VMEM((total, width), jnp.bfloat16)
    cut = width // WEIGHT_CUTS
    whole_gradient = jax.ShapeDtypeStruct((local_count, half, inner_width), jnp.bfloat16)
    *parts, inner_own, tokens_turned, done = pl.pallas_call(
        functools.partial(expert_kernel, count, slots, devices, pair),
        grid_spec=pltpu.PrefetchScalarGridSpec(
            num_scalar_prefetch=1,
            grid=(count,),
            in_specs=[whole(array.shape) for array in pick_outs[:6]]
            + [
                pl.BlockSpec(
                    (1, cut, inner_width),
                    lambda step, place, part=part: (place[0] * count + step, part, 0),
                )
                for part in range(WEIGHT_CUTS)
            ]
            + [whole(one.shape) for one in packed for _ in range(devices)],
            out_specs=([whole(near_part.shape)] * groups + [whole(far_part.shape)]) * 2
            + [
                pl.BlockSpec((1, 2 * slots, inner_width), lambda step, place: (step, 0, 0)),
                pl.BlockSpec((half // count, 2 * total), lambda step, place: (step, 0)),
                pl.BlockSpec(
                    (1, half, inner_width), lambda step, place: (place[0] * count + step, 0, 0)
                ),
            ],
            scratch_shapes=[tokens] * 3
            + [
                pltpu.VMEM((3 * rows, width), jnp.bfloat16),
                pltpu.VMEM((rows, width), jnp.bfloat16),
                pltpu.VMEM((rows, width), jnp.bfloat16),
                pltpu.VMEM((2 * slots, inner_width), jnp.bfloat16),
            ],
        ),
        out_shape=([near_part] * groups + [far_part]) * 2 + [inner, turned, whole_gradient],
        compiler_params=pltpu.CompilerParams(
            vmem_limit_bytes=EXPERTS_LIMIT, dimension_semantics=("arbitrary",)
        ),
        cost_estimate=pl.CostEstimate(
            flops=pass_flops, bytes_accessed=pass_flops // 512, transcendentals=0
        ),
        name="experts",
    )(place, *picks[:6], *[weights] * WEIGHT_CUTS, *blocks)
    *layer_parts, layer_far = parts[: groups + 1]
    *grad_parts, grad_far = parts[groups + 1 :]
    layer_far, grad_far = onward(layer_far), onward(grad_far)
    inner_other = onward(after(layer_far, inner_own))

    def gradient(first, number, earlier):
        operands = [picks[6], inner_other, tokens_turned, earlier]
        return pl.pallas_call(
            functools.partial(weight_kernel, first, number, count, slots),
            in_specs=[in_smem, in_vmem, in_vmem, in_vmem, anywhere],
            out_specs=anywhere,
            out_shape=whole_gradient,
            scratch_shapes=[
                pltpu.VMEM((2 * total, number * LANES), jnp.bfloat16),
                pltpu.VMEM((half, number * LANES), jnp.bfloat16),
                pltpu.VMEM((number, half, inner_width), jnp.bfloat16),
                pltpu.SemaphoreType.DMA((number, half // CHUNK)),
            ],
            compiler_params=pltpu.CompilerParams(vmem_limit_bytes=VMEM_LIMIT),
            cost_estimate=pl.CostEstimate(
                flops=number * pass_flops // count // 2,
                bytes_accessed=number * half * inner_width * 4,
                transcendentals=0,
            ),
            input_output_aliases={len(operands): 0},
            name=f"weight_gradient_{first}",
        )(place, *operands)

    def pair_sums(near_parts, far):
        return [summed(part, far[group]).astype(jnp.bfloat16) for group, part in enumerate(near_parts)]

    piece = count // 2
    layer_sums = pair_sums(layer_parts, layer_far)
    layer_near = across(layer_sums[1:])
    grad_sums = pair_sums(grad_parts, after((layer_sums, inner_other), grad_far))
    grad_near = across(grad_sums[1:])
    done = gradient(0, piece, after(grad_sums, done))
    layer_near = after((done, grad_near[:-1]), layer_near)
    layer_out = summed(section_inputs[0], layer_sums[0], *layer_near).astype(jnp.bfloat16)
    next_inputs = shifted(layer_out, "pipe", 1)[None]
    done = gradient(piece, count - piece, after(layer_out, done))
    grad_near = after((done, next_inputs), grad_near)
    input_grads = summed(output_grads[0], grad_sums[0], *grad_near).astype(jnp.bfloat16)
    prior_grads = shifted(input_grads, "pipe", -1)[None]
    return (next_inputs, prior_grads, done[None])


def on_device(*arrays):
    token_count = arrays[0].shape[1]
    local_count = arrays[-1].shape[1]
    groups, pair = lax.axis_size("expert"), lax.axis_size("dp")
    gathered = groups * token_count
    packed = groups * local_count * CAP
    paired = pair == 2 and local_count % 8 == 0 and groups & (groups - 1) == 0
    if gathered <= packed and paired and gathered * pair % LANES == 0:
        return gathered_plan(*arrays)
    return packed_plan(*arrays)


def solution(mesh):
    placed = (
        P("pipe", ("expert", "dp"), None),
        P("pipe", ("expert", "dp"), None),
        P("pipe", ("expert", "dp"), None),
        P("pipe", ("expert", "dp"), None),
        P("pipe", ("expert", "dp"), None),
        P("pipe", ("expert", "dp"), None),
        P("pipe", ("expert", "dp"), None),
        P("pipe", "expert", None, None),
    )
    return jax.shard_map(
        on_device,
        mesh=mesh,
        in_specs=placed,
        out_specs=(
            P("pipe", ("expert", "dp"), None),
            P("pipe", ("expert", "dp"), None),
            P("pipe", "expert", "dp", None),
        ),
        check_vma=False,
    )
```

```python
import functools

import jax
import jax.numpy as jnp
from jax import lax
from jax.experimental import pallas as pl
from jax.experimental.pallas import tpu as pltpu
from jax.sharding import PartitionSpec as P

CAP = 5
LANES = 128
CHUNK = 256
VMEM_LIMIT = 24 * 1024 * 1024
EXPERTS_LIMIT = 40 * 1024 * 1024
WEIGHT_CUTS = 4


def shifted(value, axis, steps):
    count = lax.axis_size(axis)
    pairs = [(source, (source + steps) % count) for source in range(count)]
    return lax.ppermute(value, axis, pairs)


def slot_index(routing, experts, capacity):
    one_hot = (routing[..., None] == jnp.arange(experts, dtype=jnp.int32)).astype(jnp.int32)
    before = jnp.cumsum(one_hot, axis=-2) - one_hot
    return routing * capacity + jnp.sum(before * one_hot, axis=-1)


def pack_rows(source, slot_ids, slot_total, spread):
    row_count = slot_ids.shape[0]
    owner_row = (
        jnp.zeros((slot_total,), jnp.int32)
        .at[slot_ids]
        .set(jnp.arange(row_count, dtype=jnp.int32) + 1)
    )
    filled = owner_row > 0
    picked = jnp.take(source, jnp.maximum(owner_row - 1, 0) // spread, axis=0)
    return jnp.where(filled[:, None], picked, jnp.zeros_like(picked))


def expert_forward(slot_rows, weights):
    hidden = jnp.einsum("nlcd,ldh->nlch", slot_rows, weights, preferred_element_type=jnp.float32)
    active = jax.nn.silu(hidden).astype(jnp.bfloat16)
    return jnp.einsum("nlch,ldh->nlcd", active, weights, preferred_element_type=jnp.float32).astype(
        jnp.bfloat16
    )


def expert_backward(saved_rows, slot_grads, weights):
    hidden = jnp.einsum("nlcd,ldh->nlch", saved_rows, weights, preferred_element_type=jnp.float32)
    active = jax.nn.silu(hidden).astype(jnp.bfloat16)
    active_grads = jnp.einsum(
        "nlcd,ldh->nlch", slot_grads, weights, preferred_element_type=jnp.float32
    )
    sigma = jax.nn.sigmoid(hidden)
    hidden_grads = (active_grads * sigma * (1.0 + hidden * (1.0 - sigma))).astype(jnp.bfloat16)
    row_grads = jnp.einsum(
        "nlch,ldh->nlcd", hidden_grads, weights, preferred_element_type=jnp.float32
    ).astype(jnp.bfloat16)
    weight_part = jnp.einsum(
        "nlcd,nlch->ldh", saved_rows, hidden_grads, preferred_element_type=jnp.float32
    )
    weight_part = weight_part + jnp.einsum(
        "nlcd,nlch->ldh", slot_grads, active, preferred_element_type=jnp.float32
    )
    return (row_grads, weight_part)


def packed_plan(
    section_inputs,
    saved_inputs,
    output_grads,
    forward_routes,
    backward_routes,
    forward_gates,
    backward_gates,
    expert_weights,
):
    token_count = section_inputs.shape[1]
    route_count = forward_routes.shape[2]
    local_count = expert_weights.shape[1]
    model_width = expert_weights.shape[2]
    groups = lax.axis_size("expert")
    experts = groups * local_count
    slot_total = experts * CAP
    block_shape = (groups, local_count, CAP, model_width)
    weights = expert_weights[0]
    forward_slot = slot_index(forward_routes[0].reshape(-1), experts, CAP)
    backward_slot = slot_index(backward_routes[0].reshape(-1), experts, CAP)
    forward_rows = pack_rows(section_inputs[0], forward_slot, slot_total, route_count).reshape(
        block_shape
    )
    saved_rows = pack_rows(saved_inputs[0], backward_slot, slot_total, route_count).reshape(
        block_shape
    )
    grad_block = output_grads[0]
    scaled = backward_gates[0][:, :, None] * grad_block.astype(jnp.float32)[:, None, :]
    scaled = scaled.astype(jnp.bfloat16).reshape(token_count * route_count, model_width)
    slot_grads = pack_rows(scaled, backward_slot, slot_total, 1).reshape(block_shape)
    forward_back = lax.all_to_all(
        expert_forward(
            lax.all_to_all(forward_rows, "expert", split_axis=0, concat_axis=0, tiled=True), weights
        ),
        "expert",
        split_axis=0,
        concat_axis=0,
        tiled=True,
    )
    saved_recv, grads_recv = (
        lax.all_to_all(saved_rows, "expert", split_axis=0, concat_axis=0, tiled=True),
        lax.all_to_all(slot_grads, "expert", split_axis=0, concat_axis=0, tiled=True),
    )
    row_grads, weight_part = expert_backward(saved_recv, grads_recv, weights)
    grads_back = lax.all_to_all(row_grads, "expert", split_axis=0, concat_axis=0, tiled=True)
    forward_pick = jnp.take(forward_back.reshape(slot_total, model_width), forward_slot, axis=0)
    forward_pick = forward_pick.reshape(token_count, route_count, model_width).astype(jnp.float32)
    layer_out = section_inputs[0].astype(jnp.float32) + jnp.sum(
        forward_gates[0][:, :, None] * forward_pick, axis=1
    )
    layer_out = layer_out.astype(jnp.bfloat16)
    grads_pick = jnp.take(grads_back.reshape(slot_total, model_width), backward_slot, axis=0)
    grads_pick = grads_pick.reshape(token_count, route_count, model_width).astype(jnp.float32)
    input_grads = (grad_block.astype(jnp.float32) + jnp.sum(grads_pick, axis=1)).astype(
        jnp.bfloat16
    )
    next_inputs = shifted(layer_out, "pipe", 1)[None]
    prior_grads = shifted(input_grads, "pipe", -1)[None]
    weight_grads = lax.psum_scatter(
        weight_part.astype(jnp.bfloat16), "dp", scatter_dimension=1, tiled=True
    )[None]
    return (next_inputs, prior_grads, weight_grads)


def swapped(value, code):
    axes = ("expert", "dp")
    count = lax.axis_size(axes[0]) * lax.axis_size(axes[1])
    return lax.ppermute(value, axes, [(source, source ^ code) for source in range(count)])


def pack_kernel(*refs):
    sources, (one, two), (*held, notes, done) = list(refs[:7]), refs[7:9], refs[9:]
    size, width = sources[0].shape
    half = width // 2
    top = sources[3].shape[0]
    targets = [one.at[:, pl.ds(0, width)], one.at[:, pl.ds(width, half)]]
    targets += [two.at[:, pl.ds(0, half)], two.at[:, pl.ds(half, width)]] + held
    sources[1:2] = [sources[1].at[:, pl.ds(0, half)], sources[1].at[:, pl.ds(half, half)]]
    copies = [
        pltpu.make_async_copy(source, target, done.at[place])
        for place, (source, target) in enumerate(zip(sources, targets))
    ]
    for copy in copies:
        copy.start()
    for copy in copies:
        copy.wait()
    back_routes, back_gates, fore_routes, fore_gates = held
    for place, (target, lane, routes, gates) in enumerate(
        ((two, half + width, back_routes, back_gates), (one, width + half, fore_routes, fore_gates))
    ):
        first = place * 4 * top
        notes[...] = jnp.zeros_like(notes)
        notes[pl.ds(first, top), 0:size] = routes[...].astype(jnp.float32)
        rest = gates[...]
        for term in range(1, 4):
            part = rest.astype(jnp.bfloat16).astype(jnp.float32)
            notes[pl.ds(first + term * top, top), 0:size] = part
            rest = rest - part
        target[:, pl.ds(lane, LANES)] = notes[...].T[:size, :].astype(jnp.bfloat16)


def picks_kernel(count, top, slots, devices, place_ref, *refs):
    blocks, outs, (notes, turned) = refs[: 2 * devices], refs[2 * devices : -2], refs[-2:]
    tokens = notes.shape[0]
    for code, (one, two) in enumerate(zip(blocks[:devices], blocks[devices:])):
        size = one.shape[0]
        rows = pl.ds(pl.multiple_of(place_ref[3 + code], size), size)
        notes[rows, :] = one[...].astype(jnp.float32) + two[...].astype(jnp.float32)
    turned[...] = notes[...].T
    row = lax.broadcasted_iota(jnp.int32, (tokens, tokens), 0)
    column = lax.broadcasted_iota(jnp.int32, (tokens, tokens), 1)
    earlier = jnp.where(row < column, 1.0, 0.0).astype(jnp.bfloat16)
    slot = lax.broadcasted_iota(jnp.int32, (slots, tokens), 0).astype(jnp.float32)

    def find(first, start):
        ids = (first + lax.broadcasted_iota(jnp.int32, (count, tokens), 0)).astype(jnp.float32)
        named = jnp.zeros((count, tokens), jnp.float32)
        gated = jnp.zeros((count, tokens), jnp.float32)
        for column in range(start, start + top):
            same = turned[column : column + 1, :] == ids
            terms = [turned[column + term * top : column + term * top + 1, :] for term in (1, 2, 3)]
            named = named + jnp.where(same, 1.0, 0.0)
            gated = gated + jnp.where(same, terms[0] + terms[1] + terms[2], 0.0)
        place = jnp.dot(named.astype(jnp.bfloat16), earlier, preferred_element_type=jnp.float32)
        return jnp.where(named > 0.0, place, -1.0), gated

    def fill(place, gated, picks, gates, flipped):
        for expert in range(count):
            rows = pl.ds(expert * slots, slots)
            hit = place[expert : expert + 1, :] == slot
            picks[rows, :] = jnp.where(hit, 1.0, 0.0).astype(jnp.bfloat16)
            own = jnp.sum(jnp.where(hit, gated[expert : expert + 1, :], 0.0), axis=1, keepdims=True)
            gates[rows, :] = jnp.broadcast_to(own, (slots, LANES))
        flipped[...] = picks[...].T

    places, gated = find(place_ref[1], 4 * top)
    fill(places, gated, outs[0], outs[1], outs[2])
    places, gated = find(place_ref[1], 0)
    fill(places, gated, outs[3], outs[4], outs[5])
    other_places, other_gated = find(place_ref[2], 0)
    turned[...] = jnp.zeros_like(turned)
    for row, value in enumerate((places, other_places, gated, other_gated)):
        turned[pl.ds(row * count, count), :] = value
    outs[6][...] = turned[...].T


def spread_gate(gates, rows, width):
    gate = gates[rows, 0:1]
    return jnp.broadcast_to(gate, (gate.shape[0], width))


def assemble(place_ref, first, second, tokens):
    width = tokens[0].shape[1]
    half = width // 2
    for code, (one, two) in enumerate(zip(first, second)):
        size = one.shape[0]
        rows = pl.ds(pl.multiple_of(place_ref[3 + code], size), size)
        tokens[0][rows, :] = one[:, pl.ds(0, width)]
        tokens[1][rows, pl.ds(0, half)] = one[:, pl.ds(width, half)]
        tokens[1][rows, pl.ds(half, half)] = two[:, pl.ds(0, half)]
        tokens[2][rows, :] = two[:, pl.ds(half, width)]


def combine(flipped, results, sums):
    width = sums.shape[1]
    for start in range(0, width, CHUNK):
        columns = pl.ds(start, CHUNK)
        sums[:, columns] = jnp.dot(
            flipped[...], results[:, columns], preferred_element_type=jnp.float32
        ).astype(sums.dtype)


def gather(count, slots, picks, gates, tokens_ref, rows, first, stride):
    width = tokens_ref.shape[1]
    for start in range(0, width, CHUNK):
        columns = pl.ds(start, CHUNK)
        taken = jnp.dot(picks[...], tokens_ref[:, columns], preferred_element_type=jnp.float32)
        if gates is not None:
            taken = taken * spread_gate(gates, pl.ds(0, count * slots), CHUNK)
        taken = taken.astype(rows.dtype)
        for expert in range(count):
            part = slice(expert * slots, (expert + 1) * slots)
            rows[pl.ds(first + expert * stride, slots), columns] = taken[part]


def expert_kernel(count, slots, devices, pair, place_ref, *refs):
    fore_picks, fore_gates, fore_flip, back_picks, back_gates, back_flip = refs[:6]
    weights, blocks = refs[6 : 6 + WEIGHT_CUTS], refs[6 + WEIGHT_CUTS :][: 2 * devices]
    groups = devices // pair
    outs = refs[6 + WEIGHT_CUTS + 2 * devices :][: 2 * groups + 2]
    inner, turned, gradient, *scratch = refs[8 + WEIGHT_CUTS + 2 * devices + 2 * groups :]
    tokens, (rows, fore_results, back_results, second) = scratch[:3], scratch[3:]
    total, width = tokens[0].shape
    step = pl.program_id(0)

    @pl.when(step == 0)
    def _():
        taken = ((fore_picks, None), (back_picks, None), (back_picks, back_gates))
        assemble(place_ref, blocks[:devices], blocks[devices:], tokens)
        for place, (picks, gates) in enumerate(taken):
            gather(count, slots, picks, gates, tokens[place], rows, place * slots, 3 * slots)

    mine = pl.ds(pl.multiple_of(step * slots, slots), slots)
    three = pl.ds(pl.multiple_of(step * 3 * slots, 3 * slots), 3 * slots)
    cut = width // WEIGHT_CUTS
    for start in range(0, inner.shape[2], CHUNK):
        lanes = pl.ds(start, CHUNK)
        product = functools.reduce(
            jnp.add,
            [
                jnp.dot(
                    rows[three, pl.ds(place * cut, cut)],
                    weight[0, :, lanes],
                    preferred_element_type=jnp.float32,
                )
                for place, weight in enumerate(weights)
            ],
        )
        ahead, hidden, active_grads = (
            product[:slots],
            product[slots : 2 * slots],
            product[2 * slots :],
        )
        sigma = jax.nn.sigmoid(hidden)
        hidden_grads = (active_grads * sigma * (1.0 + hidden * (1.0 - sigma))).astype(jnp.bfloat16)
        inner[0, :slots, lanes] = hidden_grads
        inner[0, slots:, lanes] = (hidden * sigma).astype(jnp.bfloat16)
        gate = spread_gate(fore_gates, mine, CHUNK)
        second[:slots, lanes] = (ahead * jax.nn.sigmoid(ahead) * gate).astype(jnp.bfloat16)
        second[slots:, lanes] = hidden_grads
    for start in range(0, width, CHUNK):
        columns = pl.ds(start, CHUNK)
        result = lax.dot_general(
            second[...],
            weights[start // cut][0, pl.ds(start % cut, CHUNK), :],
            (((1,), (1,)), ((), ())),
            preferred_element_type=jnp.float32,
        ).astype(fore_results.dtype)
        fore_results[mine, columns] = result[:slots]
        back_results[mine, columns] = result[slots:]

    half = gradient.shape[1]
    two = pl.ds(pl.multiple_of(step * 3 * slots + slots, slots), 2 * slots)
    flat = rows[two, pl.ds(pl.multiple_of(place_ref[0] * half, LANES), half)].T
    for start in range(0, gradient.shape[2], CHUNK):
        columns = pl.ds(start, CHUNK)
        gradient[0, :, columns] = jnp.dot(
            flat, inner[0, :, columns], preferred_element_type=jnp.float32
        ).astype(gradient.dtype)

    span = turned.shape[0]
    first = place_ref[0] * half + step * span
    for place in range(2):
        some = tokens[1 + place][:, pl.ds(pl.multiple_of(first, LANES), span)]
        turned[:, pl.ds(place * total, total)] = some.T

    @pl.when(step == count - 1)
    def _():
        for lead, (flipped, results) in enumerate(
            ((fore_flip, fore_results), (back_flip, back_results))
        ):
            sums = tokens[lead]
            combine(flipped, results, sums)
            *near_outs, far_out = outs[lead * (groups + 1) : (lead + 1) * (groups + 1)]
            size = far_out.shape[1]
            for group, out in enumerate(near_outs):
                near, far = (
                    pl.ds(pl.multiple_of(place_ref[3 + pair * group + code], size), size)
                    for code in range(pair)
                )
                out[...] = sums[near, :]
                far_out[group] = sums[far, :]


def weight_kernel(first, number, count, slots, place_ref, *refs):
    columns, inner, turned = refs[:3]
    out_ref, picks, rows, staged, out_done = refs[-5:]
    total, half = columns.shape[0], turned.shape[0]
    owner = 1 - place_ref[0]
    lane = lax.broadcasted_iota(jnp.int32, (total, LANES), 1).astype(jnp.float32)
    is_saved = lax.broadcasted_iota(jnp.int32, (1, LANES), 1) < slots
    scales = []
    for step in range(number):
        column = count + first + step
        slot = jnp.broadcast_to(columns[:, column : column + 1], (total, LANES))
        column += 2 * count
        gate = jnp.broadcast_to(columns[:, column : column + 1], (total, LANES))
        saved, grads = slot == lane, slot == lane - slots
        lanes = pl.ds(step * LANES, LANES)
        picks[pl.ds(0, total), lanes] = jnp.where(saved, 1.0, 0.0).astype(picks.dtype)
        picks[pl.ds(total, total), lanes] = jnp.where(
            jnp.logical_and(grads, lane >= slots), 1.0, 0.0
        ).astype(picks.dtype)
        scale = jnp.sum(jnp.where(grads, gate, 0.0), axis=0, keepdims=True)
        scales.append(jnp.where(is_saved, 1.0, scale))
    leaving = []
    for step in range(number):
        if step % 2 == 0:
            lanes = pl.ds(step * LANES, 2 * LANES)
            scale = jnp.concatenate(scales[step : step + 2], axis=1)
            rows[:, lanes] = (
                jnp.dot(turned[...], picks[:, lanes], preferred_element_type=jnp.float32) * scale
            ).astype(rows.dtype)
        for start in range(0, half, CHUNK):
            chunk = pl.ds(start, CHUNK)
            for corner in range(start, start + CHUNK, LANES):
                for column in range(0, inner.shape[2], CHUNK):
                    tile = (step, pl.ds(corner, LANES), pl.ds(column, CHUNK))
                    staged[tile] = jnp.dot(
                        rows[tile[1], pl.ds(step * LANES, 2 * slots)],
                        inner[first + step, :, tile[2]],
                        preferred_element_type=jnp.float32,
                    ).astype(staged.dtype)
            leaving.append(
                pltpu.make_async_copy(
                    staged.at[step, chunk, :],
                    out_ref.at[owner * count + first + step, chunk, :],
                    out_done.at[step, start // CHUNK],
                )
            )
            leaving[-1].start()
    for copy in leaving:
        copy.wait()


def gathered_plan(
    section_inputs,
    saved_inputs,
    output_grads,
    forward_routes,
    backward_routes,
    forward_gates,
    backward_gates,
    expert_weights,
):
    token_count = section_inputs.shape[1]
    top = forward_routes.shape[2]
    _, local_count, width, inner_width = expert_weights.shape
    groups, pair = lax.axis_size("expert"), lax.axis_size("dp")
    devices = groups * pair
    count = local_count // pair
    total = devices * token_count
    slots = -(-devices * CAP // 16) * 16
    rows = count * slots
    half = width // pair
    weights = expert_weights[0]

    side, group = lax.axis_index("dp"), lax.axis_index("expert")
    index = group * pair + side
    base = group * local_count
    place = jnp.stack(
        [side, base + side * count, base + (1 - side) * count]
        + [(index ^ code) * token_count for code in range(devices)]
    ).astype(jnp.int32)
    params = pltpu.CompilerParams(vmem_limit_bytes=VMEM_LIMIT, dimension_semantics=("arbitrary",))

    def whole(shape):
        return pl.BlockSpec(shape, lambda *_: (0,) * len(shape))

    def call(kernel, name, steps, in_specs, out_specs, out_shape, scratch, flops=0, aliases=()):
        return pl.pallas_call(
            kernel,
            grid_spec=pltpu.PrefetchScalarGridSpec(
                num_scalar_prefetch=1,
                grid=(steps,),
                in_specs=in_specs,
                out_specs=out_specs,
                scratch_shapes=scratch,
            ),
            out_shape=out_shape,
            compiler_params=params,
            cost_estimate=pl.CostEstimate(
                flops=flops, bytes_accessed=flops // 512 + 1024, transcendentals=0
            ),
            input_output_aliases=dict(aliases),
            name=name,
        )

    def onward(block):
        return swapped(block, 1)

    def across(parts):
        return [swapped(part, code) for part, code in zip(parts, range(pair, devices, pair))]

    def after(first, then):
        then, _ = lax.optimization_barrier((then, first))
        return then

    def summed(*blocks):
        return functools.reduce(jnp.add, [block.astype(jnp.float32) for block in blocks])

    packed = [
        jax.ShapeDtypeStruct((token_count, 3 * width // 2 + LANES), jnp.bfloat16)
    ] * 2
    own = pl.pallas_call(
        pack_kernel,
        in_specs=[pl.BlockSpec(memory_space=pl.ANY)] * 7,
        out_specs=[pl.BlockSpec(memory_space=pltpu.VMEM)] * 2,
        out_shape=packed,
        scratch_shapes=[
            pltpu.VMEM((top, token_count), jnp.int32),
            pltpu.VMEM((top, token_count), jnp.float32),
            pltpu.VMEM((top, token_count), jnp.int32),
            pltpu.VMEM((top, token_count), jnp.float32),
            pltpu.VMEM((LANES, LANES), jnp.float32),
            pltpu.SemaphoreType.DMA((8,)),
        ],
        compiler_params=pltpu.CompilerParams(vmem_limit_bytes=VMEM_LIMIT),
        name="pack",
    )(
        *[
            pltpu.with_memory_space_constraint(array, pltpu.HBM)
            for array in (
                section_inputs[0],
                saved_inputs[0],
                output_grads[0],
                backward_routes[0].T,
                backward_gates[0].T,
                forward_routes[0].T,
                forward_gates[0].T,
            )
        ]
    )
    bits = groups.bit_length() - 1
    far_own = [onward(block) for block in own]
    near = []
    for way, (block, far) in enumerate(zip(own, far_own)):
        held = {0: block}
        for bit in range(bits):
            step = 1 << (bit if way == 0 else bits - 1 - bit)
            sources = dict(held) if bit == 0 else {0: block} | after(far, {k: v for k, v in held.items() if k})
            held |= {group ^ step: swapped(source, step * pair) for group, source in sources.items()}
        near.append([held[group] for group in range(groups)])
    direct = [1 << bit for bit in range(bits)]
    settled = lax.optimization_barrier([[half_blocks[group] for group in direct] for half_blocks in near])
    blocks = []
    for half_blocks, far, firm in zip(near, far_own, settled):
        ready = list(half_blocks)
        for group, block in zip(direct, firm):
            ready[group] = block
        distant = [far] + [onward(block) for block in ready[1:]]
        blocks += [block for both in zip(half_blocks, distant) for block in both]

    pick = jax.ShapeDtypeStruct((rows, total), jnp.bfloat16)
    flip = jax.ShapeDtypeStruct((total, rows), jnp.bfloat16)
    gate = jax.ShapeDtypeStruct((rows, LANES), jnp.float32)
    columns = jax.ShapeDtypeStruct((total, LANES), jnp.float32)
    pick_outs = [pick, gate, flip, pick, gate, flip, columns]
    picks = call(
        functools.partial(picks_kernel, count, top, slots, devices),
        "slot_picks",
        1,
        [pl.BlockSpec((token_count, LANES), lambda *_: (0, 3 * width // 2 // LANES))]
        * (2 * devices),
        [whole(out.shape) for out in pick_outs],
        pick_outs,
        [pltpu.VMEM((total, LANES), jnp.float32), pltpu.VMEM((LANES, total), jnp.float32)],
    )(place, *blocks)

    pass_flops = 2 * 2 * count * CHUNK * width * inner_width
    near_part = jax.ShapeDtypeStruct((token_count, width), jnp.bfloat16)
    far_part = jax.ShapeDtypeStruct((groups, token_count, width), jnp.bfloat16)
    inner = jax.ShapeDtypeStruct((count, 2 * slots, inner_width), jnp.bfloat16)
    turned = jax.ShapeDtypeStruct((half, 2 * total), jnp.bfloat16)
    in_smem, in_vmem, anywhere = (
        pl.BlockSpec(memory_space=space) for space in (pltpu.SMEM, pltpu.VMEM, pl.ANY)
    )
    tokens = pltpu.VMEM((total, width), jnp.bfloat16)
    cut = width // WEIGHT_CUTS
    whole_gradient = jax.ShapeDtypeStruct((local_count, half, inner_width), jnp.bfloat16)
    *parts, inner_own, tokens_turned, done = pl.pallas_call(
        functools.partial(expert_kernel, count, slots, devices, pair),
        grid_spec=pltpu.PrefetchScalarGridSpec(
            num_scalar_prefetch=1,
            grid=(count,),
            in_specs=[whole(array.shape) for array in pick_outs[:6]]
            + [
                pl.BlockSpec(
                    (1, cut, inner_width),
                    lambda step, place, part=part: (place[0] * count + step, part, 0),
                )
                for part in range(WEIGHT_CUTS)
            ]
            + [whole(one.shape) for one in packed for _ in range(devices)],
            out_specs=([whole(near_part.shape)] * groups + [whole(far_part.shape)]) * 2
            + [
                pl.BlockSpec((1, 2 * slots, inner_width), lambda step, place: (step, 0, 0)),
                pl.BlockSpec((half // count, 2 * total), lambda step, place: (step, 0)),
                pl.BlockSpec(
                    (1, half, inner_width), lambda step, place: (place[0] * count + step, 0, 0)
                ),
            ],
            scratch_shapes=[tokens] * 3
            + [
                pltpu.VMEM((3 * rows, width), jnp.bfloat16),
                pltpu.VMEM((rows, width), jnp.bfloat16),
                pltpu.VMEM((rows, width), jnp.bfloat16),
                pltpu.VMEM((2 * slots, inner_width), jnp.bfloat16),
            ],
        ),
        out_shape=([near_part] * groups + [far_part]) * 2 + [inner, turned, whole_gradient],
        compiler_params=pltpu.CompilerParams(
            vmem_limit_bytes=EXPERTS_LIMIT, dimension_semantics=("arbitrary",)
        ),
        cost_estimate=pl.CostEstimate(
            flops=pass_flops, bytes_accessed=pass_flops // 512, transcendentals=0
        ),
        name="experts",
    )(place, *picks[:6], *[weights] * WEIGHT_CUTS, *blocks)
    *layer_parts, layer_far = parts[: groups + 1]
    *grad_parts, grad_far = parts[groups + 1 :]
    layer_far, grad_far = onward(layer_far), onward(grad_far)
    inner_other = onward(after(layer_far, inner_own))

    def gradient(first, number, earlier):
        operands = [picks[6], inner_other, tokens_turned, earlier]
        return pl.pallas_call(
            functools.partial(weight_kernel, first, number, count, slots),
            in_specs=[in_smem, in_vmem, in_vmem, in_vmem, anywhere],
            out_specs=anywhere,
            out_shape=whole_gradient,
            scratch_shapes=[
                pltpu.VMEM((2 * total, number * LANES), jnp.bfloat16),
                pltpu.VMEM((half, number * LANES), jnp.bfloat16),
                pltpu.VMEM((number, half, inner_width), jnp.bfloat16),
                pltpu.SemaphoreType.DMA((number, half // CHUNK)),
            ],
            compiler_params=pltpu.CompilerParams(vmem_limit_bytes=VMEM_LIMIT),
            cost_estimate=pl.CostEstimate(
                flops=number * pass_flops // count // 2,
                bytes_accessed=number * half * inner_width * 4,
                transcendentals=0,
            ),
            input_output_aliases={len(operands): 0},
            name=f"weight_gradient_{first}",
        )(place, *operands)

    def pair_sums(near_parts, far):
        return [summed(part, far[group]).astype(jnp.bfloat16) for group, part in enumerate(near_parts)]

    piece = count // 2
    layer_sums = pair_sums(layer_parts, layer_far)
    layer_near = across(layer_sums[1:])
    grad_sums = pair_sums(grad_parts, after((layer_sums, inner_other), grad_far))
    grad_near = across(grad_sums[1:])
    done = gradient(0, piece, after(grad_sums, done))
    layer_near = after((done, grad_near[:-1]), layer_near)
    layer_out = summed(section_inputs[0], layer_sums[0], *layer_near).astype(jnp.bfloat16)
    next_inputs = shifted(layer_out, "pipe", 1)[None]
    done = gradient(piece, count - piece, after(layer_out, done))
    grad_near = after((done, next_inputs), grad_near)
    input_grads = summed(output_grads[0], grad_sums[0], *grad_near).astype(jnp.bfloat16)
    prior_grads = shifted(input_grads, "pipe", -1)[None]
    return (next_inputs, prior_grads, done[None])


def on_device(*arrays):
    token_count = arrays[0].shape[1]
    local_count = arrays[-1].shape[1]
    groups, pair = lax.axis_size("expert"), lax.axis_size("dp")
    gathered = groups * token_count
    packed = groups * local_count * CAP
    paired = pair == 2 and local_count % 8 == 0 and groups & (groups - 1) == 0
    if gathered <= packed and paired and gathered * pair % LANES == 0:
        return gathered_plan(*arrays)
    return packed_plan(*arrays)


def solution(mesh):
    placed = (
        P("pipe", ("expert", "dp"), None),
        P("pipe", ("expert", "dp"), None),
        P("pipe", ("expert", "dp"), None),
        P("pipe", ("expert", "dp"), None),
        P("pipe", ("expert", "dp"), None),
        P("pipe", ("expert", "dp"), None),
        P("pipe", ("expert", "dp"), None),
        P("pipe", "expert", None, None),
    )
    return jax.shard_map(
        on_device,
        mesh=mesh,
        in_specs=placed,
        out_specs=(
            P("pipe", ("expert", "dp"), None),
            P("pipe", ("expert", "dp"), None),
            P("pipe", "expert", "dp", None),
        ),
        check_vma=False,
    )
```

```python
import functools

import jax
import jax.numpy as jnp
from jax import lax
from jax.experimental import pallas as pl
from jax.experimental.pallas import tpu as pltpu
from jax.sharding import PartitionSpec as P

CAP = 5
LANES = 128
CHUNK = 256
VMEM_LIMIT = 24 * 1024 * 1024
EXPERTS_LIMIT = 40 * 1024 * 1024
WEIGHT_CUTS = 4


def shifted(value, axis, steps):
    count = lax.axis_size(axis)
    pairs = [(source, (source + steps) % count) for source in range(count)]
    return lax.ppermute(value, axis, pairs)


def slot_index(routing, experts, capacity):
    one_hot = (routing[..., None] == jnp.arange(experts, dtype=jnp.int32)).astype(jnp.int32)
    before = jnp.cumsum(one_hot, axis=-2) - one_hot
    return routing * capacity + jnp.sum(before * one_hot, axis=-1)


def pack_rows(source, slot_ids, slot_total, spread):
    row_count = slot_ids.shape[0]
    owner_row = (
        jnp.zeros((slot_total,), jnp.int32)
        .at[slot_ids]
        .set(jnp.arange(row_count, dtype=jnp.int32) + 1)
    )
    filled = owner_row > 0
    picked = jnp.take(source, jnp.maximum(owner_row - 1, 0) // spread, axis=0)
    return jnp.where(filled[:, None], picked, jnp.zeros_like(picked))


def expert_forward(slot_rows, weights):
    hidden = jnp.einsum("nlcd,ldh->nlch", slot_rows, weights, preferred_element_type=jnp.float32)
    active = jax.nn.silu(hidden).astype(jnp.bfloat16)
    return jnp.einsum("nlch,ldh->nlcd", active, weights, preferred_element_type=jnp.float32).astype(
        jnp.bfloat16
    )


def expert_backward(saved_rows, slot_grads, weights):
    hidden = jnp.einsum("nlcd,ldh->nlch", saved_rows, weights, preferred_element_type=jnp.float32)
    active = jax.nn.silu(hidden).astype(jnp.bfloat16)
    active_grads = jnp.einsum(
        "nlcd,ldh->nlch", slot_grads, weights, preferred_element_type=jnp.float32
    )
    sigma = jax.nn.sigmoid(hidden)
    hidden_grads = (active_grads * sigma * (1.0 + hidden * (1.0 - sigma))).astype(jnp.bfloat16)
    row_grads = jnp.einsum(
        "nlch,ldh->nlcd", hidden_grads, weights, preferred_element_type=jnp.float32
    ).astype(jnp.bfloat16)
    weight_part = jnp.einsum(
        "nlcd,nlch->ldh", saved_rows, hidden_grads, preferred_element_type=jnp.float32
    )
    weight_part = weight_part + jnp.einsum(
        "nlcd,nlch->ldh", slot_grads, active, preferred_element_type=jnp.float32
    )
    return (row_grads, weight_part)


def packed_plan(
    section_inputs,
    saved_inputs,
    output_grads,
    forward_routes,
    backward_routes,
    forward_gates,
    backward_gates,
    expert_weights,
):
    token_count = section_inputs.shape[1]
    route_count = forward_routes.shape[2]
    local_count = expert_weights.shape[1]
    model_width = expert_weights.shape[2]
    groups = lax.axis_size("expert")
    experts = groups * local_count
    slot_total = experts * CAP
    block_shape = (groups, local_count, CAP, model_width)
    weights = expert_weights[0]
    forward_slot = slot_index(forward_routes[0].reshape(-1), experts, CAP)
    backward_slot = slot_index(backward_routes[0].reshape(-1), experts, CAP)
    forward_rows = pack_rows(section_inputs[0], forward_slot, slot_total, route_count).reshape(
        block_shape
    )
    saved_rows = pack_rows(saved_inputs[0], backward_slot, slot_total, route_count).reshape(
        block_shape
    )
    grad_block = output_grads[0]
    scaled = backward_gates[0][:, :, None] * grad_block.astype(jnp.float32)[:, None, :]
    scaled = scaled.astype(jnp.bfloat16).reshape(token_count * route_count, model_width)
    slot_grads = pack_rows(scaled, backward_slot, slot_total, 1).reshape(block_shape)
    forward_back = lax.all_to_all(
        expert_forward(
            lax.all_to_all(forward_rows, "expert", split_axis=0, concat_axis=0, tiled=True), weights
        ),
        "expert",
        split_axis=0,
        concat_axis=0,
        tiled=True,
    )
    saved_recv, grads_recv = (
        lax.all_to_all(saved_rows, "expert", split_axis=0, concat_axis=0, tiled=True),
        lax.all_to_all(slot_grads, "expert", split_axis=0, concat_axis=0, tiled=True),
    )
    row_grads, weight_part = expert_backward(saved_recv, grads_recv, weights)
    grads_back = lax.all_to_all(row_grads, "expert", split_axis=0, concat_axis=0, tiled=True)
    forward_pick = jnp.take(forward_back.reshape(slot_total, model_width), forward_slot, axis=0)
    forward_pick = forward_pick.reshape(token_count, route_count, model_width).astype(jnp.float32)
    layer_out = section_inputs[0].astype(jnp.float32) + jnp.sum(
        forward_gates[0][:, :, None] * forward_pick, axis=1
    )
    layer_out = layer_out.astype(jnp.bfloat16)
    grads_pick = jnp.take(grads_back.reshape(slot_total, model_width), backward_slot, axis=0)
    grads_pick = grads_pick.reshape(token_count, route_count, model_width).astype(jnp.float32)
    input_grads = (grad_block.astype(jnp.float32) + jnp.sum(grads_pick, axis=1)).astype(
        jnp.bfloat16
    )
    next_inputs = shifted(layer_out, "pipe", 1)[None]
    prior_grads = shifted(input_grads, "pipe", -1)[None]
    weight_grads = lax.psum_scatter(
        weight_part.astype(jnp.bfloat16), "dp", scatter_dimension=1, tiled=True
    )[None]
    return (next_inputs, prior_grads, weight_grads)


def swapped(value, code):
    axes = ("expert", "dp")
    count = lax.axis_size(axes[0]) * lax.axis_size(axes[1])
    return lax.ppermute(value, axes, [(source, source ^ code) for source in range(count)])


def pack_kernel(*refs):
    sources, (one, two), (*held, notes, done) = list(refs[:7]), refs[7:9], refs[9:]
    size, width = sources[0].shape
    half = width // 2
    top = sources[3].shape[0]
    targets = [one.at[:, pl.ds(0, width)], one.at[:, pl.ds(width, half)]]
    targets += [two.at[:, pl.ds(0, half)], two.at[:, pl.ds(half, width)]] + held
    sources[1:2] = [sources[1].at[:, pl.ds(0, half)], sources[1].at[:, pl.ds(half, half)]]
    copies = [
        pltpu.make_async_copy(source, target, done.at[place])
        for place, (source, target) in enumerate(zip(sources, targets))
    ]
    for copy in copies:
        copy.start()
    for copy in copies:
        copy.wait()
    back_routes, back_gates, fore_routes, fore_gates = held
    for place, (target, lane, routes, gates) in enumerate(
        ((two, half + width, back_routes, back_gates), (one, width + half, fore_routes, fore_gates))
    ):
        first = place * 4 * top
        notes[...] = jnp.zeros_like(notes)
        notes[pl.ds(first, top), 0:size] = routes[...].astype(jnp.float32)
        rest = gates[...]
        for term in range(1, 4):
            part = rest.astype(jnp.bfloat16).astype(jnp.float32)
            notes[pl.ds(first + term * top, top), 0:size] = part
            rest = rest - part
        target[:, pl.ds(lane, LANES)] = notes[...].T[:size, :].astype(jnp.bfloat16)


def picks_kernel(count, top, slots, devices, place_ref, *refs):
    blocks, outs, (notes, turned) = refs[: 2 * devices], refs[2 * devices : -2], refs[-2:]
    tokens = notes.shape[0]
    for code, (one, two) in enumerate(zip(blocks[:devices], blocks[devices:])):
        size = one.shape[0]
        rows = pl.ds(pl.multiple_of(place_ref[3 + code], size), size)
        notes[rows, :] = one[...].astype(jnp.float32) + two[...].astype(jnp.float32)
    turned[...] = notes[...].T
    row = lax.broadcasted_iota(jnp.int32, (tokens, tokens), 0)
    column = lax.broadcasted_iota(jnp.int32, (tokens, tokens), 1)
    earlier = jnp.where(row < column, 1.0, 0.0).astype(jnp.bfloat16)
    slot = lax.broadcasted_iota(jnp.int32, (slots, tokens), 0).astype(jnp.float32)

    def find(first, start):
        ids = (first + lax.broadcasted_iota(jnp.int32, (count, tokens), 0)).astype(jnp.float32)
        named = jnp.zeros((count, tokens), jnp.float32)
        gated = jnp.zeros((count, tokens), jnp.float32)
        for column in range(start, start + top):
            same = turned[column : column + 1, :] == ids
            terms = [turned[column + term * top : column + term * top + 1, :] for term in (1, 2, 3)]
            named = named + jnp.where(same, 1.0, 0.0)
            gated = gated + jnp.where(same, terms[0] + terms[1] + terms[2], 0.0)
        place = jnp.dot(named.astype(jnp.bfloat16), earlier, preferred_element_type=jnp.float32)
        return jnp.where(named > 0.0, place, -1.0), gated

    def fill(place, gated, picks, gates, flipped):
        for expert in range(count):
            rows = pl.ds(expert * slots, slots)
            hit = place[expert : expert + 1, :] == slot
            picks[rows, :] = jnp.where(hit, 1.0, 0.0).astype(jnp.bfloat16)
            own = jnp.sum(jnp.where(hit, gated[expert : expert + 1, :], 0.0), axis=1, keepdims=True)
            gates[rows, :] = jnp.broadcast_to(own, (slots, LANES))
        flipped[...] = picks[...].T

    places, gated = find(place_ref[1], 4 * top)
    fill(places, gated, outs[0], outs[1], outs[2])
    places, gated = find(place_ref[1], 0)
    fill(places, gated, outs[3], outs[4], outs[5])
    other_places, other_gated = find(place_ref[2], 0)
    turned[...] = jnp.zeros_like(turned)
    for row, value in enumerate((places, other_places, gated, other_gated)):
        turned[pl.ds(row * count, count), :] = value
    outs[6][...] = turned[...].T


def spread_gate(gates, rows, width):
    gate = gates[rows, 0:1]
    return jnp.broadcast_to(gate, (gate.shape[0], width))


def assemble(place_ref, first, second, tokens):
    width = tokens[0].shape[1]
    half = width // 2
    for code, (one, two) in enumerate(zip(first, second)):
        size = one.shape[0]
        rows = pl.ds(pl.multiple_of(place_ref[3 + code], size), size)
        tokens[0][rows, :] = one[:, pl.ds(0, width)]
        tokens[1][rows, pl.ds(0, half)] = one[:, pl.ds(width, half)]
        tokens[1][rows, pl.ds(half, half)] = two[:, pl.ds(0, half)]
        tokens[2][rows, :] = two[:, pl.ds(half, width)]


def combine(flipped, results, sums):
    width = sums.shape[1]
    for start in range(0, width, CHUNK):
        columns = pl.ds(start, CHUNK)
        sums[:, columns] = jnp.dot(
            flipped[...], results[:, columns], preferred_element_type=jnp.float32
        ).astype(sums.dtype)


def gather(count, slots, picks, gates, tokens_ref, rows, first, stride):
    width = tokens_ref.shape[1]
    for start in range(0, width, CHUNK):
        columns = pl.ds(start, CHUNK)
        taken = jnp.dot(picks[...], tokens_ref[:, columns], preferred_element_type=jnp.float32)
        if gates is not None:
            taken = taken * spread_gate(gates, pl.ds(0, count * slots), CHUNK)
        taken = taken.astype(rows.dtype)
        for expert in range(count):
            part = slice(expert * slots, (expert + 1) * slots)
            rows[pl.ds(first + expert * stride, slots), columns] = taken[part]


def expert_kernel(count, slots, devices, pair, place_ref, *refs):
    fore_picks, fore_gates, fore_flip, back_picks, back_gates, back_flip = refs[:6]
    weights, blocks = refs[6 : 6 + WEIGHT_CUTS], refs[6 + WEIGHT_CUTS :][: 2 * devices]
    groups = devices // pair
    outs = refs[6 + WEIGHT_CUTS + 2 * devices :][: 2 * groups + 2]
    inner, turned, gradient, *scratch = refs[8 + WEIGHT_CUTS + 2 * devices + 2 * groups :]
    tokens, (rows, fore_results, back_results, second) = scratch[:3], scratch[3:]
    total, width = tokens[0].shape
    step = pl.program_id(0)

    @pl.when(step == 0)
    def _():
        taken = ((fore_picks, None), (back_picks, None), (back_picks, back_gates))
        assemble(place_ref, blocks[:devices], blocks[devices:], tokens)
        for place, (picks, gates) in enumerate(taken):
            gather(count, slots, picks, gates, tokens[place], rows, place * slots, 3 * slots)

    mine = pl.ds(pl.multiple_of(step * slots, slots), slots)
    three = pl.ds(pl.multiple_of(step * 3 * slots, 3 * slots), 3 * slots)
    cut = width // WEIGHT_CUTS
    for start in range(0, inner.shape[2], CHUNK):
        lanes = pl.ds(start, CHUNK)
        product = functools.reduce(
            jnp.add,
            [
                jnp.dot(
                    rows[three, pl.ds(place * cut, cut)],
                    weight[0, :, lanes],
                    preferred_element_type=jnp.float32,
                )
                for place, weight in enumerate(weights)
            ],
        )
        ahead, hidden, active_grads = (
            product[:slots],
            product[slots : 2 * slots],
            product[2 * slots :],
        )
        sigma = jax.nn.sigmoid(hidden)
        hidden_grads = (active_grads * sigma * (1.0 + hidden * (1.0 - sigma))).astype(jnp.bfloat16)
        inner[0, :slots, lanes] = hidden_grads
        inner[0, slots:, lanes] = (hidden * sigma).astype(jnp.bfloat16)
        gate = spread_gate(fore_gates, mine, CHUNK)
        second[:slots, lanes] = (ahead * jax.nn.sigmoid(ahead) * gate).astype(jnp.bfloat16)
        second[slots:, lanes] = hidden_grads
    for start in range(0, width, CHUNK):
        columns = pl.ds(start, CHUNK)
        result = lax.dot_general(
            second[...],
            weights[start // cut][0, pl.ds(start % cut, CHUNK), :],
            (((1,), (1,)), ((), ())),
            preferred_element_type=jnp.float32,
        ).astype(fore_results.dtype)
        fore_results[mine, columns] = result[:slots]
        back_results[mine, columns] = result[slots:]

    half = gradient.shape[1]
    two = pl.ds(pl.multiple_of(step * 3 * slots + slots, slots), 2 * slots)
    flat = rows[two, pl.ds(pl.multiple_of(place_ref[0] * half, LANES), half)].T
    for start in range(0, gradient.shape[2], CHUNK):
        columns = pl.ds(start, CHUNK)
        gradient[0, :, columns] = jnp.dot(
            flat, inner[0, :, columns], preferred_element_type=jnp.float32
        ).astype(gradient.dtype)

    span = turned.shape[0]
    first = place_ref[0] * half + step * span
    for place in range(2):
        some = tokens[1 + place][:, pl.ds(pl.multiple_of(first, LANES), span)]
        turned[:, pl.ds(place * total, total)] = some.T

    @pl.when(step == count - 1)
    def _():
        for lead, (flipped, results) in enumerate(
            ((fore_flip, fore_results), (back_flip, back_results))
        ):
            sums = tokens[lead]
            combine(flipped, results, sums)
            *near_outs, far_out = outs[lead * (groups + 1) : (lead + 1) * (groups + 1)]
            size = far_out.shape[1]
            for group, out in enumerate(near_outs):
                near, far = (
                    pl.ds(pl.multiple_of(place_ref[3 + pair * group + code], size), size)
                    for code in range(pair)
                )
                out[...] = sums[near, :]
                far_out[group] = sums[far, :]


def weight_kernel(first, number, count, slots, place_ref, *refs):
    columns, inner, turned = refs[:3]
    out_ref, picks, rows, staged, out_done = refs[-5:]
    total, half = columns.shape[0], turned.shape[0]
    owner = 1 - place_ref[0]
    lane = lax.broadcasted_iota(jnp.int32, (total, LANES), 1).astype(jnp.float32)
    is_saved = lax.broadcasted_iota(jnp.int32, (1, LANES), 1) < slots
    scales = []
    for step in range(number):
        column = count + first + step
        slot = jnp.broadcast_to(columns[:, column : column + 1], (total, LANES))
        column += 2 * count
        gate = jnp.broadcast_to(columns[:, column : column + 1], (total, LANES))
        saved, grads = slot == lane, slot == lane - slots
        lanes = pl.ds(step * LANES, LANES)
        picks[pl.ds(0, total), lanes] = jnp.where(saved, 1.0, 0.0).astype(picks.dtype)
        picks[pl.ds(total, total), lanes] = jnp.where(
            jnp.logical_and(grads, lane >= slots), 1.0, 0.0
        ).astype(picks.dtype)
        scale = jnp.sum(jnp.where(grads, gate, 0.0), axis=0, keepdims=True)
        scales.append(jnp.where(is_saved, 1.0, scale))
    for step in range(0, number, 2):
        lanes = pl.ds(step * LANES, 2 * LANES)
        scale = jnp.concatenate(scales[step : step + 2], axis=1)
        rows[:, lanes] = (
            jnp.dot(turned[...], picks[:, lanes], preferred_element_type=jnp.float32) * scale
        ).astype(rows.dtype)

    leaving = []
    for step in range(number):
        for start in range(0, half, CHUNK):
            chunk = pl.ds(start, CHUNK)
            for corner in range(start, start + CHUNK, LANES):
                for column in range(0, inner.shape[2], CHUNK):
                    tile = (step, pl.ds(corner, LANES), pl.ds(column, CHUNK))
                    staged[tile] = jnp.dot(
                        rows[tile[1], pl.ds(step * LANES, 2 * slots)],
                        inner[first + step, :, tile[2]],
                        preferred_element_type=jnp.float32,
                    ).astype(staged.dtype)
            leaving.append(
                pltpu.make_async_copy(
                    staged.at[step, chunk, :],
                    out_ref.at[owner * count + first + step, chunk, :],
                    out_done.at[step, start // CHUNK],
                )
            )
            leaving[-1].start()
    for copy in leaving:
        copy.wait()


def deliver_kernel(*refs):
    sources, targets, done = refs[:2], refs[2:4], refs[4]
    copies = [
        pltpu.make_async_copy(source, target, done.at[place])
        for place, (source, target) in enumerate(zip(sources, targets))
    ]
    for copy in copies:
        copy.start()
    for copy in copies:
        copy.wait()


def gathered_plan(
    section_inputs,
    saved_inputs,
    output_grads,
    forward_routes,
    backward_routes,
    forward_gates,
    backward_gates,
    expert_weights,
):
    token_count = section_inputs.shape[1]
    top = forward_routes.shape[2]
    _, local_count, width, inner_width = expert_weights.shape
    groups, pair = lax.axis_size("expert"), lax.axis_size("dp")
    devices = groups * pair
    count = local_count // pair
    total = devices * token_count
    slots = -(-devices * CAP // 16) * 16
    rows = count * slots
    half = width // pair
    weights = expert_weights[0]

    side, group = lax.axis_index("dp"), lax.axis_index("expert")
    index = group * pair + side
    base = group * local_count
    place = jnp.stack(
        [side, base + side * count, base + (1 - side) * count]
        + [(index ^ code) * token_count for code in range(devices)]
    ).astype(jnp.int32)
    params = pltpu.CompilerParams(vmem_limit_bytes=VMEM_LIMIT, dimension_semantics=("arbitrary",))

    def whole(shape):
        return pl.BlockSpec(shape, lambda *_: (0,) * len(shape))

    def call(kernel, name, steps, in_specs, out_specs, out_shape, scratch, flops=0, aliases=()):
        return pl.pallas_call(
            kernel,
            grid_spec=pltpu.PrefetchScalarGridSpec(
                num_scalar_prefetch=1,
                grid=(steps,),
                in_specs=in_specs,
                out_specs=out_specs,
                scratch_shapes=scratch,
            ),
            out_shape=out_shape,
            compiler_params=params,
            cost_estimate=pl.CostEstimate(
                flops=flops, bytes_accessed=flops // 512 + 1024, transcendentals=0
            ),
            input_output_aliases=dict(aliases),
            name=name,
        )

    def onward(block):
        return swapped(block, 1)

    def across(parts):
        return [swapped(part, code) for part, code in zip(parts, range(pair, devices, pair))]

    def after(first, then):
        then, _ = lax.optimization_barrier((then, first))
        return then

    def summed(*blocks):
        return functools.reduce(jnp.add, [block.astype(jnp.float32) for block in blocks])

    packed = [
        jax.ShapeDtypeStruct((token_count, 3 * width // 2 + LANES), jnp.bfloat16)
    ] * 2
    own = pl.pallas_call(
        pack_kernel,
        in_specs=[pl.BlockSpec(memory_space=pl.ANY)] * 7,
        out_specs=[pl.BlockSpec(memory_space=pltpu.VMEM)] * 2,
        out_shape=packed,
        scratch_shapes=[
            pltpu.VMEM((top, token_count), jnp.int32),
            pltpu.VMEM((top, token_count), jnp.float32),
            pltpu.VMEM((top, token_count), jnp.int32),
            pltpu.VMEM((top, token_count), jnp.float32),
            pltpu.VMEM((LANES, LANES), jnp.float32),
            pltpu.SemaphoreType.DMA((8,)),
        ],
        compiler_params=pltpu.CompilerParams(vmem_limit_bytes=VMEM_LIMIT),
        name="pack",
    )(
        *[
            pltpu.with_memory_space_constraint(array, pltpu.HBM)
            for array in (
                section_inputs[0],
                saved_inputs[0],
                output_grads[0],
                backward_routes[0].T,
                backward_gates[0].T,
                forward_routes[0].T,
                forward_gates[0].T,
            )
        ]
    )
    bits = groups.bit_length() - 1
    far_own = [onward(block) for block in own]
    near = []
    for way, (block, far) in enumerate(zip(own, far_own)):
        held = {0: block}
        for bit in range(bits):
            step = 1 << (bit if way == 0 else bits - 1 - bit)
            sources = dict(held) if bit == 0 else {0: block} | after(far, {k: v for k, v in held.items() if k})
            held |= {group ^ step: swapped(source, step * pair) for group, source in sources.items()}
        near.append([held[group] for group in range(groups)])
    direct = [1 << bit for bit in range(bits)]
    settled = lax.optimization_barrier([[half_blocks[group] for group in direct] for half_blocks in near])
    blocks = []
    for half_blocks, far, firm in zip(near, far_own, settled):
        ready = list(half_blocks)
        for group, block in zip(direct, firm):
            ready[group] = block
        distant = [far] + [onward(block) for block in ready[1:]]
        blocks += [block for both in zip(half_blocks, distant) for block in both]

    pick = jax.ShapeDtypeStruct((rows, total), jnp.bfloat16)
    flip = jax.ShapeDtypeStruct((total, rows), jnp.bfloat16)
    gate = jax.ShapeDtypeStruct((rows, LANES), jnp.float32)
    columns = jax.ShapeDtypeStruct((total, LANES), jnp.float32)
    pick_outs = [pick, gate, flip, pick, gate, flip, columns]
    picks = call(
        functools.partial(picks_kernel, count, top, slots, devices),
        "slot_picks",
        1,
        [pl.BlockSpec((token_count, LANES), lambda *_: (0, 3 * width // 2 // LANES))]
        * (2 * devices),
        [whole(out.shape) for out in pick_outs],
        pick_outs,
        [pltpu.VMEM((total, LANES), jnp.float32), pltpu.VMEM((LANES, total), jnp.float32)],
    )(place, *blocks)

    pass_flops = 2 * 2 * count * CHUNK * width * inner_width
    near_part = jax.ShapeDtypeStruct((token_count, width), jnp.bfloat16)
    far_part = jax.ShapeDtypeStruct((groups, token_count, width), jnp.bfloat16)
    inner = jax.ShapeDtypeStruct((count, 2 * slots, inner_width), jnp.bfloat16)
    turned = jax.ShapeDtypeStruct((half, 2 * total), jnp.bfloat16)
    in_smem, in_vmem, anywhere = (
        pl.BlockSpec(memory_space=space) for space in (pltpu.SMEM, pltpu.VMEM, pl.ANY)
    )
    tokens = pltpu.VMEM((total, width), jnp.bfloat16)
    cut = width // WEIGHT_CUTS
    whole_gradient = jax.ShapeDtypeStruct((local_count, half, inner_width), jnp.bfloat16)
    *parts, inner_own, tokens_turned, done = pl.pallas_call(
        functools.partial(expert_kernel, count, slots, devices, pair),
        grid_spec=pltpu.PrefetchScalarGridSpec(
            num_scalar_prefetch=1,
            grid=(count,),
            in_specs=[whole(array.shape) for array in pick_outs[:6]]
            + [
                pl.BlockSpec(
                    (1, cut, inner_width),
                    lambda step, place, part=part: (place[0] * count + step, part, 0),
                )
                for part in range(WEIGHT_CUTS)
            ]
            + [whole(one.shape) for one in packed for _ in range(devices)],
            out_specs=([whole(near_part.shape)] * groups + [whole(far_part.shape)]) * 2
            + [
                pl.BlockSpec((1, 2 * slots, inner_width), lambda step, place: (step, 0, 0)),
                pl.BlockSpec((half // count, 2 * total), lambda step, place: (step, 0)),
                pl.BlockSpec(
                    (1, half, inner_width), lambda step, place: (place[0] * count + step, 0, 0)
                ),
            ],
            scratch_shapes=[tokens] * 3
            + [
                pltpu.VMEM((3 * rows, width), jnp.bfloat16),
                pltpu.VMEM((rows, width), jnp.bfloat16),
                pltpu.VMEM((rows, width), jnp.bfloat16),
                pltpu.VMEM((2 * slots, inner_width), jnp.bfloat16),
            ],
        ),
        out_shape=([near_part] * groups + [far_part]) * 2 + [inner, turned, whole_gradient],
        compiler_params=pltpu.CompilerParams(
            vmem_limit_bytes=EXPERTS_LIMIT, dimension_semantics=("arbitrary",)
        ),
        cost_estimate=pl.CostEstimate(
            flops=pass_flops, bytes_accessed=pass_flops // 512, transcendentals=0
        ),
        name="experts",
    )(place, *picks[:6], *[weights] * WEIGHT_CUTS, *blocks)
    *layer_parts, layer_far = parts[: groups + 1]
    *grad_parts, grad_far = parts[groups + 1 :]
    layer_far, grad_far = onward(layer_far), onward(grad_far)
    inner_other = onward(after(layer_far, inner_own))

    def gradient(first, number, earlier):
        operands = [picks[6], inner_other, tokens_turned, earlier]
        return pl.pallas_call(
            functools.partial(weight_kernel, first, number, count, slots),
            in_specs=[in_smem, in_vmem, in_vmem, in_vmem, anywhere],
            out_specs=anywhere,
            out_shape=whole_gradient,
            scratch_shapes=[
                pltpu.VMEM((2 * total, number * LANES), jnp.bfloat16),
                pltpu.VMEM((half, number * LANES), jnp.bfloat16),
                pltpu.VMEM((number, half, inner_width), jnp.bfloat16),
                pltpu.SemaphoreType.DMA((number, half // CHUNK)),
            ],
            compiler_params=pltpu.CompilerParams(vmem_limit_bytes=VMEM_LIMIT),
            cost_estimate=pl.CostEstimate(
                flops=number * pass_flops // count // 2,
                bytes_accessed=number * half * inner_width * 4,
                transcendentals=0,
            ),
            input_output_aliases={len(operands): 0},
            name=f"weight_gradient_{first}",
        )(place, *operands)

    def pair_sums(near_parts, far):
        return [summed(part, far[group]).astype(jnp.bfloat16) for group, part in enumerate(near_parts)]

    piece = count // 2
    layer_sums = pair_sums(layer_parts, layer_far)
    layer_near = across(layer_sums[1:])
    grad_sums = pair_sums(grad_parts, after((layer_sums, inner_other), grad_far))
    grad_near = across(grad_sums[1:])
    done = gradient(0, piece, after(grad_sums, done))
    layer_near = after((done, grad_near[:-1]), layer_near)
    layer_out = summed(section_inputs[0], layer_sums[0], *layer_near).astype(jnp.bfloat16)
    next_inputs = shifted(layer_out, "pipe", 1)[None]
    done = gradient(piece, count - piece, after(layer_out, done))
    grad_near = after((done, next_inputs), grad_near)
    input_grads = summed(output_grads[0], grad_sums[0], *grad_near).astype(jnp.bfloat16)
    prior_grads = shifted(input_grads, "pipe", -1)[None]
    delivered = pl.pallas_call(
        deliver_kernel,
        in_specs=[anywhere] * 2,
        out_specs=[anywhere] * 2,
        out_shape=[pltpu.HBM(array.shape, array.dtype) for array in (next_inputs, prior_grads)],
        scratch_shapes=[pltpu.SemaphoreType.DMA((2,))],
        name="deliver",
    )(next_inputs, prior_grads)
    return (*delivered, done[None])


def on_device(*arrays):
    token_count = arrays[0].shape[1]
    local_count = arrays[-1].shape[1]
    groups, pair = lax.axis_size("expert"), lax.axis_size("dp")
    gathered = groups * token_count
    packed = groups * local_count * CAP
    paired = pair == 2 and local_count % 8 == 0 and groups & (groups - 1) == 0
    if gathered <= packed and paired and gathered * pair % LANES == 0:
        return gathered_plan(*arrays)
    return packed_plan(*arrays)


def solution(mesh):
    placed = (
        P("pipe", ("expert", "dp"), None),
        P("pipe", ("expert", "dp"), None),
        P("pipe", ("expert", "dp"), None),
        P("pipe", ("expert", "dp"), None),
        P("pipe", ("expert", "dp"), None),
        P("pipe", ("expert", "dp"), None),
        P("pipe", ("expert", "dp"), None),
        P("pipe", "expert", None, None),
    )
    return jax.shard_map(
        on_device,
        mesh=mesh,
        in_specs=placed,
        out_specs=(
            P("pipe", ("expert", "dp"), None),
            P("pipe", ("expert", "dp"), None),
            P("pipe", "expert", "dp", None),
        ),
        check_vma=False,
    )
```

```python
import functools

import jax
import jax.numpy as jnp
from jax import lax
from jax.experimental import pallas as pl
from jax.experimental.pallas import tpu as pltpu
from jax.sharding import PartitionSpec as P

CAP = 5
LANES = 128
CHUNK = 256
VMEM_LIMIT = 24 * 1024 * 1024
EXPERTS_LIMIT = 40 * 1024 * 1024
WEIGHT_CUTS = 4


def shifted(value, axis, steps):
    count = lax.axis_size(axis)
    pairs = [(source, (source + steps) % count) for source in range(count)]
    return lax.ppermute(value, axis, pairs)


def slot_index(routing, experts, capacity):
    one_hot = (routing[..., None] == jnp.arange(experts, dtype=jnp.int32)).astype(jnp.int32)
    before = jnp.cumsum(one_hot, axis=-2) - one_hot
    return routing * capacity + jnp.sum(before * one_hot, axis=-1)


def pack_rows(source, slot_ids, slot_total, spread):
    row_count = slot_ids.shape[0]
    owner_row = (
        jnp.zeros((slot_total,), jnp.int32)
        .at[slot_ids]
        .set(jnp.arange(row_count, dtype=jnp.int32) + 1)
    )
    filled = owner_row > 0
    picked = jnp.take(source, jnp.maximum(owner_row - 1, 0) // spread, axis=0)
    return jnp.where(filled[:, None], picked, jnp.zeros_like(picked))


def expert_forward(slot_rows, weights):
    hidden = jnp.einsum("nlcd,ldh->nlch", slot_rows, weights, preferred_element_type=jnp.float32)
    active = jax.nn.silu(hidden).astype(jnp.bfloat16)
    return jnp.einsum("nlch,ldh->nlcd", active, weights, preferred_element_type=jnp.float32).astype(
        jnp.bfloat16
    )


def expert_backward(saved_rows, slot_grads, weights):
    hidden = jnp.einsum("nlcd,ldh->nlch", saved_rows, weights, preferred_element_type=jnp.float32)
    active = jax.nn.silu(hidden).astype(jnp.bfloat16)
    active_grads = jnp.einsum(
        "nlcd,ldh->nlch", slot_grads, weights, preferred_element_type=jnp.float32
    )
    sigma = jax.nn.sigmoid(hidden)
    hidden_grads = (active_grads * sigma * (1.0 + hidden * (1.0 - sigma))).astype(jnp.bfloat16)
    row_grads = jnp.einsum(
        "nlch,ldh->nlcd", hidden_grads, weights, preferred_element_type=jnp.float32
    ).astype(jnp.bfloat16)
    weight_part = jnp.einsum(
        "nlcd,nlch->ldh", saved_rows, hidden_grads, preferred_element_type=jnp.float32
    )
    weight_part = weight_part + jnp.einsum(
        "nlcd,nlch->ldh", slot_grads, active, preferred_element_type=jnp.float32
    )
    return (row_grads, weight_part)


def packed_plan(
    section_inputs,
    saved_inputs,
    output_grads,
    forward_routes,
    backward_routes,
    forward_gates,
    backward_gates,
    expert_weights,
):
    token_count = section_inputs.shape[1]
    route_count = forward_routes.shape[2]
    local_count = expert_weights.shape[1]
    model_width = expert_weights.shape[2]
    groups = lax.axis_size("expert")
    experts = groups * local_count
    slot_total = experts * CAP
    block_shape = (groups, local_count, CAP, model_width)
    weights = expert_weights[0]
    forward_slot = slot_index(forward_routes[0].reshape(-1), experts, CAP)
    backward_slot = slot_index(backward_routes[0].reshape(-1), experts, CAP)
    forward_rows = pack_rows(section_inputs[0], forward_slot, slot_total, route_count).reshape(
        block_shape
    )
    saved_rows = pack_rows(saved_inputs[0], backward_slot, slot_total, route_count).reshape(
        block_shape
    )
    grad_block = output_grads[0]
    scaled = backward_gates[0][:, :, None] * grad_block.astype(jnp.float32)[:, None, :]
    scaled = scaled.astype(jnp.bfloat16).reshape(token_count * route_count, model_width)
    slot_grads = pack_rows(scaled, backward_slot, slot_total, 1).reshape(block_shape)
    forward_back = lax.all_to_all(
        expert_forward(
            lax.all_to_all(forward_rows, "expert", split_axis=0, concat_axis=0, tiled=True), weights
        ),
        "expert",
        split_axis=0,
        concat_axis=0,
        tiled=True,
    )
    saved_recv, grads_recv = (
        lax.all_to_all(saved_rows, "expert", split_axis=0, concat_axis=0, tiled=True),
        lax.all_to_all(slot_grads, "expert", split_axis=0, concat_axis=0, tiled=True),
    )
    row_grads, weight_part = expert_backward(saved_recv, grads_recv, weights)
    grads_back = lax.all_to_all(row_grads, "expert", split_axis=0, concat_axis=0, tiled=True)
    forward_pick = jnp.take(forward_back.reshape(slot_total, model_width), forward_slot, axis=0)
    forward_pick = forward_pick.reshape(token_count, route_count, model_width).astype(jnp.float32)
    layer_out = section_inputs[0].astype(jnp.float32) + jnp.sum(
        forward_gates[0][:, :, None] * forward_pick, axis=1
    )
    layer_out = layer_out.astype(jnp.bfloat16)
    grads_pick = jnp.take(grads_back.reshape(slot_total, model_width), backward_slot, axis=0)
    grads_pick = grads_pick.reshape(token_count, route_count, model_width).astype(jnp.float32)
    input_grads = (grad_block.astype(jnp.float32) + jnp.sum(grads_pick, axis=1)).astype(
        jnp.bfloat16
    )
    next_inputs = shifted(layer_out, "pipe", 1)[None]
    prior_grads = shifted(input_grads, "pipe", -1)[None]
    weight_grads = lax.psum_scatter(
        weight_part.astype(jnp.bfloat16), "dp", scatter_dimension=1, tiled=True
    )[None]
    return (next_inputs, prior_grads, weight_grads)


def swapped(value, code):
    axes = ("expert", "dp")
    count = lax.axis_size(axes[0]) * lax.axis_size(axes[1])
    return lax.ppermute(value, axes, [(source, source ^ code) for source in range(count)])


def pack_kernel(*refs):
    sources, (one, two), (*held, notes, done) = list(refs[:7]), refs[7:9], refs[9:]
    size, width = sources[0].shape
    half = width // 2
    top = sources[3].shape[0]
    targets = [one.at[:, pl.ds(0, width)], one.at[:, pl.ds(width, half)]]
    targets += [two.at[:, pl.ds(0, half)], two.at[:, pl.ds(half, width)]] + held
    sources[1:2] = [sources[1].at[:, pl.ds(0, half)], sources[1].at[:, pl.ds(half, half)]]
    copies = [
        pltpu.make_async_copy(source, target, done.at[place])
        for place, (source, target) in enumerate(zip(sources, targets))
    ]
    for copy in copies:
        copy.start()
    for copy in copies:
        copy.wait()
    back_routes, back_gates, fore_routes, fore_gates = held
    for place, (target, lane, routes, gates) in enumerate(
        ((two, half + width, back_routes, back_gates), (one, width + half, fore_routes, fore_gates))
    ):
        first = place * 4 * top
        notes[...] = jnp.zeros_like(notes)
        notes[pl.ds(first, top), 0:size] = routes[...].astype(jnp.float32)
        rest = gates[...]
        for term in range(1, 4):
            part = rest.astype(jnp.bfloat16).astype(jnp.float32)
            notes[pl.ds(first + term * top, top), 0:size] = part
            rest = rest - part
        target[:, pl.ds(lane, LANES)] = notes[...].T[:size, :].astype(jnp.bfloat16)


def picks_kernel(count, top, slots, devices, place_ref, *refs):
    blocks, outs, (notes, turned) = refs[: 2 * devices], refs[2 * devices : -2], refs[-2:]
    tokens = notes.shape[0]
    for code, (one, two) in enumerate(zip(blocks[:devices], blocks[devices:])):
        size = one.shape[0]
        rows = pl.ds(pl.multiple_of(place_ref[3 + code], size), size)
        notes[rows, :] = one[...].astype(jnp.float32) + two[...].astype(jnp.float32)
    turned[...] = notes[...].T
    row = lax.broadcasted_iota(jnp.int32, (tokens, tokens), 0)
    column = lax.broadcasted_iota(jnp.int32, (tokens, tokens), 1)
    earlier = jnp.where(row < column, 1.0, 0.0).astype(jnp.bfloat16)
    slot = lax.broadcasted_iota(jnp.int32, (slots, tokens), 0).astype(jnp.float32)

    def find(first, start):
        ids = (first + lax.broadcasted_iota(jnp.int32, (count, tokens), 0)).astype(jnp.float32)
        named = jnp.zeros((count, tokens), jnp.float32)
        gated = jnp.zeros((count, tokens), jnp.float32)
        for column in range(start, start + top):
            same = turned[column : column + 1, :] == ids
            terms = [turned[column + term * top : column + term * top + 1, :] for term in (1, 2, 3)]
            named = named + jnp.where(same, 1.0, 0.0)
            gated = gated + jnp.where(same, terms[0] + terms[1] + terms[2], 0.0)
        place = jnp.dot(named.astype(jnp.bfloat16), earlier, preferred_element_type=jnp.float32)
        return jnp.where(named > 0.0, place, -1.0), gated

    def fill(place, gated, picks, gates, flipped):
        for expert in range(count):
            rows = pl.ds(expert * slots, slots)
            hit = place[expert : expert + 1, :] == slot
            picks[rows, :] = jnp.where(hit, 1.0, 0.0).astype(jnp.bfloat16)
            own = jnp.sum(jnp.where(hit, gated[expert : expert + 1, :], 0.0), axis=1, keepdims=True)
            gates[rows, :] = jnp.broadcast_to(own, (slots, LANES))
        flipped[...] = picks[...].T

    places, gated = find(place_ref[1], 4 * top)
    fill(places, gated, outs[0], outs[1], outs[2])
    places, gated = find(place_ref[1], 0)
    fill(places, gated, outs[3], outs[4], outs[5])
    other_places, other_gated = find(place_ref[2], 0)
    turned[...] = jnp.zeros_like(turned)
    for row, value in enumerate((places, other_places, gated, other_gated)):
        turned[pl.ds(row * count, count), :] = value
    outs[6][...] = turned[...].T


def spread_gate(gates, rows, width):
    gate = gates[rows, 0:1]
    return jnp.broadcast_to(gate, (gate.shape[0], width))


def assemble(place_ref, first, second, tokens):
    width = tokens[0].shape[1]
    half = width // 2
    for code, (one, two) in enumerate(zip(first, second)):
        size = one.shape[0]
        rows = pl.ds(pl.multiple_of(place_ref[3 + code], size), size)
        tokens[0][rows, :] = one[:, pl.ds(0, width)]
        tokens[1][rows, pl.ds(0, half)] = one[:, pl.ds(width, half)]
        tokens[1][rows, pl.ds(half, half)] = two[:, pl.ds(0, half)]
        tokens[2][rows, :] = two[:, pl.ds(half, width)]


def combine(flipped, results, sums):
    width = sums.shape[1]
    for start in range(0, width, CHUNK):
        columns = pl.ds(start, CHUNK)
        sums[:, columns] = jnp.dot(
            flipped[...], results[:, columns], preferred_element_type=jnp.float32
        ).astype(sums.dtype)


def gather(count, slots, picks, gates, tokens_ref, rows, first, stride):
    width = tokens_ref.shape[1]
    for start in range(0, width, CHUNK):
        columns = pl.ds(start, CHUNK)
        taken = jnp.dot(picks[...], tokens_ref[:, columns], preferred_element_type=jnp.float32)
        if gates is not None:
            taken = taken * spread_gate(gates, pl.ds(0, count * slots), CHUNK)
        taken = taken.astype(rows.dtype)
        for expert in range(count):
            part = slice(expert * slots, (expert + 1) * slots)
            rows[pl.ds(first + expert * stride, slots), columns] = taken[part]


def expert_kernel(count, slots, devices, pair, place_ref, *refs):
    fore_picks, fore_gates, fore_flip, back_picks, back_gates, back_flip = refs[:6]
    weights, blocks = refs[6 : 6 + WEIGHT_CUTS], refs[6 + WEIGHT_CUTS :][: 2 * devices]
    groups = devices // pair
    outs = refs[6 + WEIGHT_CUTS + 2 * devices :][: 2 * groups + 2]
    inner, turned, gradient, *scratch = refs[8 + WEIGHT_CUTS + 2 * devices + 2 * groups :]
    tokens, (rows, fore_results, back_results, second) = scratch[:3], scratch[3:]
    total, width = tokens[0].shape
    step = pl.program_id(0)

    @pl.when(step == 0)
    def _():
        taken = ((fore_picks, None), (back_picks, None), (back_picks, back_gates))
        assemble(place_ref, blocks[:devices], blocks[devices:], tokens)
        for place, (picks, gates) in enumerate(taken):
            gather(count, slots, picks, gates, tokens[place], rows, place * slots, 3 * slots)

    mine = pl.ds(pl.multiple_of(step * slots, slots), slots)
    three = pl.ds(pl.multiple_of(step * 3 * slots, 3 * slots), 3 * slots)
    cut = width // WEIGHT_CUTS
    for start in range(0, inner.shape[2], CHUNK):
        lanes = pl.ds(start, CHUNK)
        product = functools.reduce(
            jnp.add,
            [
                jnp.dot(
                    rows[three, pl.ds(place * cut, cut)],
                    weight[0, :, lanes],
                    preferred_element_type=jnp.float32,
                )
                for place, weight in enumerate(weights)
            ],
        )
        ahead, hidden, active_grads = (
            product[:slots],
            product[slots : 2 * slots],
            product[2 * slots :],
        )
        sigma = jax.nn.sigmoid(hidden)
        hidden_grads = (active_grads * sigma * (1.0 + hidden * (1.0 - sigma))).astype(jnp.bfloat16)
        inner[0, :slots, lanes] = hidden_grads
        inner[0, slots:, lanes] = (hidden * sigma).astype(jnp.bfloat16)
        gate = spread_gate(fore_gates, mine, CHUNK)
        second[:slots, lanes] = (ahead * jax.nn.sigmoid(ahead) * gate).astype(jnp.bfloat16)
        second[slots:, lanes] = hidden_grads
    for start in range(0, width, CHUNK):
        columns = pl.ds(start, CHUNK)
        result = lax.dot_general(
            second[...],
            weights[start // cut][0, pl.ds(start % cut, CHUNK), :],
            (((1,), (1,)), ((), ())),
            preferred_element_type=jnp.float32,
        ).astype(fore_results.dtype)
        fore_results[mine, columns] = result[:slots]
        back_results[mine, columns] = result[slots:]

    half = gradient.shape[1]
    two = pl.ds(pl.multiple_of(step * 3 * slots + slots, slots), 2 * slots)
    flat = rows[two, pl.ds(pl.multiple_of(place_ref[0] * half, LANES), half)].T
    for start in range(0, gradient.shape[2], CHUNK):
        columns = pl.ds(start, CHUNK)
        gradient[0, :, columns] = jnp.dot(
            flat, inner[0, :, columns], preferred_element_type=jnp.float32
        ).astype(gradient.dtype)

    span = turned.shape[0]
    first = place_ref[0] * half + step * span
    for place in range(2):
        some = tokens[1 + place][:, pl.ds(pl.multiple_of(first, LANES), span)]
        turned[:, pl.ds(place * total, total)] = some.T

    @pl.when(step == count - 1)
    def _():
        for lead, (flipped, results) in enumerate(
            ((fore_flip, fore_results), (back_flip, back_results))
        ):
            sums = tokens[lead]
            combine(flipped, results, sums)
            *near_outs, far_out = outs[lead * (groups + 1) : (lead + 1) * (groups + 1)]
            size = far_out.shape[1]
            for group, out in enumerate(near_outs):
                near, far = (
                    pl.ds(pl.multiple_of(place_ref[3 + pair * group + code], size), size)
                    for code in range(pair)
                )
                out[...] = sums[near, :]
                far_out[group] = sums[far, :]


def weight_kernel(first, number, count, slots, place_ref, *refs):
    columns, inner, turned = refs[:3]
    out_ref, picks, rows, staged, out_done = refs[-5:]
    total, half = columns.shape[0], turned.shape[0]
    owner = 1 - place_ref[0]
    lane = lax.broadcasted_iota(jnp.int32, (total, LANES), 1).astype(jnp.float32)
    is_saved = lax.broadcasted_iota(jnp.int32, (1, LANES), 1) < slots
    scales = []
    for step in range(number):
        column = count + first + step
        slot = jnp.broadcast_to(columns[:, column : column + 1], (total, LANES))
        column += 2 * count
        gate = jnp.broadcast_to(columns[:, column : column + 1], (total, LANES))
        saved, grads = slot == lane, slot == lane - slots
        lanes = pl.ds(step * LANES, LANES)
        picks[pl.ds(0, total), lanes] = jnp.where(saved, 1.0, 0.0).astype(picks.dtype)
        picks[pl.ds(total, total), lanes] = jnp.where(
            jnp.logical_and(grads, lane >= slots), 1.0, 0.0
        ).astype(picks.dtype)
        scale = jnp.sum(jnp.where(grads, gate, 0.0), axis=0, keepdims=True)
        scales.append(jnp.where(is_saved, 1.0, scale))
    for step in range(0, number, 2):
        lanes = pl.ds(step * LANES, 2 * LANES)
        scale = jnp.concatenate(scales[step : step + 2], axis=1)
        rows[:, lanes] = (
            jnp.dot(turned[...], picks[:, lanes], preferred_element_type=jnp.float32) * scale
        ).astype(rows.dtype)

    leaving = []
    for step in range(number):
        for start in range(0, half, CHUNK):
            chunk = pl.ds(start, CHUNK)
            for corner in range(start, start + CHUNK, LANES):
                for column in range(0, inner.shape[2], CHUNK):
                    tile = (step, pl.ds(corner, LANES), pl.ds(column, CHUNK))
                    staged[tile] = jnp.dot(
                        rows[tile[1], pl.ds(step * LANES, 2 * slots)],
                        inner[first + step, :, tile[2]],
                        preferred_element_type=jnp.float32,
                    ).astype(staged.dtype)
            leaving.append(
                pltpu.make_async_copy(
                    staged.at[step, chunk, :],
                    out_ref.at[owner * count + first + step, chunk, :],
                    out_done.at[step, start // CHUNK],
                )
            )
            leaving[-1].start()
    for copy in leaving:
        copy.wait()


def gathered_plan(
    section_inputs,
    saved_inputs,
    output_grads,
    forward_routes,
    backward_routes,
    forward_gates,
    backward_gates,
    expert_weights,
):
    token_count = section_inputs.shape[1]
    top = forward_routes.shape[2]
    _, local_count, width, inner_width = expert_weights.shape
    groups, pair = lax.axis_size("expert"), lax.axis_size("dp")
    devices = groups * pair
    count = local_count // pair
    total = devices * token_count
    slots = -(-devices * CAP // 16) * 16
    rows = count * slots
    half = width // pair
    weights = expert_weights[0]

    side, group = lax.axis_index("dp"), lax.axis_index("expert")
    index = group * pair + side
    base = group * local_count
    place = jnp.stack(
        [side, base + side * count, base + (1 - side) * count]
        + [(index ^ code) * token_count for code in range(devices)]
    ).astype(jnp.int32)
    params = pltpu.CompilerParams(vmem_limit_bytes=VMEM_LIMIT, dimension_semantics=("arbitrary",))

    def whole(shape):
        return pl.BlockSpec(shape, lambda *_: (0,) * len(shape))

    def call(kernel, name, steps, in_specs, out_specs, out_shape, scratch, flops=0, aliases=()):
        return pl.pallas_call(
            kernel,
            grid_spec=pltpu.PrefetchScalarGridSpec(
                num_scalar_prefetch=1,
                grid=(steps,),
                in_specs=in_specs,
                out_specs=out_specs,
                scratch_shapes=scratch,
            ),
            out_shape=out_shape,
            compiler_params=params,
            cost_estimate=pl.CostEstimate(
                flops=flops, bytes_accessed=flops // 512 + 1024, transcendentals=0
            ),
            input_output_aliases=dict(aliases),
            name=name,
        )

    def onward(block):
        return swapped(block, 1)

    def across(parts):
        return [swapped(part, code) for part, code in zip(parts, range(pair, devices, pair))]

    def after(first, then):
        then, _ = lax.optimization_barrier((then, first))
        return then

    def summed(*blocks):
        return functools.reduce(jnp.add, [block.astype(jnp.float32) for block in blocks])

    packed = [
        jax.ShapeDtypeStruct((token_count, 3 * width // 2 + LANES), jnp.bfloat16)
    ] * 2
    own = pl.pallas_call(
        pack_kernel,
        in_specs=[pl.BlockSpec(memory_space=pl.ANY)] * 7,
        out_specs=[pl.BlockSpec(memory_space=pltpu.VMEM)] * 2,
        out_shape=packed,
        scratch_shapes=[
            pltpu.VMEM((top, token_count), jnp.int32),
            pltpu.VMEM((top, token_count), jnp.float32),
            pltpu.VMEM((top, token_count), jnp.int32),
            pltpu.VMEM((top, token_count), jnp.float32),
            pltpu.VMEM((LANES, LANES), jnp.float32),
            pltpu.SemaphoreType.DMA((8,)),
        ],
        compiler_params=pltpu.CompilerParams(vmem_limit_bytes=VMEM_LIMIT),
        name="pack",
    )(
        *[
            pltpu.with_memory_space_constraint(array, pltpu.HBM)
            for array in (
                section_inputs[0],
                saved_inputs[0],
                output_grads[0],
                backward_routes[0].T,
                backward_gates[0].T,
                forward_routes[0].T,
                forward_gates[0].T,
            )
        ]
    )
    bits = groups.bit_length() - 1
    far_own = [onward(block) for block in own]
    near = []
    for way, (block, far) in enumerate(zip(own, far_own)):
        held = {0: block}
        for bit in range(bits):
            step = 1 << (bit if way == 0 else bits - 1 - bit)
            sources = dict(held) if bit == 0 else {0: block} | after(far, {k: v for k, v in held.items() if k})
            held |= {group ^ step: swapped(source, step * pair) for group, source in sources.items()}
        near.append([held[group] for group in range(groups)])
    direct = [1 << bit for bit in range(bits)]
    settled = lax.optimization_barrier([[half_blocks[group] for group in direct] for half_blocks in near])
    blocks = []
    for half_blocks, far, firm in zip(near, far_own, settled):
        ready = list(half_blocks)
        for group, block in zip(direct, firm):
            ready[group] = block
        distant = [far] + [onward(block) for block in ready[1:]]
        blocks += [block for both in zip(half_blocks, distant) for block in both]

    pick = jax.ShapeDtypeStruct((rows, total), jnp.bfloat16)
    flip = jax.ShapeDtypeStruct((total, rows), jnp.bfloat16)
    gate = jax.ShapeDtypeStruct((rows, LANES), jnp.float32)
    columns = jax.ShapeDtypeStruct((total, LANES), jnp.float32)
    pick_outs = [pick, gate, flip, pick, gate, flip, columns]
    picks = call(
        functools.partial(picks_kernel, count, top, slots, devices),
        "slot_picks",
        1,
        [pl.BlockSpec((token_count, LANES), lambda *_: (0, 3 * width // 2 // LANES))]
        * (2 * devices),
        [whole(out.shape) for out in pick_outs],
        pick_outs,
        [pltpu.VMEM((total, LANES), jnp.float32), pltpu.VMEM((LANES, total), jnp.float32)],
    )(place, *blocks)

    pass_flops = 2 * 2 * count * CHUNK * width * inner_width
    near_part = jax.ShapeDtypeStruct((token_count, width), jnp.bfloat16)
    far_part = jax.ShapeDtypeStruct((groups, token_count, width), jnp.bfloat16)
    inner = jax.ShapeDtypeStruct((count, 2 * slots, inner_width), jnp.bfloat16)
    turned = jax.ShapeDtypeStruct((half, 2 * total), jnp.bfloat16)
    in_smem, in_vmem, anywhere = (
        pl.BlockSpec(memory_space=space) for space in (pltpu.SMEM, pltpu.VMEM, pl.ANY)
    )
    tokens = pltpu.VMEM((total, width), jnp.bfloat16)
    cut = width // WEIGHT_CUTS
    whole_gradient = jax.ShapeDtypeStruct((local_count, half, inner_width), jnp.bfloat16)
    *parts, inner_own, tokens_turned, done = pl.pallas_call(
        functools.partial(expert_kernel, count, slots, devices, pair),
        grid_spec=pltpu.PrefetchScalarGridSpec(
            num_scalar_prefetch=1,
            grid=(count,),
            in_specs=[whole(array.shape) for array in pick_outs[:6]]
            + [
                pl.BlockSpec(
                    (1, cut, inner_width),
                    lambda step, place, part=part: (place[0] * count + step, part, 0),
                )
                for part in range(WEIGHT_CUTS)
            ]
            + [whole(one.shape) for one in packed for _ in range(devices)],
            out_specs=([whole(near_part.shape)] * groups + [whole(far_part.shape)]) * 2
            + [
                pl.BlockSpec((1, 2 * slots, inner_width), lambda step, place: (step, 0, 0)),
                pl.BlockSpec((half // count, 2 * total), lambda step, place: (step, 0)),
                pl.BlockSpec(
                    (1, half, inner_width), lambda step, place: (place[0] * count + step, 0, 0)
                ),
            ],
            scratch_shapes=[tokens] * 3
            + [
                pltpu.VMEM((3 * rows, width), jnp.bfloat16),
                pltpu.VMEM((rows, width), jnp.bfloat16),
                pltpu.VMEM((rows, width), jnp.bfloat16),
                pltpu.VMEM((2 * slots, inner_width), jnp.bfloat16),
            ],
        ),
        out_shape=([near_part] * groups + [far_part]) * 2 + [inner, turned, whole_gradient],
        compiler_params=pltpu.CompilerParams(
            vmem_limit_bytes=EXPERTS_LIMIT, dimension_semantics=("arbitrary",)
        ),
        cost_estimate=pl.CostEstimate(
            flops=pass_flops, bytes_accessed=pass_flops // 512, transcendentals=0
        ),
        name="experts",
    )(place, *picks[:6], *[weights] * WEIGHT_CUTS, *blocks)
    *layer_parts, layer_far = parts[: groups + 1]
    *grad_parts, grad_far = parts[groups + 1 :]
    layer_far, grad_far = onward(layer_far), onward(grad_far)
    inner_other = onward(after(layer_far, inner_own))

    def gradient(first, number, earlier):
        operands = [picks[6], inner_other, tokens_turned, earlier]
        return pl.pallas_call(
            functools.partial(weight_kernel, first, number, count, slots),
            in_specs=[in_smem, in_vmem, in_vmem, in_vmem, anywhere],
            out_specs=anywhere,
            out_shape=whole_gradient,
            scratch_shapes=[
                pltpu.VMEM((2 * total, number * LANES), jnp.bfloat16),
                pltpu.VMEM((half, number * LANES), jnp.bfloat16),
                pltpu.VMEM((number, half, inner_width), jnp.bfloat16),
                pltpu.SemaphoreType.DMA((number, half // CHUNK)),
            ],
            compiler_params=pltpu.CompilerParams(vmem_limit_bytes=VMEM_LIMIT),
            cost_estimate=pl.CostEstimate(
                flops=number * pass_flops // count // 2,
                bytes_accessed=number * half * inner_width * 4,
                transcendentals=0,
            ),
            input_output_aliases={len(operands): 0},
            name=f"weight_gradient_{first}",
        )(place, *operands)

    def pair_sums(near_parts, far):
        return [summed(part, far[group]).astype(jnp.bfloat16) for group, part in enumerate(near_parts)]

    piece = count // 2
    layer_sums = pair_sums(layer_parts, layer_far)
    layer_near = across(layer_sums[1:])
    grad_sums = pair_sums(grad_parts, after((layer_sums, inner_other), grad_far))
    grad_near = across(grad_sums[1:])
    done = gradient(0, piece, after(grad_sums, done))
    layer_near = after((done, grad_near[:-1]), layer_near)
    layer_out = summed(section_inputs[0], layer_sums[0], *layer_near).astype(jnp.bfloat16)
    next_inputs = shifted(layer_out, "pipe", 1)[None]
    done = gradient(piece, count - piece, after(layer_out, done))
    grad_near = after((done, next_inputs), grad_near)
    input_grads = summed(output_grads[0], grad_sums[0], *grad_near).astype(jnp.bfloat16)
    prior_grads = shifted(input_grads, "pipe", -1)[None]
    return (next_inputs, prior_grads, done[None])


def on_device(*arrays):
    token_count = arrays[0].shape[1]
    local_count = arrays[-1].shape[1]
    groups, pair = lax.axis_size("expert"), lax.axis_size("dp")
    gathered = groups * token_count
    packed = groups * local_count * CAP
    paired = pair == 2 and local_count % 8 == 0 and groups & (groups - 1) == 0
    if gathered <= packed and paired and gathered * pair % LANES == 0:
        return gathered_plan(*arrays)
    return packed_plan(*arrays)


def solution(mesh):
    placed = (
        P("pipe", ("expert", "dp"), None),
        P("pipe", ("expert", "dp"), None),
        P("pipe", ("expert", "dp"), None),
        P("pipe", ("expert", "dp"), None),
        P("pipe", ("expert", "dp"), None),
        P("pipe", ("expert", "dp"), None),
        P("pipe", ("expert", "dp"), None),
        P("pipe", "expert", None, None),
    )
    return jax.shard_map(
        on_device,
        mesh=mesh,
        in_specs=placed,
        out_specs=(
            P("pipe", ("expert", "dp"), None),
            P("pipe", ("expert", "dp"), None),
            P("pipe", "expert", "dp", None),
        ),
        check_vma=False,
    )
```
